128 devices in a mesh: tile: 8 (over x, core), mode: 16 (over z, y).
Axes of the slice: x: 4, y: 4, z: 4, core: 2. Of those that a mesh axis runs over, the one named last changes fastest.
Arguments:
- object_field: float32 [2, 2048, 512], P(None, 'tile'), may hold values from -3 to 3
- probe_modes: float32 [16, 2, 256, 256], P('mode'), may hold values from -3 to 3
- patterns: bfloat16 [64, 256, 256], P('tile'), may hold values from 0 to 16
- offsets: int32 [64, 2], P('tile'), may hold values from 0 to 256, as said below
- counts: int32 [8], P('tile'), may hold values from 1 to 8, as said below
Outputs:
- updated_object: float32 [2, 2048, 512], P(None, 'tile')
The draws below stay inside these ranges and needn't reach their ends.
Inputs may be any that keep to these rules, and one draw needn't show every extreme that they name: `offsets`: column 0 is the patch's first row within its strip of 256 rows, column 1 its first column; a patch may reach into the next strip. Some slot starts at row 255 and column 256, some at row 0 and column 0. A strip's live slots are its first counts[t] slots; the other slots hold offsets and patterns that are not used. Some strip has 8 live slots.
All inputs are finite; a program needn't handle non-finite values.
Results may differ from the reference program's by a relative error of at most 0.003.
Values may be sent and summed in bfloat16 or wider, within the bound.
A program may use at most 128 MiB of HBM per device.

```python
import math
import jax
import jax.numpy as jnp
from jax import lax

PATCH = 256
SH = 256
W = 512
MOST = 8
PASSES = 2
MODES = 16
H = 2048
POSITIONS = 64


def draw_probe_modes(key, part):
    key = jax.random.fold_in(key, 37)
    key_magnitude, key_phase, key_separate = jax.random.split(key, 3)
    magnitude = jax.random.uniform(key_magnitude, (1, PATCH, PATCH), jnp.float32, 0.6, 1.2)
    separate = jax.random.truncated_normal(key_separate, -3.0, 3.0, (MODES, 2, PATCH, PATCH), jnp.float32)
    shared_weight = 0.89
    phase_angle = jax.random.uniform(key_phase, (1, PATCH, PATCH), jnp.float32, -math.pi, math.pi)
    common = jnp.stack([magnitude * jnp.cos(phase_angle), magnitude * jnp.sin(phase_angle)], axis=1)
    separate_weight = math.sqrt(1.0 - shared_weight * shared_weight)
    return (shared_weight * common + separate_weight * separate).astype(jnp.float32)


def draw_offsets(key, part):
    key = jax.random.fold_in(key, 11)
    key_rows, key_cols, key_pick = jax.random.split(key, 3)
    first_rows = jax.random.randint(key_rows, (POSITIONS,), 0, SH)
    first_cols = jax.random.randint(key_cols, (POSITIONS,), 0, W - PATCH + 1)
    chosen = jax.random.randint(key_pick, (), 0, POSITIONS)
    places = jnp.arange(POSITIONS)
    second = (chosen + 1) % POSITIONS
    first_rows = jnp.where(places == chosen, SH - 1, first_rows)
    first_cols = jnp.where(places == chosen, W - PATCH, first_cols)
    first_rows = jnp.where(places == second, 0, first_rows)
    first_cols = jnp.where(places == second, 0, first_cols)
    return jnp.stack([first_rows, first_cols], axis=1).astype(jnp.int32)


def draw_counts(key, part):
    key = jax.random.fold_in(key, 23)
    key_count, key_pick = jax.random.split(key, 2)
    strips = POSITIONS // MOST
    values = jax.random.randint(key_count, (strips,), 1, MOST + 1)
    chosen = jax.random.randint(key_pick, (), 0, strips)
    places = jnp.arange(strips)
    values = jnp.where(places == chosen, MOST, values)
    values = jnp.where(places == (chosen + 1) % strips, 1, values)
    return values.astype(jnp.int32)


def block_levels(rng, extent, pieces, least, top_value):
    def one(dim, blocks):
        draws = jax.random.uniform(jax.random.fold_in(jax.random.fold_in(rng, 6), dim), (blocks,), jnp.float32, least / len(pieces), top_value / len(pieces))
        return jnp.repeat(jnp.exp(draws), extent[dim] // blocks).reshape((-1,) + (1,) * (len(extent) - dim - 1))

    factor_of = one(*pieces[0])
    for cut in pieces[1:]:
        factor_of = factor_of * one(*cut)
    return factor_of


def bell_draw(rng, shape, deviation, reach, cuts=(), kind=jnp.bfloat16):
    loudness = block_levels(rng, shape, cuts, -0.22, 0.18) if cuts else 1.0
    array = jax.random.normal(rng, shape, jnp.float32) * deviation * loudness
    return jnp.minimum(jnp.maximum(array, -reach), reach).astype(kind)


def setup_inputs(seed: int = 0) -> dict:
    key_of = jax.random.split(jax.random.key(seed), 6)
    return {
        "object_field": bell_draw(key_of[0], (2, H, W), 0.5, 3.0, ((1, 8),), jnp.float32),
        "probe_modes": draw_probe_modes(jax.random.fold_in(key_of[5], 71), 0),
        "patterns": jnp.clip(16.0 * jax.random.uniform(key_of[2], (POSITIONS, PATCH, PATCH), jnp.float32) ** block_levels(key_of[2], (POSITIONS, PATCH, PATCH), ((0, 8),), -0.2, 0.2), 0.0, 16.0).astype(jnp.bfloat16),
        "offsets": draw_offsets(jax.random.fold_in(key_of[5], 71), 0),
        "counts": draw_counts(jax.random.fold_in(key_of[5], 71), 0),
    }


STEP_SIZE = 0.9

def make_tables():
    indices = jnp.arange(PATCH, dtype=jnp.int32)
    product = indices[:, None] * indices[None, :] % PATCH
    angles = product.astype(jnp.float32) * (2.0 * math.pi / PATCH)
    factor = 1.0 / math.sqrt(PATCH)
    cosine = (jnp.cos(angles) * factor).astype(jnp.bfloat16)
    minus_sine = (-jnp.sin(angles) * factor).astype(jnp.bfloat16)
    first_table = jnp.stack([jnp.stack([cosine, -minus_sine]), jnp.stack([minus_sine, cosine])])
    second_table = jnp.stack([jnp.stack([cosine, minus_sine]), jnp.stack([-minus_sine, cosine])])
    return (first_table, second_table)

def transform(values, first_table, second_table):
    halfway = jnp.einsum('cdux,...dxy->...cuy', first_table.astype(jnp.float32), values.astype(jnp.float32))
    halfway = halfway.astype(jnp.bfloat16)
    return jnp.einsum('...dux,dcxy->...cuy', halfway.astype(jnp.float32), second_table.astype(jnp.float32))

def apply_probe(probes, field):
    real_part = probes[..., 0, :, :] * field[..., 0, :, :] - probes[..., 1, :, :] * field[..., 1, :, :]
    imag_part = probes[..., 0, :, :] * field[..., 1, :, :] + probes[..., 1, :, :] * field[..., 0, :, :]
    return jnp.stack([real_part, imag_part], axis=-3)

def conj_probe(probes, field):
    real_part = probes[..., 0, :, :] * field[..., 0, :, :] + probes[..., 1, :, :] * field[..., 1, :, :]
    imag_part = probes[..., 0, :, :] * field[..., 1, :, :] - probes[..., 1, :, :] * field[..., 0, :, :]
    return jnp.stack([real_part, imag_part], axis=-3)

def reference(object_field, probe_modes, patterns, offsets, counts):
    first_table, second_table = make_tables()
    extended = jnp.pad(object_field, ((0, 0), (0, SH), (0, 0)))
    probe_power = lax.optimization_barrier(jnp.sum(probe_modes[:, 0] ** 2 + probe_modes[:, 1] ** 2, axis=0))
    highest = jnp.max(probe_power)
    tile_index = jnp.arange(POSITIONS, dtype=jnp.int32) // MOST
    slot_index = jnp.arange(POSITIONS, dtype=jnp.int32) % MOST
    live_mask = (slot_index < counts[tile_index]).astype(jnp.float32)
    first_row = (tile_index * SH + offsets[:, 0]).astype(jnp.int32)
    first_col = offsets[:, 1].astype(jnp.int32)

    def refine(inputs):
        row_start, col_start, measured = inputs
        initial = lax.dynamic_slice(extended, (jnp.int32(0), row_start, col_start), (2, PATCH, PATCH))
        current = initial
        for repeat in range(PASSES):
            exit_wave = apply_probe(probe_modes, current[None]).astype(jnp.bfloat16)
            far_field = transform(exit_wave, first_table, second_table)
            intensity = lax.optimization_barrier(jnp.sum(far_field[:, 0] ** 2 + far_field[:, 1] ** 2, axis=0))
            amp_ratio = jnp.sqrt(measured.astype(jnp.float32) / jnp.maximum(intensity, 1.0))
            far_change = ((amp_ratio - 1.0) * far_field).astype(jnp.bfloat16)
            near_change = transform(far_change, second_table, first_table)
            mode_term = conj_probe(probe_modes, near_change).astype(jnp.bfloat16)
            update = lax.optimization_barrier(jnp.sum(mode_term.astype(jnp.float32), axis=0))
            current = current + STEP_SIZE / highest * update
        return current - initial
    changes = lax.map(refine, (first_row, first_col, patterns))

    def add_position(position, carry):
        summed, covered = carry
        row_start = first_row[position]
        col_start = first_col[position]
        piece = lax.dynamic_slice(summed, (jnp.int32(0), row_start, col_start), (2, PATCH, PATCH))
        piece = piece + changes[position] * live_mask[position]
        summed = lax.dynamic_update_slice(summed, piece, (jnp.int32(0), row_start, col_start))
        count_piece = lax.dynamic_slice(covered, (row_start, col_start), (PATCH, PATCH)) + live_mask[position]
        covered = lax.dynamic_update_slice(covered, count_piece, (row_start, col_start))
        return (summed, covered)
    summed = jnp.zeros((2, H + SH, W), jnp.float32)
    covered = jnp.zeros((H + SH, W), jnp.float32)
    summed, covered = lax.fori_loop(0, POSITIONS, add_position, (summed, covered))
    return object_field + summed[:, :H] / jnp.maximum(covered[:H], 1.0)
```

```python
import math

import numpy as np
import ml_dtypes
import jax
import jax.numpy as jnp
from jax import lax
from jax.experimental import pallas as pl
from jax.experimental.pallas import tpu as pltpu
from jax.sharding import PartitionSpec as P

PATCH = 256
HALF = 128
PASSES = 2
STEP_SIZE = 0.9
SLAB = 16
MESH = pl.DeviceIdType.MESH
BF16 = jnp.bfloat16
F32 = jnp.float32

ORDER = ((0, 0), (1, 0), (0, 1), (0, 3), (1, 1), (1, 3), (0, 2), (1, 2))


def make_tables():
    q = np.arange(HALF)
    tables = []
    for s in range(2):
        a = 2 * np.arange(HALF) + s
        angle = (q[:, None] * a[None, :] % PATCH).astype(np.float32) * np.float32(2.0 * math.pi / PATCH)
        factor = np.float32(1.0 / math.sqrt(PATCH))
        real = (np.cos(angle) * factor).astype(ml_dtypes.bfloat16)
        imag = (-np.sin(angle) * factor).astype(ml_dtypes.bfloat16)
        tables.append(np.block([[real, -imag], [imag, real]]))
    tables = np.stack(tables)
    return np.stack([tables, tables.transpose(0, 2, 1)])


def mm(a, b):
    return jnp.dot(a, b, preferred_element_type=F32)


def natural(position):
    return jnp.where(position < HALF, 2 * position, 2 * position - (PATCH - 1))


def kernel(
    obj_hbm, probe_hbm, pat_hbm, tab_hbm, offs_ref, counts_ref, out_hbm,
    probe, strip, strip_b, ext, pat, tab, info, modes, half, far, init, cur,
    inten, ratio, upd, power, inten_b, upd_b, last_b, power_b, inten_in, upd_in, last_in, power_in,
    place_r, place_c, canvas, slabs, spill, spill_in, ring_y, ring_z,
    local_sem, gather_send, gather_recv, strip_sem, info_sem, patch_sem, pat_sem,
    pair_send, pair_recv, slab_send, slab_recv, spill_sem, ring_send, ring_recv,
):
    t = lax.axis_index("tile")
    j = lax.axis_index("mode")
    x, z = t // 2, j // 4
    c, y = t - 2 * x, j - 4 * z
    group = z // 2
    owner = c == group
    s_tile = 2 * x + group
    slot = j - 8 * group
    partner = 2 * x + (1 - c)
    up_tile = (t + 1) % 8
    down_tile = (t + 7) % 8

    load_probe = pltpu.make_async_copy(probe_hbm.at[0], probe, local_sem.at[0])
    load_strip = pltpu.make_async_copy(obj_hbm, strip, local_sem.at[1])
    load_tab = pltpu.make_async_copy(tab_hbm, tab, local_sem.at[2])
    load_pat = pltpu.make_async_copy(pat_hbm.at[slot], pat, local_sem.at[3])
    @pl.when(owner)
    def _():
        load_probe.start()
        load_pat.start()

    load_strip.start()
    load_tab.start()

    barrier = pltpu.get_barrier_semaphore()

    def greet(tile, mode):
        pl.semaphore_signal(barrier, inc=1, device_id=(tile, mode), device_id_type=MESH)

    for k in range(1, 16):
        greet(t, (j + k) % 16)
    greet(partner, j)
    across = jnp.where(c == 1, up_tile, down_tile)
    greet(across, j)
    for k in range(8):
        greet(partner, 8 * c + k)

    lane = lax.broadcasted_iota(jnp.int32, (8, HALF), 1)
    live = (lax.broadcasted_iota(jnp.int32, (8, HALF), 0) < counts_ref[0]).astype(jnp.int32)
    offs = offs_ref[...]
    info[0] = jnp.where(lane == 0, offs[:, 0:1], jnp.where(lane == 1, offs[:, 1:2], live))

    pl.semaphore_wait(barrier, 15 + 2 + jnp.where(owner, 0, 16))

    def to(src, dst, send, recv, tile, mode):
        return pltpu.make_async_remote_copy(
            src_ref=src, dst_ref=dst, send_sem=send, recv_sem=recv,
            device_id=(tile, mode), device_id_type=MESH,
        )

    info_pair = to(info.at[0], info.at[1], info_sem.at[0], info_sem.at[1], partner, j)
    info_next = to(info.at[0], info.at[2], info_sem.at[2], info_sem.at[3], up_tile, j)
    info_pair.start()

    @pl.when(c == 1)
    def _():
        info_next.start()

    def block(m, s, h):
        return modes.at[m, s, pl.ds(h * HALF, HALF), :]

    def mode_slot(row, home, dy):
        d = (row - 2 * c + 4) % 4
        nearer = 2 * c + jnp.where((d == 1) | (d == 2), 1, 0)
        return jnp.where(home == nearer, ORDER.index((0, dy)), ORDER.index((1, dy)))

    def relay(k, s, h, home, dy, step_z, step_y):
        row = (z + step_z + 4) % 4
        there = mode_slot(row, home, (dy + step_y) % 4)
        to(
            block(k, s, h), block(there, s, h), gather_send, gather_recv.at[there, s, h],
            t, row * 4 + (y + step_y + 4) % 4,
        ).start()

    def take(k):
        which, dy = ORDER[k]
        d = (z - 2 * c + 4) % 4
        nearer = jnp.where((d == 1) | (d == 2), 1, 0)
        home = 2 * c + (nearer if which == 0 else 1 - nearer)
        dz = (z - home + 4) % 4
        for h in range(2):
            for s in range(2):
                def wait():
                    to(
                        block(k, s, h), block(k, s, h), gather_send, gather_recv.at[k, s, h], t, j
                    ).wait_recv()

                if k == 0:
                    pl.when(dz != 0)(wait)
                else:
                    wait()
                steps = []
                if dy == 0 or (dy == 1 and h == 0):
                    steps.append(1)
                if dy == 0 or (dy == 3 and h == 1):
                    steps.append(-1)

                def along_y():
                    for step in steps:
                        relay(k, s, h, home, dy, 0, step)

                if steps and s == 0:
                    pl.when(dz == 0)(along_y)
                elif steps:
                    along_y()
                if s == 0 or dy == 0:
                    up = (dz == 0) | (dz == 1) if h == 0 else dz == 0
                    down = (dz == 0) | (dz == 3) if h == 1 else dz == 0
                    for step, wanted in ((1, up), (-1, down)):
                        @pl.when(wanted)
                        def _():
                            relay(k, s, h, home, dy, step, 0)

    @pl.when(owner)
    def _():
        load_probe.wait()
        rows = lax.broadcasted_iota(jnp.int32, (PATCH, PATCH), 0)
        cols = lax.broadcasted_iota(jnp.int32, (PATCH, PATCH), 1)
        sort_r = jnp.where(cols == natural(rows), 1.0, 0.0).astype(BF16)
        sort_c = jnp.where(rows == natural(cols), 1.0, 0.0).astype(BF16)
        for ri in range(2):
            plane = mm(sort_r, probe[ri].astype(BF16)).astype(BF16)
            plane = mm(plane, sort_c).astype(BF16)
            for s in range(2):
                modes[0, s, ri * HALF:(ri + 1) * HALF, :] = plane[s * HALF:(s + 1) * HALF]
        take(0)

    send_strip = to(
        strip_b, ext.at[:, pl.ds(PATCH, PATCH), :], strip_sem.at[0], strip_sem.at[1], down_tile, j
    )
    pat_pair = to(pat_hbm.at[slot], pat, pat_sem.at[0], pat_sem.at[1], partner, j)
    load_strip.wait()

    @pl.when(jnp.logical_not(owner))
    def _():
        strip_b[...] = strip[...].astype(BF16)
        send_strip.start()

    @pl.when(owner)
    def _():
        pat_pair.start()
        high = strip[...].astype(BF16)
        ext[:, 0:PATCH, :] = high
        strip_b[...] = (strip[...] - high.astype(F32)).astype(BF16)

    @pl.when(jnp.logical_not(owner))
    def _():
        take(0)

    for k in range(1, 4):
        take(k)

    load_tab.wait()
    info_pair.wait_recv()

    @pl.when(owner)
    def _():
        info[3] = info[0]

    @pl.when(jnp.logical_not(owner))
    def _():
        info[3] = info[1]

    row = info[3, pl.ds(slot, 1), :]
    first_row, first_col, alive = row[:, 0:1], row[:, 1:2], row[:, 2:3]
    rows = lax.broadcasted_iota(jnp.int32, (PATCH, PATCH), 0)
    cols = lax.broadcasted_iota(jnp.int32, (PATCH, PATCH), 1)

    def wrapped(at):
        return jnp.where(at >= PATCH, at - PATCH, at)

    place_r[...] = jnp.where((rows == wrapped(first_row + natural(cols))) & (alive > 0), 1.0, 0.0).astype(BF16)
    place_c[...] = jnp.where(cols == wrapped(first_col + natural(rows)), 1.0, 0.0).astype(BF16)

    send_patch = to(init, init, patch_sem.at[0], patch_sem.at[1], partner, j)

    @pl.when(owner)
    def _():
        send_strip.wait_recv()
        inside = jnp.where(t == 7, PATCH, 2 * PATCH)
        rows = lax.broadcasted_iota(jnp.int32, (PATCH, 2 * PATCH), 0)
        cols = lax.broadcasted_iota(jnp.int32, (PATCH, 2 * PATCH), 1)
        cut_r = jnp.where((cols == first_row + natural(rows)) & (cols < inside), 1.0, 0.0).astype(BF16)
        rows2 = lax.broadcasted_iota(jnp.int32, (2 * PATCH, PATCH), 0)
        cols2 = lax.broadcasted_iota(jnp.int32, (2 * PATCH, PATCH), 1)
        cut_c = jnp.where(rows2 == first_col + natural(cols2), 1.0, 0.0).astype(BF16)
        for ri in range(2):
            high = mm(cut_r, ext[ri]).astype(BF16)
            low = mm(cut_r[:, 0:PATCH], strip_b[ri]).astype(BF16)
            piece = mm(high, cut_c) + mm(low, cut_c)
            for s in range(2):
                init[s, ri * HALF:(ri + 1) * HALF, :] = piece[s * HALF:(s + 1) * HALF]
        send_patch.start()

    for k in range(4, 6):
        take(k)

    @pl.when(owner)
    def _():
        load_pat.wait()
        pat_pair.wait_send()
        send_patch.wait_send()

    @pl.when(jnp.logical_not(owner))
    def _():
        pat_pair.wait_recv()
        send_patch.wait_recv()
        send_strip.wait_send()

    def far_rows(m, b):
        return pl.ds((2 * m + b) * PATCH, PATCH)

    def exit_and_left(m, field, with_power):
        ends = []
        for s in range(2):
            pr = modes[m, s, 0:HALF, :].astype(F32)
            pi = modes[m, s, HALF:PATCH, :].astype(F32)
            cr = field[s, 0:HALF, :]
            ci = field[s, HALF:PATCH, :]
            wave = jnp.concatenate(
                [(pr * cr - pi * ci).astype(BF16), (pr * ci + pi * cr).astype(BF16)], axis=0
            )
            if with_power:
                power[s] += pr * pr + pi * pi
            ends.append(mm(tab[0, s], wave))
        for b, part in enumerate((ends[0] + ends[1], ends[0] - ends[1])):
            part = part.astype(BF16)
            for s in range(2):
                for ri in range(2):
                    half[m, s, b * HALF:(b + 1) * HALF, ri * HALF:(ri + 1) * HALF] = part[
                        ri * HALF:(ri + 1) * HALF, s * HALF:(s + 1) * HALF
                    ]

    def right_and_power(first):
        sums = [0.0, 0.0]
        for m in (first, first + 1):
            even = mm(half[m, 0], tab[1, 0])
            odd = mm(half[m, 1], tab[1, 1])
            for b, part in enumerate((even + odd, even - odd)):
                far[far_rows(m, b), :] = part
                re, im = part[:, 0:HALF], part[:, HALF:PATCH]
                sums[b] += re * re + im * im
        for b in range(2):
            inten[b] = sums[b] if first == 0 else inten[b] + sums[b]

    def change_and_right(m):
        ra, rb = ratio[0], ratio[1]
        ya = far[far_rows(m, 0), :] * jnp.concatenate([ra, ra], axis=1)
        yb = far[far_rows(m, 1), :] * jnp.concatenate([rb, rb], axis=1)
        for s, part in enumerate(((ya + yb).astype(BF16), (ya - yb).astype(BF16))):
            near = mm(part, tab[0, s])
            lo, hi = near[0:HALF], near[HALF:PATCH]
            for b, mixed in enumerate((lo + hi, lo - hi)):
                mixed = mixed.astype(BF16)
                for ri in range(2):
                    half[m, b, ri * HALF:(ri + 1) * HALF, s * HALF:(s + 1) * HALF] = mixed[
                        :, ri * HALF:(ri + 1) * HALF
                    ]

    def left_and_update(first):
        for s in range(2):
            re = im = 0.0
            for m in (first, first + 1):
                near = mm(tab[1, s], half[m, s])
                nr, ni = near[0:HALF], near[HALF:PATCH]
                pr = modes[m, s, 0:HALF, :].astype(F32)
                pi = modes[m, s, HALF:PATCH, :].astype(F32)
                re += pr * nr + pi * ni
                im += pr * ni - pi * nr
            if first == 0:
                upd[s, 0:HALF, :] = re
                upd[s, HALF:PATCH, :] = im
            else:
                upd[s, 0:HALF, :] += re
                upd[s, HALF:PATCH, :] += im

    def swap(src, dst, which):
        copy = to(src, dst, pair_send.at[which], pair_recv.at[which], partner, j)
        copy.start()
        return copy

    power[...] = jnp.zeros_like(power)
    for repeat in range(PASSES):
        last = repeat == PASSES - 1
        if repeat == 0:
            for k in range(4):
                exit_and_left(k, init, True)
            take(6)
            for k in range(4, 6):
                exit_and_left(k, init, True)
            take(7)
            for k in range(6, 8):
                exit_and_left(k, init, True)
        else:
            for k in range(8):
                exit_and_left(k, cur, False)
        for k in range(0, 8, 2):
            right_and_power(k)
        inten_b[repeat] = inten[...].astype(BF16)
        copy = swap(inten_b.at[repeat], inten_in.at[repeat], 3 * repeat)
        if repeat == 0:
            power_b[...] = power[...].astype(BF16)
            power_copy = swap(power_b, power_in, 1)
        copy.wait()
        for b in range(2):
            total = inten[b] + inten_in[repeat, b].astype(F32)
            measured = pat[:, b * HALF:(b + 1) * HALF].astype(F32)
            ratio[b] = jnp.sqrt(measured / jnp.maximum(total, 1.0)) - 1.0

        for k in range(8):
            change_and_right(k)
        for k in range(0, 8, 2):
            left_and_update(k)
        if repeat == 0:
            power_copy.wait()
            whole = power[...] + power_in[...].astype(F32)
            whole = jnp.maximum(whole[0], whole[1])
            highest = jnp.max(jnp.max(whole, axis=0, keepdims=True), axis=1, keepdims=True)
            scale = STEP_SIZE / highest
        if not last:
            upd_b[...] = upd[...].astype(BF16)
            copy = swap(upd_b, upd_in, 2)
            copy.wait()
            for s in range(2):
                cur[s] = init[s] + scale * (upd[s] + upd_in[s].astype(F32))
        else:
            mine = pl.ds(pl.multiple_of(c * HALF, HALF), HALF)
            other = pl.ds(pl.multiple_of((1 - c) * HALF, HALF), HALF)
            last_b[...] = upd[:, other, :].astype(BF16)
            copy = swap(last_b, last_in, 4)
            copy.wait()
            moved = []
            for s in range(2):
                change = cur[s, mine, :] - init[s, mine, :]
                change += scale * (upd[s, mine, :] + last_in[s].astype(F32))
                moved.append(change.astype(BF16))
            moved = jnp.concatenate(moved, axis=0)

    placed = mm(place_r[...], moved).astype(BF16)
    canvas[...] = mm(placed, place_c[...]).astype(BF16)

    for step in range(16):
        mode = (j + step) % 16
        src = canvas.at[pl.ds(pl.multiple_of(mode * SLAB, SLAB), SLAB), :]
        dst = slabs.at[c * 8 + slot]
        if step == 0:
            @pl.when(owner)
            def _():
                pltpu.make_async_copy(src, dst, slab_recv).start()

            @pl.when(jnp.logical_not(owner))
            def _():
                to(src, dst, slab_send, slab_recv, s_tile, mode).start()
        else:
            to(src, dst, slab_send, slab_recv, s_tile, mode).start()

    @pl.when(c == 0)
    def _():
        info_next.wait_recv()
        info[4] = info[2]

    @pl.when(c == 1)
    def _():
        info[4] = info[1]

    at_row = lax.broadcasted_iota(jnp.int32, (SLAB, 2 * PATCH), 0) + j * SLAB
    at_col = lax.broadcasted_iota(jnp.int32, (SLAB, 2 * PATCH), 1)
    from_above = jnp.where(t > 0, 1.0, 0.0)
    cover = jnp.zeros((SLAB, 2 * PATCH), F32)
    for k in range(2):
        here = info[4 * k]
        part = jnp.zeros((SLAB, 2 * PATCH), F32)
        for i in range(8):
            dr = at_row + k * PATCH - here[i:i + 1, 0:1]
            dc = at_col - here[i:i + 1, 1:2]
            inside = (dr >= 0) & (dr < PATCH) & (dc >= 0) & (dc < PATCH) & (here[i:i + 1, 2:3] > 0)
            part += jnp.where(inside, 1.0, 0.0)
        cover += part if k == 0 else part * from_above
    share = 1.0 / jnp.maximum(cover, 1.0)

    pltpu.make_async_copy(slabs, slabs, slab_recv).wait()
    at_row = lax.broadcasted_iota(jnp.int32, (SLAB, PATCH), 0) + j * SLAB
    at_col = lax.broadcasted_iota(jnp.int32, (SLAB, PATCH), 1)
    own = []
    for ri in range(2):
        parts = [jnp.zeros((SLAB, PATCH), F32) for _ in range(4)]
        for i in range(8):
            value = slabs[ri * 8 + i].astype(F32)
            in_strip = at_row >= info[0, i:i + 1, 0:1]
            in_left = at_col >= info[0, i:i + 1, 1:2]
            left = jnp.where(in_left, value, 0.0)
            right = value - left
            left_own = jnp.where(in_strip, left, 0.0)
            right_own = jnp.where(in_strip, right, 0.0)
            for p, term in enumerate((left_own, right_own, left - left_own, right - right_own)):
                parts[p] += term
        own.append(jnp.concatenate(parts[0:2], axis=1))
        spill[ri] = jnp.concatenate(parts[2:4], axis=1).astype(BF16)

    spill_copy = to(spill, spill_in, spill_sem.at[0], spill_sem.at[1], up_tile, j)
    spill_copy.start()
    spill_copy.wait()
    ring_y[y] = ((own[0] + spill_in[0].astype(F32) * from_above) * share).astype(BF16)
    ring_z[z] = ((own[1] + spill_in[1].astype(F32) * from_above) * share).astype(BF16)

    for k in range(1, 4):
        to(ring_y.at[y], ring_y.at[y], ring_send.at[0], ring_recv.at[0], t, 4 * z + (y + k) % 4).start()
        to(ring_z.at[z], ring_z.at[z], ring_send.at[1], ring_recv.at[1], t, 4 * ((z + k) % 4) + y).start()
    keep = (
        pltpu.make_async_copy(ring_y, out_hbm.at[0, z], local_sem.at[4]),
        pltpu.make_async_copy(ring_z, out_hbm.at[1, :, y], local_sem.at[5]),
    )
    three = ring_y.at[pl.ds(0, 3)]
    for p in range(2):
        pltpu.make_async_copy(three, three, ring_recv.at[p]).wait()
        for k in range(1, 4):
            if p == 0:
                to(ring_y, out_hbm.at[0, z], ring_send.at[2], ring_recv.at[2], t, 4 * ((z + k) % 4) + y).start()
            else:
                to(ring_z, out_hbm.at[1, :, y], ring_send.at[3], ring_recv.at[3], t, 4 * z + (y + k) % 4).start()
        keep[p].start()

    info_pair.wait_send()

    @pl.when(c == 1)
    def _():
        info_next.wait_send()

    for here, count in ((owner, 43), (jnp.logical_not(owner), 17)):
        @pl.when(here)
        def _():
            rows = far.at[pl.ds(0, count * 64), :]
            pltpu.make_async_copy(rows, rows, gather_send).wait()

    for here, count in ((owner, 15), (jnp.logical_not(owner), 16)):
        @pl.when(here)
        def _():
            rows = slabs.at[pl.ds(0, count)]
            pltpu.make_async_copy(rows, rows, slab_send).wait()

    rings = strip.at[0, pl.ds(0, 96), :]
    for p in range(2):
        pltpu.make_async_copy(three, three, ring_send.at[p]).wait()
        pltpu.make_async_copy(rings, rings, ring_send.at[2 + p]).wait()
        pltpu.make_async_copy(rings, rings, ring_recv.at[2 + p]).wait()
        keep[p].wait()


def shards(object_field, probe_modes, patterns, offsets, counts):
    tables = jnp.asarray(make_tables())
    any_space = pl.BlockSpec(memory_space=pl.ANY)
    vmem = pltpu.VMEM
    dma = pltpu.SemaphoreType.DMA
    change = pl.pallas_call(
        kernel,
        out_shape=jax.ShapeDtypeStruct((2, 4, 4, SLAB, 2 * PATCH), BF16),
        in_specs=[
            any_space, any_space, any_space, any_space,
            pl.BlockSpec(memory_space=vmem),
            pl.BlockSpec(memory_space=pltpu.SMEM),
        ],
        out_specs=any_space,
        scratch_shapes=[
            vmem((2, PATCH, PATCH), F32),
            vmem((2, PATCH, 2 * PATCH), F32),
            vmem((2, PATCH, 2 * PATCH), BF16),
            vmem((2, 2 * PATCH, 2 * PATCH), BF16),
            vmem((PATCH, PATCH), BF16),
            vmem((2, 2, PATCH, PATCH), BF16),
            vmem((5, 8, HALF), jnp.int32),
            vmem((8, 2, PATCH, PATCH), BF16),
            vmem((8, 2, PATCH, PATCH), BF16),
            vmem((16 * PATCH, PATCH), F32),
            vmem((2, PATCH, PATCH), F32),
            vmem((2, PATCH, PATCH), F32),
            vmem((2, PATCH, HALF), F32),
            vmem((2, PATCH, HALF), F32),
            vmem((2, PATCH, PATCH), F32),
            vmem((2, HALF, PATCH), F32),
            vmem((PASSES, 2, PATCH, HALF), BF16),
            vmem((2, PATCH, PATCH), BF16),
            vmem((2, HALF, PATCH), BF16),
            vmem((2, HALF, PATCH), BF16),
            vmem((PASSES, 2, PATCH, HALF), BF16),
            vmem((2, PATCH, PATCH), BF16),
            vmem((2, HALF, PATCH), BF16),
            vmem((2, HALF, PATCH), BF16),
            vmem((PATCH, PATCH), BF16),
            vmem((PATCH, PATCH), BF16),
            vmem((PATCH, PATCH), BF16),
            vmem((16, SLAB, PATCH), BF16),
            vmem((2, SLAB, 2 * PATCH), BF16),
            vmem((2, SLAB, 2 * PATCH), BF16),
            vmem((4, SLAB, 2 * PATCH), BF16),
            vmem((4, SLAB, 2 * PATCH), BF16),
            dma((6,)), dma, dma((8, 2, 2)), dma((2,)), dma((4,)), dma((2,)), dma((2,)),
            dma((5,)), dma((5,)), dma, dma, dma((2,)), dma((4,)), dma((4,)),
        ],
        compiler_params=pltpu.CompilerParams(
            collective_id=0, has_side_effects=True, vmem_limit_bytes=60 * 1024 * 1024
        ),
        cost_estimate=pl.CostEstimate(flops=6 * 10**9, bytes_accessed=8 * 2**20, transcendentals=131072),
    )(object_field, probe_modes, patterns, tables, offsets, counts)
    return object_field + change.reshape(object_field.shape).astype(F32)


def solution(mesh):
    return jax.shard_map(
        shards,
        mesh=mesh,
        in_specs=(
            P(None, "tile", None),
            P("mode", None, None, None),
            P("tile", None, None),
            P("tile", None),
            P("tile"),
        ),
        out_specs=P(None, "tile", None),
        check_vma=False,
    )
```

```python
import math

import numpy as np
import ml_dtypes
import jax
import jax.numpy as jnp
from jax import lax
from jax.experimental import pallas as pl
from jax.experimental.pallas import tpu as pltpu
from jax.sharding import PartitionSpec as P

PATCH = 256
HALF = 128
PASSES = 2
STEP_SIZE = 0.9
SLAB = 16
MESH = pl.DeviceIdType.MESH
BF16 = jnp.bfloat16
F32 = jnp.float32

ORDER = ((0, 0), (1, 0), (0, 1), (0, 3), (1, 1), (1, 3), (0, 2), (1, 2))
FAR_FIRST = sorted(
    ((dz, dy) for dz in range(4) for dy in range(4)), key=lambda d: -min(d[0], 4 - d[0]) - min(d[1], 4 - d[1])
)


def make_tables():
    q = np.arange(HALF)
    tables = []
    for s in range(2):
        a = 2 * np.arange(HALF) + s
        angle = (q[:, None] * a[None, :] % PATCH).astype(np.float32) * np.float32(2.0 * math.pi / PATCH)
        factor = np.float32(1.0 / math.sqrt(PATCH))
        real = (np.cos(angle) * factor).astype(ml_dtypes.bfloat16)
        imag = (-np.sin(angle) * factor).astype(ml_dtypes.bfloat16)
        tables.append(np.block([[real, -imag], [imag, real]]))
    tables = np.stack(tables)
    return np.stack([tables, tables.transpose(0, 2, 1)])


def mm(a, b):
    return jnp.dot(a, b, preferred_element_type=F32)


def natural(position):
    return jnp.where(position < HALF, 2 * position, 2 * position - (PATCH - 1))


def kernel(
    obj_hbm, probe_hbm, pat_hbm, tab_hbm, offs_ref, counts_ref, out_hbm,
    probe, strip, strip_b, ext, pat, tab, info, modes, half, far, init, cur,
    inten, ratio, upd, power, inten_b, upd_b, last_b, power_b, inten_in, upd_in, last_in, power_in,
    place_r, place_c, canvas, slabs, spill, spill_in, own, quot,
    local_sem, gather_send, gather_recv, strip_sem, info_sem, patch_sem, pat_sem,
    pair_send, pair_recv, slab_send, slab_recv, spill_sem, quot_send, quot_recv,
):
    t = lax.axis_index("tile")
    j = lax.axis_index("mode")
    x, z = t // 2, j // 4
    c, y = t - 2 * x, j - 4 * z
    group = z // 2
    owner = c == group
    s_tile = 2 * x + group
    slot = j - 8 * group
    partner = 2 * x + (1 - c)
    up_tile, down_tile = t + 1, t - 1

    load_probe = pltpu.make_async_copy(probe_hbm.at[0], probe, local_sem.at[0])
    load_strip = pltpu.make_async_copy(obj_hbm, strip, local_sem.at[1])
    load_tab = pltpu.make_async_copy(tab_hbm, tab, local_sem.at[2])
    load_pat = pltpu.make_async_copy(pat_hbm.at[slot], pat, local_sem.at[3])
    @pl.when(owner)
    def _():
        load_probe.start()
        load_pat.start()

    load_strip.start()
    load_tab.start()

    barrier = pltpu.get_barrier_semaphore()

    def greet(tile, mode):
        pl.semaphore_signal(barrier, inc=1, device_id=(tile, mode), device_id_type=MESH)

    for k in range(1, 16):
        greet(t, (j + k) % 16)
    greet(partner, j)
    has_up, has_down = t < 7, t > 0
    to_next_x = (c == 1) & has_up
    to_prev_x = (c == 0) & has_down

    @pl.when(to_next_x)
    def _():
        greet(up_tile, j)

    @pl.when(to_prev_x)
    def _():
        greet(down_tile, j)
        for k in range(8):
            for core in range(2):
                greet(2 * x - 2 + core, 8 + k)

    for k in range(8):
        greet(partner, 8 * c + k)

    lane = lax.broadcasted_iota(jnp.int32, (8, HALF), 1)
    live = (lax.broadcasted_iota(jnp.int32, (8, HALF), 0) < counts_ref[0]).astype(jnp.int32)
    place = jnp.where(lane == 2, live, 0)
    line = lax.broadcasted_iota(jnp.int32, (8, HALF), 0)
    for i in range(8):
        for p in range(2):
            place = jnp.where((line == i) & (lane == p), offs_ref[p, i], place)
    info[0] = place

    @pl.when(jnp.logical_not(has_down))
    def _():
        info[2] = jnp.zeros((8, HALF), jnp.int32)


    far_slabs = (group == 1) & (x < 3)
    across = to_next_x | to_prev_x
    pl.semaphore_wait(
        barrier, 16 + jnp.where(across, 1, 0) + jnp.where(owner, 0, 16) + jnp.where(far_slabs, 16, 0)
    )

    def to(src, dst, send, recv, tile, mode):
        return pltpu.make_async_remote_copy(
            src_ref=src, dst_ref=dst, send_sem=send, recv_sem=recv,
            device_id=(tile, mode), device_id_type=MESH,
        )

    info_pair = to(info.at[0], info.at[1], info_sem.at[0], info_sem.at[1], partner, j)
    info_next = to(info.at[0], info.at[2], info_sem.at[2], info_sem.at[3], up_tile, j)
    info_pair.start()

    @pl.when(to_next_x)
    def _():
        info_next.start()

    def block(m, s, h):
        return modes.at[m, s, pl.ds(h * HALF, HALF), :]

    def mode_slot(row, home, dy):
        d = (row - 2 * c + 4) % 4
        nearer = 2 * c + jnp.where((d == 1) | (d == 2), 1, 0)
        return jnp.where(home == nearer, ORDER.index((0, dy)), ORDER.index((1, dy)))

    def relay(k, s, h, home, dy, step_z, step_y):
        row = (z + step_z + 4) % 4
        there = mode_slot(row, home, (dy + step_y) % 4)
        to(
            block(k, s, h), block(there, s, h), gather_send, gather_recv.at[there, s, h],
            t, row * 4 + (y + step_y + 4) % 4,
        ).start()

    def take(k):
        which, dy = ORDER[k]
        d = (z - 2 * c + 4) % 4
        nearer = jnp.where((d == 1) | (d == 2), 1, 0)
        home = 2 * c + (nearer if which == 0 else 1 - nearer)
        dz = (z - home + 4) % 4
        for h in range(2):
            for s in range(2):
                def wait():
                    to(
                        block(k, s, h), block(k, s, h), gather_send, gather_recv.at[k, s, h], t, j
                    ).wait_recv()

                if k == 0:
                    pl.when(dz != 0)(wait)
                else:
                    wait()
                if s == 0 and dy == 0:
                    @pl.when(dz == 0)
                    def _():
                        for step in (2, 1, -1):
                            relay(k, s, h, home, dy, 0, step)

                if s == 1 and dy == 0:
                    @pl.when(dz == 2)
                    def _():
                        relay(k, s, h, home, dy, 0, 2)

                    for step in (1, -1):
                        relay(k, s, h, home, dy, 0, step)
                if s == 1 and (dy, h) in ((1, 0), (3, 1)):
                    @pl.when(dz != 2)
                    def _():
                        relay(k, s, h, home, dy, 0, 2 - dy)

                if s == 0 or dy == 0:
                    @pl.when(dz == 0)
                    def _():
                        if s == 1 or dy == 2:
                            relay(k, s, h, home, dy, 2, 0)
                        relay(k, s, h, home, dy, 1, 0)
                        relay(k, s, h, home, dy, -1, 0)

                if s == 0 and dy != 2:
                    @pl.when(dz == (1 if h == 0 else 3))
                    def _():
                        relay(k, s, h, home, dy, 1 if h == 0 else -1, 0)

    @pl.when(owner)
    def _():
        load_probe.wait()
        rows = lax.broadcasted_iota(jnp.int32, (PATCH, PATCH), 0)
        cols = lax.broadcasted_iota(jnp.int32, (PATCH, PATCH), 1)
        sort_r = jnp.where(cols == natural(rows), 1.0, 0.0).astype(BF16)
        sort_c = jnp.where(rows == natural(cols), 1.0, 0.0).astype(BF16)
        for ri in range(2):
            plane = mm(sort_r, probe[ri].astype(BF16)).astype(BF16)
            plane = mm(plane, sort_c).astype(BF16)
            for s in range(2):
                modes[0, s, ri * HALF:(ri + 1) * HALF, :] = plane[s * HALF:(s + 1) * HALF]
        take(0)

    send_strip = to(
        strip_b, ext.at[:, pl.ds(PATCH, PATCH), :], strip_sem.at[0], strip_sem.at[1], down_tile, j
    )
    pat_pair = to(pat_hbm.at[slot], pat, pat_sem.at[0], pat_sem.at[1], partner, j)
    load_strip.wait()

    sends_strip = jnp.logical_not(owner) & has_down

    @pl.when(sends_strip)
    def _():
        strip_b[...] = strip[...].astype(BF16)
        send_strip.start()

    @pl.when(t == 7)
    def _():
        ext[:, PATCH:2 * PATCH, :] = jnp.zeros((2, PATCH, 2 * PATCH), BF16)

    @pl.when(owner)
    def _():
        pat_pair.start()
        high = strip[...].astype(BF16)
        ext[:, 0:PATCH, :] = high
        strip_b[...] = (strip[...] - high.astype(F32)).astype(BF16)

    @pl.when(jnp.logical_not(owner))
    def _():
        take(0)

    for k in range(1, 4):
        take(k)

    load_tab.wait()
    info_pair.wait_recv()

    @pl.when(owner)
    def _():
        info[3] = info[0]

    @pl.when(jnp.logical_not(owner))
    def _():
        info[3] = info[1]

    row = info[3, pl.ds(slot, 1), :]
    first_row, first_col, alive = row[:, 0:1], row[:, 1:2], row[:, 2:3]
    rows = lax.broadcasted_iota(jnp.int32, (PATCH, PATCH), 0)
    cols = lax.broadcasted_iota(jnp.int32, (PATCH, PATCH), 1)

    def wrapped(at):
        return jnp.where(at >= PATCH, at - PATCH, at)

    place_r[...] = jnp.where((rows == wrapped(first_row + natural(cols))) & (alive > 0), 1.0, 0.0).astype(BF16)
    place_c[...] = jnp.where(cols == wrapped(first_col + natural(rows)), 1.0, 0.0).astype(BF16)

    send_patch = to(init, init, patch_sem.at[0], patch_sem.at[1], partner, j)

    @pl.when(owner)
    def _():
        @pl.when(has_up)
        def _():
            send_strip.wait_recv()

        inside = jnp.where(t == 7, PATCH, 2 * PATCH)
        rows = lax.broadcasted_iota(jnp.int32, (PATCH, 2 * PATCH), 0)
        cols = lax.broadcasted_iota(jnp.int32, (PATCH, 2 * PATCH), 1)
        cut_r = jnp.where((cols == first_row + natural(rows)) & (cols < inside), 1.0, 0.0).astype(BF16)
        rows2 = lax.broadcasted_iota(jnp.int32, (2 * PATCH, PATCH), 0)
        cols2 = lax.broadcasted_iota(jnp.int32, (2 * PATCH, PATCH), 1)
        cut_c = jnp.where(rows2 == first_col + natural(cols2), 1.0, 0.0).astype(BF16)
        for ri in range(2):
            high = mm(cut_r, ext[ri]).astype(BF16)
            low = mm(cut_r[:, 0:PATCH], strip_b[ri]).astype(BF16)
            piece = mm(high, cut_c) + mm(low, cut_c)
            for s in range(2):
                init[s, ri * HALF:(ri + 1) * HALF, :] = piece[s * HALF:(s + 1) * HALF]
        send_patch.start()

    for k in range(4, 6):
        take(k)

    @pl.when(owner)
    def _():
        load_pat.wait()
        pat_pair.wait_send()
        send_patch.wait_send()

    @pl.when(jnp.logical_not(owner))
    def _():
        pat_pair.wait_recv()
        send_patch.wait_recv()

    @pl.when(sends_strip)
    def _():
        send_strip.wait_send()

    def far_rows(m, b):
        return pl.ds((2 * m + b) * PATCH, PATCH)

    def exit_and_left(m, field, with_power):
        ends = []
        for s in range(2):
            pr = modes[m, s, 0:HALF, :].astype(F32)
            pi = modes[m, s, HALF:PATCH, :].astype(F32)
            cr = field[s, 0:HALF, :]
            ci = field[s, HALF:PATCH, :]
            wave = jnp.concatenate(
                [(pr * cr - pi * ci).astype(BF16), (pr * ci + pi * cr).astype(BF16)], axis=0
            )
            if with_power:
                power[s] += pr * pr + pi * pi
            ends.append(mm(tab[0, s], wave))
        for b, part in enumerate((ends[0] + ends[1], ends[0] - ends[1])):
            part = part.astype(BF16)
            for s in range(2):
                for ri in range(2):
                    half[m, s, b * HALF:(b + 1) * HALF, ri * HALF:(ri + 1) * HALF] = part[
                        ri * HALF:(ri + 1) * HALF, s * HALF:(s + 1) * HALF
                    ]

    def right_and_power(first):
        sums = [0.0, 0.0]
        for m in (first, first + 1):
            even = mm(half[m, 0], tab[1, 0])
            odd = mm(half[m, 1], tab[1, 1])
            for b, part in enumerate((even + odd, even - odd)):
                far[far_rows(m, b), :] = part
                re, im = part[:, 0:HALF], part[:, HALF:PATCH]
                sums[b] += re * re + im * im
        for b in range(2):
            inten[b] = sums[b] if first == 0 else inten[b] + sums[b]

    def change_and_right(m):
        ra, rb = ratio[0], ratio[1]
        ya = far[far_rows(m, 0), :] * jnp.concatenate([ra, ra], axis=1)
        yb = far[far_rows(m, 1), :] * jnp.concatenate([rb, rb], axis=1)
        for s, part in enumerate(((ya + yb).astype(BF16), (ya - yb).astype(BF16))):
            near = mm(part, tab[0, s])
            lo, hi = near[0:HALF], near[HALF:PATCH]
            for b, mixed in enumerate((lo + hi, lo - hi)):
                mixed = mixed.astype(BF16)
                for ri in range(2):
                    half[m, b, ri * HALF:(ri + 1) * HALF, s * HALF:(s + 1) * HALF] = mixed[
                        :, ri * HALF:(ri + 1) * HALF
                    ]

    def left_and_update(first):
        for s in range(2):
            re = im = 0.0
            for m in (first, first + 1):
                near = mm(tab[1, s], half[m, s])
                nr, ni = near[0:HALF], near[HALF:PATCH]
                pr = modes[m, s, 0:HALF, :].astype(F32)
                pi = modes[m, s, HALF:PATCH, :].astype(F32)
                re += pr * nr + pi * ni
                im += pr * ni - pi * nr
            if first == 0:
                upd[s, 0:HALF, :] = re
                upd[s, HALF:PATCH, :] = im
            else:
                upd[s, 0:HALF, :] += re
                upd[s, HALF:PATCH, :] += im

    def swap(src, dst, which):
        copy = to(src, dst, pair_send.at[which], pair_recv.at[which], partner, j)
        copy.start()
        return copy

    power[...] = jnp.zeros_like(power)
    for repeat in range(PASSES):
        last = repeat == PASSES - 1
        if repeat == 0:
            for k in range(4):
                exit_and_left(k, init, True)
            take(6)
            for k in range(4, 6):
                exit_and_left(k, init, True)
            take(7)
            for k in range(6, 8):
                exit_and_left(k, init, True)
        else:
            for k in range(8):
                exit_and_left(k, cur, False)
        for k in range(0, 8, 2):
            right_and_power(k)
        inten_b[repeat] = inten[...].astype(BF16)
        copy = swap(inten_b.at[repeat], inten_in.at[repeat], 3 * repeat)
        if repeat == 0:
            power_b[...] = power[...].astype(BF16)
            power_copy = swap(power_b, power_in, 1)
        copy.wait()
        for b in range(2):
            total = inten[b] + inten_in[repeat, b].astype(F32)
            measured = pat[:, b * HALF:(b + 1) * HALF].astype(F32)
            ratio[b] = jnp.sqrt(measured / jnp.maximum(total, 1.0)) - 1.0

        for k in range(8):
            change_and_right(k)
        for k in range(0, 8, 2):
            left_and_update(k)
        if repeat == 0:
            power_copy.wait()
            whole = power[...] + power_in[...].astype(F32)
            whole = jnp.maximum(whole[0], whole[1])
            highest = jnp.max(jnp.max(whole, axis=0, keepdims=True), axis=1, keepdims=True)
            scale = STEP_SIZE / highest
        if not last:
            upd_b[...] = upd[...].astype(BF16)
            copy = swap(upd_b, upd_in, 2)
            copy.wait()
            for s in range(2):
                cur[s] = init[s] + scale * (upd[s] + upd_in[s].astype(F32))
        else:
            mine = pl.ds(pl.multiple_of(c * HALF, HALF), HALF)
            other = pl.ds(pl.multiple_of((1 - c) * HALF, HALF), HALF)
            last_b[...] = upd[:, other, :].astype(BF16)
            copy = swap(last_b, last_in, 4)
            copy.wait()
            moved = []
            for s in range(2):
                change = cur[s, mine, :] - init[s, mine, :]
                change += scale * (upd[s, mine, :] + last_in[s].astype(F32))
                moved.append(change.astype(BF16))
            moved = jnp.concatenate(moved, axis=0)

    placed = mm(place_r[...], moved).astype(BF16)
    canvas[...] = mm(placed, place_c[...]).astype(BF16)

    for dz, dy in FAR_FIRST:
        mode = ((z + dz) % 4) * 4 + (y + dy) % 4
        src = canvas.at[pl.ds(pl.multiple_of(mode * SLAB, SLAB), SLAB), :]
        dst = slabs.at[c * 8 + slot]

        @pl.when(far_slabs)
        def _():
            to(src, slabs.at[16 + c * 8 + slot], slab_send, slab_recv.at[1], s_tile + 1, mode).start()

        if (dz, dy) == (0, 0):
            @pl.when(owner)
            def _():
                pltpu.make_async_copy(src, dst, slab_recv.at[0]).start()

            @pl.when(jnp.logical_not(owner))
            def _():
                to(src, dst, slab_send, slab_recv.at[0], s_tile, mode).start()
        else:
            to(src, dst, slab_send, slab_recv.at[0], s_tile, mode).start()

    @pl.when(to_prev_x)
    def _():
        info_next.wait_recv()

    @pl.when(c == 0)
    def _():
        info[4] = info[2]

    @pl.when(c == 1)
    def _():
        info[4] = info[1]

    at_row = lax.broadcasted_iota(jnp.int32, (SLAB, 2 * PATCH), 0) + j * SLAB
    at_col = lax.broadcasted_iota(jnp.int32, (SLAB, 2 * PATCH), 1)
    from_above = jnp.where(t > 0, 1.0, 0.0)
    cover = jnp.zeros((SLAB, 2 * PATCH), F32)
    for k in range(2):
        here = info[4 * k]
        part = jnp.zeros((SLAB, 2 * PATCH), F32)
        for i in range(8):
            dr = at_row + k * PATCH - here[i:i + 1, 0:1]
            dc = at_col - here[i:i + 1, 1:2]
            inside = (dr >= 0) & (dr < PATCH) & (dc >= 0) & (dc < PATCH) & (here[i:i + 1, 2:3] > 0)
            part += jnp.where(inside, 1.0, 0.0)
        cover += part if k == 0 else part * from_above
    share = 1.0 / jnp.maximum(cover, 1.0)

    at_row = lax.broadcasted_iota(jnp.int32, (SLAB, PATCH), 0) + j * SLAB
    at_col = lax.broadcasted_iota(jnp.int32, (SLAB, PATCH), 1)

    def gathered(which, table, ri):
        parts = [jnp.zeros((SLAB, PATCH), F32) for _ in range(4)]
        for i in range(8):
            value = slabs[which * 16 + ri * 8 + i].astype(F32)
            in_strip = at_row >= info[table, i:i + 1, 0:1]
            in_left = at_col >= info[table, i:i + 1, 1:2]
            left = jnp.where(in_left, value, 0.0)
            right = value - left
            left_own = jnp.where(in_strip, left, 0.0)
            right_own = jnp.where(in_strip, right, 0.0)
            for p, term in enumerate((left_own, right_own, left - left_own, right - right_own)):
                parts[p] += term
        return jnp.concatenate(parts[0:2], axis=1), jnp.concatenate(parts[2:4], axis=1)

    first16 = slabs.at[pl.ds(0, 16)]
    pltpu.make_async_copy(first16, first16, slab_recv.at[0]).wait()
    spill_copy = to(spill, spill_in, spill_sem.at[0], spill_sem.at[1], partner, j)
    sums = [gathered(0, 0, ri) for ri in range(2)]
    for ri in range(2):
        own[ri] = sums[ri][0]

    @pl.when(c == 0)
    def _():
        for ri in range(2):
            spill[ri] = sums[ri][1].astype(BF16)
        spill_copy.start()

    @pl.when(to_prev_x)
    def _():
        pltpu.make_async_copy(first16, first16, slab_recv.at[1]).wait()
        for ri in range(2):
            own[ri] += gathered(1, 2, ri)[1]

    @pl.when(c == 1)
    def _():
        spill_copy.wait_recv()
        for ri in range(2):
            own[ri] += spill_in[ri].astype(F32)

    my_rows = out_hbm.at[:, pl.ds(pl.multiple_of(j * SLAB, SLAB), SLAB), :]
    for ri in range(2):
        quot[ri] = (own[ri] * share).astype(BF16)
    for dz, dy in FAR_FIRST[:15]:
        to(quot, my_rows, quot_send, quot_recv, t, ((z + dz) % 4) * 4 + (y + dy) % 4).start()
    keep = pltpu.make_async_copy(quot, my_rows, local_sem.at[4])
    keep.start()

    info_pair.wait_send()

    @pl.when(to_next_x)
    def _():
        info_next.wait_send()

    @pl.when(c == 0)
    def _():
        spill_copy.wait_send()

    for here, count in ((owner, 45), (jnp.logical_not(owner), 15)):
        @pl.when(here)
        def _():
            rows = far.at[pl.ds(0, count * 64), :]
            pltpu.make_async_copy(rows, rows, gather_send).wait()

    for is_owner in (0, 1):
        for is_far in (0, 1):
            @pl.when((owner == (is_owner == 1)) & (far_slabs == (is_far == 1)))
            def _():
                rows = slabs.at[pl.ds(0, 16 - is_owner + 16 * is_far)]
                pltpu.make_async_copy(rows, rows, slab_send).wait()

    rows = strip.at[0, pl.ds(0, 15 * SLAB), :]
    pltpu.make_async_copy(rows, rows, quot_send).wait()
    pltpu.make_async_copy(rows, rows, quot_recv).wait()
    keep.wait()


def shards(object_field, probe_modes, patterns, offsets, counts):
    tables = jnp.asarray(make_tables())
    in_hbm = pl.BlockSpec(memory_space=pltpu.HBM)
    vmem = pltpu.VMEM
    dma = pltpu.SemaphoreType.DMA
    change = pl.pallas_call(
        kernel,
        out_shape=jax.ShapeDtypeStruct((2, PATCH, 2 * PATCH), BF16),
        in_specs=[
            in_hbm, in_hbm, in_hbm, in_hbm,
            pl.BlockSpec(memory_space=pltpu.SMEM),
            pl.BlockSpec(memory_space=pltpu.SMEM),
        ],
        out_specs=pl.BlockSpec(memory_space=pl.ANY),
        scratch_shapes=[
            vmem((2, PATCH, PATCH), F32),
            vmem((2, PATCH, 2 * PATCH), F32),
            vmem((2, PATCH, 2 * PATCH), BF16),
            vmem((2, 2 * PATCH, 2 * PATCH), BF16),
            vmem((PATCH, PATCH), BF16),
            vmem((2, 2, PATCH, PATCH), BF16),
            vmem((5, 8, HALF), jnp.int32),
            vmem((8, 2, PATCH, PATCH), BF16),
            vmem((8, 2, PATCH, PATCH), BF16),
            vmem((16 * PATCH, PATCH), F32),
            vmem((2, PATCH, PATCH), F32),
            vmem((2, PATCH, PATCH), F32),
            vmem((2, PATCH, HALF), F32),
            vmem((2, PATCH, HALF), F32),
            vmem((2, PATCH, PATCH), F32),
            vmem((2, HALF, PATCH), F32),
            vmem((PASSES, 2, PATCH, HALF), BF16),
            vmem((2, PATCH, PATCH), BF16),
            vmem((2, HALF, PATCH), BF16),
            vmem((2, HALF, PATCH), BF16),
            vmem((PASSES, 2, PATCH, HALF), BF16),
            vmem((2, PATCH, PATCH), BF16),
            vmem((2, HALF, PATCH), BF16),
            vmem((2, HALF, PATCH), BF16),
            vmem((PATCH, PATCH), BF16),
            vmem((PATCH, PATCH), BF16),
            vmem((PATCH, PATCH), BF16),
            vmem((32, SLAB, PATCH), BF16),
            vmem((2, SLAB, 2 * PATCH), BF16),
            vmem((2, SLAB, 2 * PATCH), BF16),
            vmem((2, SLAB, 2 * PATCH), F32),
            vmem((2, SLAB, 2 * PATCH), BF16),
            dma((5,)), dma, dma((8, 2, 2)), dma((2,)), dma((4,)), dma((2,)), dma((2,)),
            dma((5,)), dma((5,)), dma, dma((2,)), dma((2,)), dma, dma,
        ],
        compiler_params=pltpu.CompilerParams(
            collective_id=0, has_side_effects=True, vmem_limit_bytes=40 * 1024 * 1024
        ),
        cost_estimate=pl.CostEstimate(flops=6 * 10**9, bytes_accessed=8 * 2**20, transcendentals=131072),
    )(object_field, probe_modes, patterns, tables, offsets.T, counts)
    return object_field + change.astype(F32)


def solution(mesh):
    return jax.shard_map(
        shards,
        mesh=mesh,
        in_specs=(
            P(None, "tile", None),
            P("mode", None, None, None),
            P("tile", None, None),
            P("tile", None),
            P("tile"),
        ),
        out_specs=P(None, "tile", None),
        check_vma=False,
    )
```

```python
import math

import numpy as np
import ml_dtypes
import jax
import jax.numpy as jnp
from jax import lax
from jax.experimental import pallas as pl
from jax.experimental.pallas import tpu as pltpu
from jax.sharding import PartitionSpec as P

PATCH = 256
HALF = 128
PASSES = 2
STEP_SIZE = 0.9
SLAB = 16
MESH = pl.DeviceIdType.MESH
BF16 = jnp.bfloat16
F32 = jnp.float32

ORDER = ((0, 0), (1, 0), (0, 1), (0, 3), (0, 2), (1, 1), (1, 3), (1, 2))
FAR_FIRST = sorted(
    ((dz, dy) for dz in range(4) for dy in range(4)), key=lambda d: -min(d[0], 4 - d[0]) - min(d[1], 4 - d[1])
)


def make_tables():
    q = np.arange(HALF)
    tables = []
    for s in range(2):
        a = 2 * np.arange(HALF) + s
        angle = (q[:, None] * a[None, :] % PATCH).astype(np.float32) * np.float32(2.0 * math.pi / PATCH)
        factor = np.float32(1.0 / math.sqrt(PATCH))
        real = (np.cos(angle) * factor).astype(ml_dtypes.bfloat16)
        imag = (-np.sin(angle) * factor).astype(ml_dtypes.bfloat16)
        tables.append(np.block([[real, -imag], [imag, real]]))
    tables = np.stack(tables)
    return np.stack([tables, tables.transpose(0, 2, 1)])


def mm(a, b):
    return jnp.dot(a, b, preferred_element_type=F32)


def natural(position):
    return jnp.where(position < HALF, 2 * position, 2 * position - (PATCH - 1))


def kernel(
    obj_hbm, probe_hbm, pat_hbm, tab_hbm, offs_ref, counts_ref, out_ref,
    probe, strip, strip_b, ext, pat, tab, info, modes, half, far, init, cur,
    inten, ratio, upd, power, inten_b, upd_b, last_b, power_b, inten_in, upd_in, last_in, power_in,
    place_r, place_c, canvas, slabs, spill, spill_in, own, quot,
    local_sem, gather_send, gather_recv, strip_sem, info_sem, patch_sem, pat_sem,
    pair_send, pair_recv, slab_send, slab_recv, spill_sem, quot_send, quot_recv,
):
    t = lax.axis_index("tile")
    j = lax.axis_index("mode")
    x, z = t // 2, j // 4
    c, y = t - 2 * x, j - 4 * z
    group = z // 2
    owner = c == group
    s_tile = 2 * x + group
    slot = j - 8 * group
    partner = 2 * x + (1 - c)
    up_tile, down_tile = t + 1, t - 1

    load_probe = pltpu.make_async_copy(probe_hbm.at[0], probe, local_sem.at[0])
    load_strip = pltpu.make_async_copy(obj_hbm, strip, local_sem.at[1])
    load_tab = pltpu.make_async_copy(tab_hbm, tab, local_sem.at[2])
    load_pat = pltpu.make_async_copy(pat_hbm.at[slot], pat, local_sem.at[3])
    @pl.when(owner)
    def _():
        load_probe.start()
        load_pat.start()

    load_strip.start()
    load_tab.start()

    barrier = pltpu.get_barrier_semaphore()

    def greet(tile, mode):
        pl.semaphore_signal(barrier, inc=1, device_id=(tile, mode), device_id_type=MESH)

    for k in range(1, 16):
        greet(t, (j + k) % 16)
    greet(partner, j)
    has_up, has_down = t < 7, t > 0
    to_next_x = (c == 1) & has_up
    to_prev_x = (c == 0) & has_down

    @pl.when(to_next_x)
    def _():
        greet(up_tile, j)

    @pl.when(to_prev_x)
    def _():
        greet(down_tile, j)
        for k in range(8):
            for core in range(2):
                greet(2 * x - 2 + core, 8 + k)

    for k in range(8):
        greet(partner, 8 * c + k)

    lane = lax.broadcasted_iota(jnp.int32, (8, HALF), 1)
    live = (lax.broadcasted_iota(jnp.int32, (8, HALF), 0) < counts_ref[0]).astype(jnp.int32)
    place = jnp.where(lane == 2, live, 0)
    line = lax.broadcasted_iota(jnp.int32, (8, HALF), 0)
    for i in range(8):
        for p in range(2):
            place = jnp.where((line == i) & (lane == p), offs_ref[p, i], place)
    info[0] = place

    @pl.when(jnp.logical_not(has_down))
    def _():
        info[2] = jnp.zeros((8, HALF), jnp.int32)


    @pl.when(owner)
    def _():
        load_probe.wait()
        rows = lax.broadcasted_iota(jnp.int32, (PATCH, PATCH), 0)
        cols = lax.broadcasted_iota(jnp.int32, (PATCH, PATCH), 1)
        sort_r = jnp.where(cols == natural(rows), 1.0, 0.0).astype(BF16)
        sort_c = jnp.where(rows == natural(cols), 1.0, 0.0).astype(BF16)
        for ri in range(2):
            plane = mm(sort_r, probe[ri].astype(BF16)).astype(BF16)
            plane = mm(plane, sort_c).astype(BF16)
            for s in range(2):
                modes[0, s, ri * HALF:(ri + 1) * HALF, :] = plane[s * HALF:(s + 1) * HALF]

    sends_strip = jnp.logical_not(owner) & has_down

    @pl.when(sends_strip)
    def _():
        load_strip.wait()
        strip_b[...] = strip[...].astype(BF16)

    @pl.when(jnp.logical_not(owner | has_down))
    def _():
        load_strip.wait()

    far_slabs = (group == 1) & (x < 3)
    across = to_next_x | to_prev_x
    pl.semaphore_wait(
        barrier, 16 + jnp.where(across, 1, 0) + jnp.where(owner, 0, 16) + jnp.where(far_slabs, 16, 0)
    )

    def to(src, dst, send, recv, tile, mode):
        return pltpu.make_async_remote_copy(
            src_ref=src, dst_ref=dst, send_sem=send, recv_sem=recv,
            device_id=(tile, mode), device_id_type=MESH,
        )

    info_pair = to(info.at[0], info.at[1], info_sem.at[0], info_sem.at[1], partner, j)
    info_next = to(info.at[0], info.at[2], info_sem.at[2], info_sem.at[3], up_tile, j)
    info_pair.start()

    @pl.when(to_next_x)
    def _():
        info_next.start()

    def block(m, s, h):
        return modes.at[m, s, pl.ds(h * HALF, HALF), :]

    def mode_slot(row, home, dy):
        d = (row - 2 * c + 4) % 4
        nearer = 2 * c + jnp.where((d == 1) | (d == 2), 1, 0)
        return jnp.where(home == nearer, ORDER.index((0, dy)), ORDER.index((1, dy)))

    def relay(k, s, h, home, dy, step_z, step_y):
        row = (z + step_z + 4) % 4
        there = mode_slot(row, home, (dy + step_y) % 4)
        to(
            block(k, s, h), block(there, s, h), gather_send, gather_recv.at[there, s, h],
            t, row * 4 + (y + step_y + 4) % 4,
        ).start()

    def take(k):
        which, dy = ORDER[k]
        d = (z - 2 * c + 4) % 4
        nearer = jnp.where((d == 1) | (d == 2), 1, 0)
        home = 2 * c + (nearer if which == 0 else 1 - nearer)
        dz = (z - home + 4) % 4
        for h in range(2):
            for s in range(2):
                to(
                    block(k, s, h), block(k, s, h), gather_send, gather_recv.at[k, s, h], t, j
                ).wait_recv()
                if s == 0 and dy == 0:
                    @pl.when(dz == 0)
                    def _():
                        for step in (2, 1, -1):
                            relay(k, s, h, home, dy, 0, step)

                if s == 1 and dy == 0:
                    @pl.when(dz == 2)
                    def _():
                        relay(k, s, h, home, dy, 0, 2)

                    for step in (1, -1):
                        relay(k, s, h, home, dy, 0, step)
                if s == 1 and (dy, h) in ((1, 0), (3, 1)):
                    @pl.when(dz != 2)
                    def _():
                        relay(k, s, h, home, dy, 0, 2 - dy)

                if s == 0 or dy == 0:
                    @pl.when(dz == 0)
                    def _():
                        if s == 1 or dy == 2:
                            relay(k, s, h, home, dy, 2, 0)
                        relay(k, s, h, home, dy, 1, 0)
                        relay(k, s, h, home, dy, -1, 0)

                if s == 0 and dy != 2:
                    @pl.when(dz == (1 if h == 0 else 3))
                    def _():
                        relay(k, s, h, home, dy, 1 if h == 0 else -1, 0)

    send_strip = to(
        strip_b, ext.at[:, pl.ds(PATCH, PATCH), :], strip_sem.at[0], strip_sem.at[1], down_tile, j
    )
    pat_pair = to(pat_hbm.at[slot], pat, pat_sem.at[0], pat_sem.at[1], partner, j)

    @pl.when(owner)
    def _():
        for h in range(2):
            for step in (2, 1, -1):
                relay(0, 0, h, z, 0, 0, step)
                relay(0, 1, h, z, 0, step, 0)
        for h in range(2):
            for step in (1, -1):
                relay(0, 0, h, z, 0, step, 0)
                relay(0, 1, h, z, 0, 0, step)

    @pl.when(sends_strip)
    def _():
        send_strip.start()

    @pl.when(t == 7)
    def _():
        ext[:, PATCH:2 * PATCH, :] = jnp.zeros((2, PATCH, 2 * PATCH), BF16)

    @pl.when(owner)
    def _():
        pat_pair.start()
        load_strip.wait()
        high = strip[...].astype(BF16)
        ext[:, 0:PATCH, :] = high
        strip_b[...] = (strip[...] - high.astype(F32)).astype(BF16)

    @pl.when(jnp.logical_not(owner))
    def _():
        take(0)

    for k in range(1, 4):
        take(k)

    load_tab.wait()
    info_pair.wait_recv()

    @pl.when(owner)
    def _():
        info[3] = info[0]

    @pl.when(jnp.logical_not(owner))
    def _():
        info[3] = info[1]

    row = info[3, pl.ds(slot, 1), :]
    first_row, first_col, alive = row[:, 0:1], row[:, 1:2], row[:, 2:3]
    rows = lax.broadcasted_iota(jnp.int32, (PATCH, PATCH), 0)
    cols = lax.broadcasted_iota(jnp.int32, (PATCH, PATCH), 1)

    def wrapped(at):
        return jnp.where(at >= PATCH, at - PATCH, at)

    place_r[...] = jnp.where((rows == wrapped(first_row + natural(cols))) & (alive > 0), 1.0, 0.0).astype(BF16)
    place_c[...] = jnp.where(cols == wrapped(first_col + natural(rows)), 1.0, 0.0).astype(BF16)

    for k in range(4, 7):
        take(k)

    send_patch = to(init, init, patch_sem.at[0], patch_sem.at[1], partner, j)

    @pl.when(owner)
    def _():
        @pl.when(has_up)
        def _():
            send_strip.wait_recv()

        inside = jnp.where(t == 7, PATCH, 2 * PATCH)
        rows = lax.broadcasted_iota(jnp.int32, (PATCH, 2 * PATCH), 0)
        cols = lax.broadcasted_iota(jnp.int32, (PATCH, 2 * PATCH), 1)
        cut_r = jnp.where((cols == first_row + natural(rows)) & (cols < inside), 1.0, 0.0).astype(BF16)
        rows2 = lax.broadcasted_iota(jnp.int32, (2 * PATCH, PATCH), 0)
        cols2 = lax.broadcasted_iota(jnp.int32, (2 * PATCH, PATCH), 1)
        cut_c = jnp.where(rows2 == first_col + natural(cols2), 1.0, 0.0).astype(BF16)
        for ri in range(2):
            high = mm(cut_r, ext[ri]).astype(BF16)
            low = mm(cut_r[:, 0:PATCH], strip_b[ri]).astype(BF16)
            piece = mm(high, cut_c) + mm(low, cut_c)
            for s in range(2):
                init[s, ri * HALF:(ri + 1) * HALF, :] = piece[s * HALF:(s + 1) * HALF]
        send_patch.start()

    @pl.when(owner)
    def _():
        load_pat.wait()
        pat_pair.wait_send()
        send_patch.wait_send()

    @pl.when(jnp.logical_not(owner))
    def _():
        pat_pair.wait_recv()
        send_patch.wait_recv()

    @pl.when(sends_strip)
    def _():
        send_strip.wait_send()

    def far_rows(m, b):
        return pl.ds((2 * m + b) * PATCH, PATCH)

    def exit_and_left(m, field, with_power):
        ends = []
        for s in range(2):
            pr = modes[m, s, 0:HALF, :].astype(F32)
            pi = modes[m, s, HALF:PATCH, :].astype(F32)
            cr = field[s, 0:HALF, :]
            ci = field[s, HALF:PATCH, :]
            wave = jnp.concatenate(
                [(pr * cr - pi * ci).astype(BF16), (pr * ci + pi * cr).astype(BF16)], axis=0
            )
            if with_power:
                power[s] += pr * pr + pi * pi
            ends.append(mm(tab[0, s], wave))
        for b, part in enumerate((ends[0] + ends[1], ends[0] - ends[1])):
            part = part.astype(BF16)
            for s in range(2):
                for ri in range(2):
                    half[m, s, b * HALF:(b + 1) * HALF, ri * HALF:(ri + 1) * HALF] = part[
                        ri * HALF:(ri + 1) * HALF, s * HALF:(s + 1) * HALF
                    ]

    def right_and_power(first):
        sums = [0.0, 0.0]
        for m in (first, first + 1):
            even = mm(half[m, 0], tab[1, 0])
            odd = mm(half[m, 1], tab[1, 1])
            for b, part in enumerate((even + odd, even - odd)):
                far[far_rows(m, b), :] = part
                re, im = part[:, 0:HALF], part[:, HALF:PATCH]
                sums[b] += re * re + im * im
        for b in range(2):
            inten[b] = sums[b] if first == 0 else inten[b] + sums[b]

    def change_and_right(m):
        ra, rb = ratio[0], ratio[1]
        ya = far[far_rows(m, 0), :] * jnp.concatenate([ra, ra], axis=1)
        yb = far[far_rows(m, 1), :] * jnp.concatenate([rb, rb], axis=1)
        for s, part in enumerate(((ya + yb).astype(BF16), (ya - yb).astype(BF16))):
            near = mm(part, tab[0, s])
            lo, hi = near[0:HALF], near[HALF:PATCH]
            for b, mixed in enumerate((lo + hi, lo - hi)):
                mixed = mixed.astype(BF16)
                for ri in range(2):
                    half[m, b, ri * HALF:(ri + 1) * HALF, s * HALF:(s + 1) * HALF] = mixed[
                        :, ri * HALF:(ri + 1) * HALF
                    ]

    def left_and_update(first):
        for s in range(2):
            re = im = 0.0
            for m in (first, first + 1):
                near = mm(tab[1, s], half[m, s])
                nr, ni = near[0:HALF], near[HALF:PATCH]
                pr = modes[m, s, 0:HALF, :].astype(F32)
                pi = modes[m, s, HALF:PATCH, :].astype(F32)
                re += pr * nr + pi * ni
                im += pr * ni - pi * nr
            if first == 0:
                upd[s, 0:HALF, :] = re
                upd[s, HALF:PATCH, :] = im
            else:
                upd[s, 0:HALF, :] += re
                upd[s, HALF:PATCH, :] += im

    def swap(src, dst, which):
        copy = to(src, dst, pair_send.at[which], pair_recv.at[which], partner, j)
        copy.start()
        return copy

    power[...] = jnp.zeros_like(power)
    for repeat in range(PASSES):
        last = repeat == PASSES - 1
        if repeat == 0:
            for k in range(7):
                exit_and_left(k, init, True)
            take(7)
            exit_and_left(7, init, True)
        else:
            for k in range(8):
                exit_and_left(k, cur, False)
        for k in range(0, 8, 2):
            right_and_power(k)
        inten_b[repeat] = inten[...].astype(BF16)
        copy = swap(inten_b.at[repeat], inten_in.at[repeat], 3 * repeat)
        if repeat == 0:
            power_b[...] = power[...].astype(BF16)
            power_copy = swap(power_b, power_in, 1)
        copy.wait()
        for b in range(2):
            total = inten[b] + inten_in[repeat, b].astype(F32)
            measured = pat[:, b * HALF:(b + 1) * HALF].astype(F32)
            ratio[b] = jnp.sqrt(measured / jnp.maximum(total, 1.0)) - 1.0

        for k in range(8):
            change_and_right(k)
        for k in range(0, 8, 2):
            left_and_update(k)
        if repeat == 0:
            power_copy.wait()
            whole = power[...] + power_in[...].astype(F32)
            whole = jnp.maximum(whole[0], whole[1])
            highest = jnp.max(jnp.max(whole, axis=0, keepdims=True), axis=1, keepdims=True)
            scale = STEP_SIZE / highest
        if not last:
            upd_b[...] = upd[...].astype(BF16)
            copy = swap(upd_b, upd_in, 2)
            copy.wait()
            for s in range(2):
                cur[s] = init[s] + scale * (upd[s] + upd_in[s].astype(F32))
        else:
            mine = pl.ds(pl.multiple_of(c * HALF, HALF), HALF)
            other = pl.ds(pl.multiple_of((1 - c) * HALF, HALF), HALF)
            last_b[...] = upd[:, other, :].astype(BF16)
            copy = swap(last_b, last_in, 4)
            copy.wait()
            moved = []
            for s in range(2):
                change = cur[s, mine, :] - init[s, mine, :]
                change += scale * (upd[s, mine, :] + last_in[s].astype(F32))
                moved.append(change.astype(BF16))
            moved = jnp.concatenate(moved, axis=0)

    placed = mm(place_r[...], moved).astype(BF16)
    canvas[...] = mm(placed, place_c[...]).astype(BF16)

    for dz, dy in FAR_FIRST:
        mode = ((z + dz) % 4) * 4 + (y + dy) % 4
        src = canvas.at[pl.ds(pl.multiple_of(mode * SLAB, SLAB), SLAB), :]
        dst = slabs.at[c * 8 + slot]

        @pl.when(far_slabs)
        def _():
            to(src, slabs.at[16 + c * 8 + slot], slab_send, slab_recv.at[1], s_tile + 1, mode).start()

        if (dz, dy) == (0, 0):
            @pl.when(owner)
            def _():
                pltpu.make_async_copy(src, dst, slab_recv.at[0]).start()

            @pl.when(jnp.logical_not(owner))
            def _():
                to(src, dst, slab_send, slab_recv.at[0], s_tile, mode).start()
        else:
            to(src, dst, slab_send, slab_recv.at[0], s_tile, mode).start()

    @pl.when(to_prev_x)
    def _():
        info_next.wait_recv()

    @pl.when(c == 0)
    def _():
        info[4] = info[2]

    @pl.when(c == 1)
    def _():
        info[4] = info[1]

    at_row = lax.broadcasted_iota(jnp.int32, (SLAB, 2 * PATCH), 0) + j * SLAB
    at_col = lax.broadcasted_iota(jnp.int32, (SLAB, 2 * PATCH), 1)
    from_above = jnp.where(t > 0, 1.0, 0.0)
    cover = jnp.zeros((SLAB, 2 * PATCH), F32)
    for k in range(2):
        here = info[4 * k]
        part = jnp.zeros((SLAB, 2 * PATCH), F32)
        for i in range(8):
            dr = at_row + k * PATCH - here[i:i + 1, 0:1]
            dc = at_col - here[i:i + 1, 1:2]
            inside = (dr >= 0) & (dr < PATCH) & (dc >= 0) & (dc < PATCH) & (here[i:i + 1, 2:3] > 0)
            part += jnp.where(inside, 1.0, 0.0)
        cover += part if k == 0 else part * from_above
    share = 1.0 / jnp.maximum(cover, 1.0)

    at_row = lax.broadcasted_iota(jnp.int32, (SLAB, PATCH), 0) + j * SLAB
    at_col = lax.broadcasted_iota(jnp.int32, (SLAB, PATCH), 1)

    def gathered(which, table, ri):
        parts = [jnp.zeros((SLAB, PATCH), F32) for _ in range(4)]
        for i in range(8):
            value = slabs[which * 16 + ri * 8 + i].astype(F32)
            in_strip = at_row >= info[table, i:i + 1, 0:1]
            in_left = at_col >= info[table, i:i + 1, 1:2]
            left = jnp.where(in_left, value, 0.0)
            right = value - left
            left_own = jnp.where(in_strip, left, 0.0)
            right_own = jnp.where(in_strip, right, 0.0)
            for p, term in enumerate((left_own, right_own, left - left_own, right - right_own)):
                parts[p] += term
        return jnp.concatenate(parts[0:2], axis=1), jnp.concatenate(parts[2:4], axis=1)

    first16 = slabs.at[pl.ds(0, 16)]
    pltpu.make_async_copy(first16, first16, slab_recv.at[0]).wait()
    spill_copy = to(spill, spill_in, spill_sem.at[0], spill_sem.at[1], partner, j)
    sums = [gathered(0, 0, ri) for ri in range(2)]
    for ri in range(2):
        own[ri] = sums[ri][0]

    @pl.when(c == 0)
    def _():
        for ri in range(2):
            spill[ri] = sums[ri][1].astype(BF16)
        spill_copy.start()

    @pl.when(to_prev_x)
    def _():
        pltpu.make_async_copy(first16, first16, slab_recv.at[1]).wait()
        for ri in range(2):
            own[ri] += gathered(1, 2, ri)[1]

    @pl.when(c == 1)
    def _():
        spill_copy.wait_recv()
        for ri in range(2):
            own[ri] += spill_in[ri].astype(F32)

    my_rows = out_ref.at[:, pl.ds(pl.multiple_of(j * SLAB, SLAB), SLAB), :]
    for ri in range(2):
        quot[ri] = (own[ri] * share).astype(BF16)
    for dz, dy in FAR_FIRST[:15]:
        to(quot, my_rows, quot_send, quot_recv, t, ((z + dz) % 4) * 4 + (y + dy) % 4).start()
    keep = pltpu.make_async_copy(quot, my_rows, local_sem.at[4])
    keep.start()

    info_pair.wait_send()

    @pl.when(to_next_x)
    def _():
        info_next.wait_send()

    @pl.when(c == 0)
    def _():
        spill_copy.wait_send()

    for here, count in ((owner, 45), (jnp.logical_not(owner), 15)):
        @pl.when(here)
        def _():
            rows = far.at[pl.ds(0, count * 64), :]
            pltpu.make_async_copy(rows, rows, gather_send).wait()

    for is_owner in (0, 1):
        for is_far in (0, 1):
            @pl.when((owner == (is_owner == 1)) & (far_slabs == (is_far == 1)))
            def _():
                rows = slabs.at[pl.ds(0, 16 - is_owner + 16 * is_far)]
                pltpu.make_async_copy(rows, rows, slab_send).wait()

    rows = strip.at[0, pl.ds(0, 15 * SLAB), :]
    pltpu.make_async_copy(rows, rows, quot_send).wait()
    pltpu.make_async_copy(rows, rows, quot_recv).wait()
    keep.wait()


def shards(object_field, probe_modes, patterns, offsets, counts):
    tables = jnp.asarray(make_tables())
    in_hbm = pl.BlockSpec(memory_space=pltpu.HBM)
    vmem = pltpu.VMEM
    dma = pltpu.SemaphoreType.DMA
    change = pl.pallas_call(
        kernel,
        out_shape=vmem((2, PATCH, 2 * PATCH), BF16),
        in_specs=[
            in_hbm, in_hbm, in_hbm, in_hbm,
            pl.BlockSpec(memory_space=pltpu.SMEM),
            pl.BlockSpec(memory_space=pltpu.SMEM),
        ],
        out_specs=pl.BlockSpec(memory_space=vmem),
        scratch_shapes=[
            vmem((2, PATCH, PATCH), F32),
            vmem((2, PATCH, 2 * PATCH), F32),
            vmem((2, PATCH, 2 * PATCH), BF16),
            vmem((2, 2 * PATCH, 2 * PATCH), BF16),
            vmem((PATCH, PATCH), BF16),
            vmem((2, 2, PATCH, PATCH), BF16),
            vmem((5, 8, HALF), jnp.int32),
            vmem((8, 2, PATCH, PATCH), BF16),
            vmem((8, 2, PATCH, PATCH), BF16),
            vmem((16 * PATCH, PATCH), F32),
            vmem((2, PATCH, PATCH), F32),
            vmem((2, PATCH, PATCH), F32),
            vmem((2, PATCH, HALF), F32),
            vmem((2, PATCH, HALF), F32),
            vmem((2, PATCH, PATCH), F32),
            vmem((2, HALF, PATCH), F32),
            vmem((PASSES, 2, PATCH, HALF), BF16),
            vmem((2, PATCH, PATCH), BF16),
            vmem((2, HALF, PATCH), BF16),
            vmem((2, HALF, PATCH), BF16),
            vmem((PASSES, 2, PATCH, HALF), BF16),
            vmem((2, PATCH, PATCH), BF16),
            vmem((2, HALF, PATCH), BF16),
            vmem((2, HALF, PATCH), BF16),
            vmem((PATCH, PATCH), BF16),
            vmem((PATCH, PATCH), BF16),
            vmem((PATCH, PATCH), BF16),
            vmem((32, SLAB, PATCH), BF16),
            vmem((2, SLAB, 2 * PATCH), BF16),
            vmem((2, SLAB, 2 * PATCH), BF16),
            vmem((2, SLAB, 2 * PATCH), F32),
            vmem((2, SLAB, 2 * PATCH), BF16),
            dma((5,)), dma, dma((8, 2, 2)), dma((2,)), dma((4,)), dma((2,)), dma((2,)),
            dma((5,)), dma((5,)), dma, dma((2,)), dma((2,)), dma, dma,
        ],
        compiler_params=pltpu.CompilerParams(
            collective_id=0, has_side_effects=True, vmem_limit_bytes=56 * 1024 * 1024
        ),
        cost_estimate=pl.CostEstimate(flops=6 * 10**9, bytes_accessed=8 * 2**20, transcendentals=131072),
    )(object_field, probe_modes, patterns, tables, offsets.T, counts)
    return object_field + change.astype(F32)


def solution(mesh):
    return jax.shard_map(
        shards,
        mesh=mesh,
        in_specs=(
            P(None, "tile", None),
            P("mode", None, None, None),
            P("tile", None, None),
            P("tile", None),
            P("tile"),
        ),
        out_specs=P(None, "tile", None),
        check_vma=False,
    )
```

```python
import math

import numpy as np
import ml_dtypes
import jax
import jax.numpy as jnp
from jax import lax
from jax.experimental import pallas as pl
from jax.experimental.pallas import tpu as pltpu
from jax.sharding import PartitionSpec as P

PATCH = 256
HALF = 128
QUARTER = 64
PASSES = 2
STEP_SIZE = 0.9
SLAB = 16
MESH = pl.DeviceIdType.MESH
BF16 = jnp.bfloat16
F32 = jnp.float32

ORDER = ((0, 0), (1, 0), (0, 1), (0, 3), (0, 2), (1, 1), (1, 3), (1, 2))
FAR_FIRST = sorted(
    ((dz, dy) for dz in range(4) for dy in range(4)), key=lambda d: -min(d[0], 4 - d[0]) - min(d[1], 4 - d[1])
)


def make_tables():
    q = np.arange(HALF)
    tables = []
    for s in range(2):
        a = 2 * np.arange(HALF) + s
        angle = (q[:, None] * a[None, :] % PATCH).astype(np.float32) * np.float32(2.0 * math.pi / PATCH)
        factor = np.float32(1.0 / math.sqrt(PATCH))
        real = (np.cos(angle) * factor).astype(ml_dtypes.bfloat16)
        imag = (-np.sin(angle) * factor).astype(ml_dtypes.bfloat16)
        tables.append(np.block([[real, -imag], [imag, real]]))
    tables = np.stack(tables)
    return np.stack([tables, tables.transpose(0, 2, 1)])


def mm(a, b):
    return jnp.dot(a, b, preferred_element_type=F32)


def natural(position):
    return jnp.where(position < HALF, 2 * position, 2 * position - (PATCH - 1))


def kernel(
    obj_hbm, probe_hbm, pat_hbm, tab_hbm, offs_ref, counts_ref, out_ref,
    probe, strip, strip_b, ext, pat, tab, info, modes, half, far, init, cur,
    inten, ratio, upd, power, inten_b, upd_b, last_b, power_b, inten_in, upd_in, last_in, power_in,
    place_r, place_c, canvas, slabs, spill, spill_in, own, quot,
    local_sem, gather_send, gather_recv, strip_sem, info_sem, patch_sem, pat_sem,
    pair_send, pair_recv, slab_send, slab_recv, spill_sem, quot_send, quot_recv,
):
    t = lax.axis_index("tile")
    j = lax.axis_index("mode")
    x, z = t // 2, j // 4
    c, y = t - 2 * x, j - 4 * z
    group = z // 2
    owner = c == group
    s_tile = 2 * x + group
    slot = j - 8 * group
    partner = 2 * x + (1 - c)
    up_tile, down_tile = t + 1, t - 1

    load_probe = pltpu.make_async_copy(probe_hbm.at[0], probe, local_sem.at[0])
    load_strip = pltpu.make_async_copy(obj_hbm, strip, local_sem.at[1])
    load_tab = pltpu.make_async_copy(tab_hbm, tab, local_sem.at[2])
    load_pat = pltpu.make_async_copy(pat_hbm.at[slot], pat, local_sem.at[3])
    @pl.when(owner)
    def _():
        load_probe.start()
        load_pat.start()

    load_strip.start()
    load_tab.start()

    barrier = pltpu.get_barrier_semaphore()

    def greet(tile, mode):
        pl.semaphore_signal(barrier, inc=1, device_id=(tile, mode), device_id_type=MESH)

    for k in range(1, 16):
        greet(t, (j + k) % 16)
    greet(partner, j)
    has_up, has_down = t < 7, t > 0
    to_next_x = (c == 1) & has_up
    to_prev_x = (c == 0) & has_down

    @pl.when(to_next_x)
    def _():
        greet(up_tile, j)

    @pl.when(to_prev_x)
    def _():
        greet(down_tile, j)

    for k in range(8):
        greet(partner, 8 * c + k)

    lane = lax.broadcasted_iota(jnp.int32, (8, HALF), 1)
    live = (lax.broadcasted_iota(jnp.int32, (8, HALF), 0) < counts_ref[0]).astype(jnp.int32)
    place = jnp.where(lane == 2, live, 0)
    line = lax.broadcasted_iota(jnp.int32, (8, HALF), 0)
    for i in range(8):
        for p in range(2):
            place = jnp.where((line == i) & (lane == p), offs_ref[p, i], place)
    info[0] = place

    @pl.when(jnp.logical_not(has_down))
    def _():
        info[2] = jnp.zeros((8, HALF), jnp.int32)


    @pl.when(owner)
    def _():
        load_probe.wait()
        rows = lax.broadcasted_iota(jnp.int32, (PATCH, PATCH), 0)
        cols = lax.broadcasted_iota(jnp.int32, (PATCH, PATCH), 1)
        sort_r = jnp.where(cols == natural(rows), 1.0, 0.0).astype(BF16)
        sort_c = jnp.where(rows == natural(cols), 1.0, 0.0).astype(BF16)
        for ri in range(2):
            plane = mm(sort_r, probe[ri].astype(BF16)).astype(BF16)
            plane = mm(plane, sort_c).astype(BF16)
            for s in range(2):
                modes[0, s, ri * HALF:(ri + 1) * HALF, :] = plane[s * HALF:(s + 1) * HALF]

    sends_strip = jnp.logical_not(owner) & has_down

    @pl.when(sends_strip)
    def _():
        load_strip.wait()
        strip_b[...] = strip[...].astype(BF16)

    @pl.when(jnp.logical_not(owner | has_down))
    def _():
        load_strip.wait()

    across = to_next_x | to_prev_x
    pl.semaphore_wait(
        barrier, 16 + jnp.where(across, 1, 0) + jnp.where(owner, 0, 16)
    )

    def to(src, dst, send, recv, tile, mode):
        return pltpu.make_async_remote_copy(
            src_ref=src, dst_ref=dst, send_sem=send, recv_sem=recv,
            device_id=(tile, mode), device_id_type=MESH,
        )

    info_pair = to(info.at[0], info.at[1], info_sem.at[0], info_sem.at[1], partner, j)
    info_next = to(info.at[0], info.at[2], info_sem.at[2], info_sem.at[3], up_tile, j)
    info_pair.start()

    @pl.when(to_next_x)
    def _():
        info_next.start()

    def block(m, s, h):
        return modes.at[m, s, pl.ds(h * HALF, HALF), :]

    def mode_slot(row, home, dy):
        d = (row - 2 * c + 4) % 4
        nearer = 2 * c + jnp.where((d == 1) | (d == 2), 1, 0)
        return jnp.where(home == nearer, ORDER.index((0, dy)), ORDER.index((1, dy)))

    def relay(k, s, h, home, dy, step_z, step_y):
        row = (z + step_z + 4) % 4
        there = mode_slot(row, home, (dy + step_y) % 4)
        to(
            block(k, s, h), block(there, s, h), gather_send, gather_recv.at[there, s, h],
            t, row * 4 + (y + step_y + 4) % 4,
        ).start()

    def take(k):
        which, dy = ORDER[k]
        d = (z - 2 * c + 4) % 4
        nearer = jnp.where((d == 1) | (d == 2), 1, 0)
        home = 2 * c + (nearer if which == 0 else 1 - nearer)
        dz = (z - home + 4) % 4
        for h in range(2):
            for s in range(2):
                to(
                    block(k, s, h), block(k, s, h), gather_send, gather_recv.at[k, s, h], t, j
                ).wait_recv()
                if s == 0 and dy == 0:
                    @pl.when(dz == 0)
                    def _():
                        for step in (2, 1, -1):
                            relay(k, s, h, home, dy, 0, step)

                if s == 1 and dy == 0:
                    @pl.when(dz == 2)
                    def _():
                        relay(k, s, h, home, dy, 0, 2)

                    for step in (1, -1):
                        relay(k, s, h, home, dy, 0, step)
                if s == 1 and (dy, h) in ((1, 0), (3, 1)):
                    @pl.when(dz != 2)
                    def _():
                        relay(k, s, h, home, dy, 0, 2 - dy)

                if s == 0 or dy == 0:
                    @pl.when(dz == 0)
                    def _():
                        if s == 1 or dy == 2:
                            relay(k, s, h, home, dy, 2, 0)
                        relay(k, s, h, home, dy, 1, 0)
                        relay(k, s, h, home, dy, -1, 0)

                if s == 0 and dy != 2:
                    @pl.when(dz == (1 if h == 0 else 3))
                    def _():
                        relay(k, s, h, home, dy, 1 if h == 0 else -1, 0)

    send_strip = to(
        strip_b, ext.at[:, pl.ds(PATCH, PATCH), :], strip_sem.at[0], strip_sem.at[1], down_tile, j
    )
    pat_pair = to(pat_hbm.at[slot], pat, pat_sem.at[0], pat_sem.at[1], partner, j)

    @pl.when(owner)
    def _():
        for h in range(2):
            for step in (2, 1, -1):
                relay(0, 0, h, z, 0, 0, step)
                relay(0, 1, h, z, 0, step, 0)
        for h in range(2):
            for step in (1, -1):
                relay(0, 0, h, z, 0, step, 0)
                relay(0, 1, h, z, 0, 0, step)

    @pl.when(sends_strip)
    def _():
        send_strip.start()

    @pl.when(t == 7)
    def _():
        ext[:, PATCH:2 * PATCH, :] = jnp.zeros((2, PATCH, 2 * PATCH), BF16)

    @pl.when(owner)
    def _():
        pat_pair.start()
        load_strip.wait()
        high = strip[...].astype(BF16)
        ext[:, 0:PATCH, :] = high
        strip_b[...] = (strip[...] - high.astype(F32)).astype(BF16)

    @pl.when(jnp.logical_not(owner))
    def _():
        take(0)

    for k in range(1, 4):
        take(k)

    load_tab.wait()
    info_pair.wait_recv()

    @pl.when(owner)
    def _():
        info[3] = info[0]

    @pl.when(jnp.logical_not(owner))
    def _():
        info[3] = info[1]

    row = info[3, pl.ds(slot, 1), :]
    first_row, first_col, alive = row[:, 0:1], row[:, 1:2], row[:, 2:3]
    rows = lax.broadcasted_iota(jnp.int32, (PATCH, PATCH), 0)
    cols = lax.broadcasted_iota(jnp.int32, (PATCH, PATCH), 1)

    def wrapped(at):
        return jnp.where(at >= PATCH, at - PATCH, at)

    place_r[...] = jnp.where((rows == wrapped(first_row + natural(cols))) & (alive > 0), 1.0, 0.0).astype(BF16)
    place_c[...] = jnp.where(cols == wrapped(first_col + natural(rows)), 1.0, 0.0).astype(BF16)

    for k in range(4, 7):
        take(k)

    send_patch = to(init, init, patch_sem.at[0], patch_sem.at[1], partner, j)

    @pl.when(owner)
    def _():
        @pl.when(has_up)
        def _():
            send_strip.wait_recv()

        inside = jnp.where(t == 7, PATCH, 2 * PATCH)
        rows = lax.broadcasted_iota(jnp.int32, (PATCH, 2 * PATCH), 0)
        cols = lax.broadcasted_iota(jnp.int32, (PATCH, 2 * PATCH), 1)
        cut_r = jnp.where((cols == first_row + natural(rows)) & (cols < inside), 1.0, 0.0).astype(BF16)
        rows2 = lax.broadcasted_iota(jnp.int32, (2 * PATCH, PATCH), 0)
        cols2 = lax.broadcasted_iota(jnp.int32, (2 * PATCH, PATCH), 1)
        cut_c = jnp.where(rows2 == first_col + natural(cols2), 1.0, 0.0).astype(BF16)
        for ri in range(2):
            high = mm(cut_r, ext[ri]).astype(BF16)
            low = mm(cut_r[:, 0:PATCH], strip_b[ri]).astype(BF16)
            piece = mm(high, cut_c) + mm(low, cut_c)
            for s in range(2):
                init[s, ri * HALF:(ri + 1) * HALF, :] = piece[s * HALF:(s + 1) * HALF]
        send_patch.start()

    @pl.when(owner)
    def _():
        load_pat.wait()
        pat_pair.wait_send()
        send_patch.wait_send()

    @pl.when(jnp.logical_not(owner))
    def _():
        pat_pair.wait_recv()
        send_patch.wait_recv()

    @pl.when(sends_strip)
    def _():
        send_strip.wait_send()


    def far_rows(m, b, r):
        return pl.ds(((2 * m + b) * 2 + r) * HALF, HALF)

    def columns(s):
        return slice(s * HALF, (s + 1) * HALF)

    def beside(parts):
        return jnp.concatenate(parts, axis=1)

    def stacked(parts):
        return jnp.concatenate(parts, axis=0)

    def exit_and_left(m):
        ends = []
        for s in range(2):
            pr = modes[m, s, 0:HALF, :].astype(F32)
            pi = modes[m, s, HALF:PATCH, :].astype(F32)
            cr = init[s, 0:HALF, :]
            ci = init[s, HALF:PATCH, :]
            wave = stacked([(pr * cr - pi * ci).astype(BF16), (pr * ci + pi * cr).astype(BF16)])
            if m == 0:
                power[s] = pr * pr + pi * pi
            else:
                power[s] += pr * pr + pi * pi
            ends.append(mm(tab[0, s], wave))
        for b, part in enumerate((ends[0] + ends[1], ends[0] - ends[1])):
            part = part.astype(BF16)
            for s in range(2):
                for ri in range(2):
                    half[m, s, b * HALF:(b + 1) * HALF, columns(ri)] = part[
                        ri * HALF:(ri + 1) * HALF, columns(s)
                    ]

    def pair_probe(first, s, c2):
        return [
            beside([modes[m, s, columns(ri), columns(c2)] for m in (first, first + 1)]).astype(F32)
            for ri in range(2)
        ]

    def exit_and_left_half(c2):
        for first in range(0, 8, 2):
            ends = []
            for s in range(2):
                pr, pi = pair_probe(first, s, c2)
                cr = beside([cur[c2, s, 0:HALF, :]] * 2)
                ci = beside([cur[c2, s, HALF:PATCH, :]] * 2)
                wave = stacked([(pr * cr - pi * ci).astype(BF16), (pr * ci + pi * cr).astype(BF16)])
                ends.append(mm(tab[0, s], wave))
            for b, part in enumerate((ends[0] + ends[1], ends[0] - ends[1])):
                part = part.astype(BF16)
                for i in range(2):
                    for ri in range(2):
                        half[first + i, c2, b * HALF:(b + 1) * HALF, columns(ri)] = part[
                            ri * HALF:(ri + 1) * HALF, columns(i)
                        ]

    def row_parts(r):
        return slice(r * QUARTER, (r + 1) * QUARTER), slice(HALF + r * QUARTER, HALF + (r + 1) * QUARTER)

    def right_and_power_half(r):
        low, high = row_parts(r)
        sums = [None, None]
        for first in range(0, 8, 2):
            ends = [
                mm(stacked([half[m, s, rows, :] for m in (first, first + 1) for rows in (low, high)]), tab[1, s])
                for s in range(2)
            ]
            for b, part in enumerate((ends[0] + ends[1], ends[0] - ends[1])):
                for i in range(2):
                    mine = part[i * HALF:(i + 1) * HALF]
                    far[far_rows(first + i, b, r), :] = mine
                    re, im = mine[:, 0:HALF], mine[:, HALF:PATCH]
                    term = re * re + im * im
                    sums[b] = term if sums[b] is None else sums[b] + term
        for b in range(2):
            inten[r, b] = sums[b]

    def set_ratio(repeat, r):
        low, high = row_parts(r)
        for b in range(2):
            total = inten[r, b] + inten_in[repeat, r, b].astype(F32)
            measured = stacked([pat[low, columns(b)], pat[high, columns(b)]]).astype(F32)
            ratio[r, b] = jnp.sqrt(measured / jnp.maximum(total, 1.0)) - 1.0

    def change_and_right_half(r):
        low, high = row_parts(r)
        for first in range(0, 8, 2):
            plus, minus = [], []
            for m in (first, first + 1):
                ya = far[far_rows(m, 0, r), :] * beside([ratio[r, 0]] * 2)
                yb = far[far_rows(m, 1, r), :] * beside([ratio[r, 1]] * 2)
                plus.append((ya + yb).astype(BF16))
                minus.append((ya - yb).astype(BF16))
            for s, part in enumerate((plus, minus)):
                near = mm(stacked(part), tab[0, s])
                for i in range(2):
                    lo = near[i * HALF:i * HALF + QUARTER]
                    hi = near[i * HALF + QUARTER:(i + 1) * HALF]
                    for b, mixed in enumerate((lo + hi, lo - hi)):
                        mixed = mixed.astype(BF16)
                        for ri, rows in enumerate((low, high)):
                            half[first + i, b, rows, columns(s)] = mixed[:, columns(ri)]

    def left_and_update_half(c2):
        for s in range(2):
            sums = [None, None]
            for first in range(0, 8, 2):
                near = mm(tab[1, s], beside([half[m, s, :, columns(c2)] for m in (first, first + 1)]))
                nr, ni = near[0:HALF], near[HALF:PATCH]
                pr, pi = pair_probe(first, s, c2)
                for ri, term in enumerate((pr * nr + pi * ni, pr * ni - pi * nr)):
                    term = term[:, 0:HALF] + term[:, HALF:PATCH]
                    sums[ri] = term if sums[ri] is None else sums[ri] + term
            for ri in range(2):
                upd[c2, s, columns(ri), :] = sums[ri]

    def swap(src, dst, which):
        copy = to(src, dst, pair_send.at[which], pair_recv.at[which], partner, j)
        copy.start()
        return copy

    mine = pl.ds(pl.multiple_of(c * HALF, HALF), HALF)
    other = pl.ds(pl.multiple_of((1 - c) * HALF, HALF), HALF)
    for repeat in range(PASSES):
        if repeat == 0:
            for k in range(7):
                exit_and_left(k)
            take(7)
            exit_and_left(7)
        copies = []
        for r in range(2):
            right_and_power_half(r)
            inten_b[repeat, r] = inten[r].astype(BF16)
            copies.append(swap(inten_b.at[repeat, r], inten_in.at[repeat, r], 2 * repeat + r))
        if repeat == 0:
            power_b[...] = power[...].astype(BF16)
            power_copy = swap(power_b, power_in, 8)
        for r in range(2):
            copies[r].wait()
            set_ratio(repeat, r)
            change_and_right_half(r)
        copies = []
        for c2 in range(2):
            left_and_update_half(c2)
            if repeat < PASSES - 1:
                upd_b[c2] = upd[c2].astype(BF16)
                copies.append(swap(upd_b.at[c2], upd_in.at[c2], 4 + c2))
            else:
                last_b[c2] = upd[c2, :, other, :].astype(BF16)
                copies.append(swap(last_b.at[c2], last_in.at[c2], 6 + c2))
        if repeat == 0:
            power_copy.wait()
            whole = power[...] + power_in[...].astype(F32)
            whole = jnp.maximum(whole[0], whole[1])
            highest = jnp.max(jnp.max(whole, axis=0, keepdims=True), axis=1, keepdims=True)
            scale = STEP_SIZE / highest
        if repeat < PASSES - 1:
            for c2 in range(2):
                copies[c2].wait()
                for s in range(2):
                    cur[c2, s] = init[s, :, columns(c2)] + scale * (upd[c2, s] + upd_in[c2, s].astype(F32))
                exit_and_left_half(c2)

    moved = []
    for c2 in range(2):
        copies[c2].wait()
        column = []
        for s in range(2):
            change = cur[c2, s, mine, :] - init[s, mine, columns(c2)]
            change += scale * (upd[c2, s, mine, :] + last_in[c2, s].astype(F32))
            column.append(change.astype(BF16))
        moved.append(stacked(column))
    moved = beside(moved)

    placed = mm(place_r[...], moved).astype(BF16)
    canvas[...] = mm(placed, place_c[...]).astype(BF16)

    for dz, dy in FAR_FIRST:
        mode = ((z + dz) % 4) * 4 + (y + dy) % 4
        src = canvas.at[pl.ds(pl.multiple_of(mode * SLAB, SLAB), SLAB), :]
        dst = slabs.at[c * 8 + slot]

        if (dz, dy) == (0, 0):
            @pl.when(owner)
            def _():
                pltpu.make_async_copy(src, dst, slab_recv).start()

            @pl.when(jnp.logical_not(owner))
            def _():
                to(src, dst, slab_send, slab_recv, s_tile, mode).start()
        else:
            to(src, dst, slab_send, slab_recv, s_tile, mode).start()

    @pl.when(to_prev_x)
    def _():
        info_next.wait_recv()

    @pl.when(c == 0)
    def _():
        info[4] = info[2]

    @pl.when(c == 1)
    def _():
        info[4] = info[1]

    at_row = lax.broadcasted_iota(jnp.int32, (SLAB, 2 * PATCH), 0) + j * SLAB
    at_col = lax.broadcasted_iota(jnp.int32, (SLAB, 2 * PATCH), 1)
    from_above = jnp.where(t > 0, 1.0, 0.0)
    cover = jnp.zeros((SLAB, 2 * PATCH), F32)
    for k in range(2):
        here = info[4 * k]
        part = jnp.zeros((SLAB, 2 * PATCH), F32)
        for i in range(8):
            dr = at_row + k * PATCH - here[i:i + 1, 0:1]
            dc = at_col - here[i:i + 1, 1:2]
            inside = (dr >= 0) & (dr < PATCH) & (dc >= 0) & (dc < PATCH) & (here[i:i + 1, 2:3] > 0)
            part += jnp.where(inside, 1.0, 0.0)
        cover += part if k == 0 else part * from_above
    share = 1.0 / jnp.maximum(cover, 1.0)

    at_row = lax.broadcasted_iota(jnp.int32, (SLAB, PATCH), 0) + j * SLAB
    at_col = lax.broadcasted_iota(jnp.int32, (SLAB, PATCH), 1)

    def gathered(which, table, ri):
        parts = [jnp.zeros((SLAB, PATCH), F32) for _ in range(4)]
        for i in range(8):
            value = slabs[which * 16 + ri * 8 + i].astype(F32)
            in_strip = at_row >= info[table, i:i + 1, 0:1]
            in_left = at_col >= info[table, i:i + 1, 1:2]
            left = jnp.where(in_left, value, 0.0)
            right = value - left
            left_own = jnp.where(in_strip, left, 0.0)
            right_own = jnp.where(in_strip, right, 0.0)
            for p, term in enumerate((left_own, right_own, left - left_own, right - right_own)):
                parts[p] += term
        return jnp.concatenate(parts[0:2], axis=1), jnp.concatenate(parts[2:4], axis=1)

    pltpu.make_async_copy(slabs, slabs, slab_recv).wait()
    spill_copy = to(spill, spill_in, spill_sem.at[0], spill_sem.at[1], up_tile, j)
    sums = [gathered(0, 0, ri) for ri in range(2)]
    for ri in range(2):
        spill[ri] = sums[ri][1].astype(BF16)
        own[ri] = sums[ri][0]

    @pl.when(has_up)
    def _():
        spill_copy.start()

    @pl.when(has_down)
    def _():
        spill_copy.wait_recv()
        for ri in range(2):
            own[ri] += spill_in[ri].astype(F32)

    my_rows = out_ref.at[:, pl.ds(pl.multiple_of(j * SLAB, SLAB), SLAB), :]
    for ri in range(2):
        quot[ri] = (own[ri] * share).astype(BF16)
    for dz, dy in FAR_FIRST[:15]:
        to(quot, my_rows, quot_send, quot_recv, t, ((z + dz) % 4) * 4 + (y + dy) % 4).start()
    keep = pltpu.make_async_copy(quot, my_rows, local_sem.at[4])
    keep.start()

    info_pair.wait_send()

    @pl.when(to_next_x)
    def _():
        info_next.wait_send()

    @pl.when(has_up)
    def _():
        spill_copy.wait_send()

    for here, count in ((owner, 45), (jnp.logical_not(owner), 15)):
        @pl.when(here)
        def _():
            rows = far.at[pl.ds(0, count * 64), :]
            pltpu.make_async_copy(rows, rows, gather_send).wait()

    for here, count in ((owner, 15), (jnp.logical_not(owner), 16)):
        @pl.when(here)
        def _():
            rows = slabs.at[pl.ds(0, count)]
            pltpu.make_async_copy(rows, rows, slab_send).wait()

    rows = strip.at[0, pl.ds(0, 15 * SLAB), :]
    pltpu.make_async_copy(rows, rows, quot_send).wait()
    pltpu.make_async_copy(rows, rows, quot_recv).wait()
    keep.wait()


def shards(object_field, probe_modes, patterns, offsets, counts):
    tables = jnp.asarray(make_tables())
    in_hbm = pl.BlockSpec(memory_space=pltpu.HBM)
    vmem = pltpu.VMEM
    dma = pltpu.SemaphoreType.DMA
    change = pl.pallas_call(
        kernel,
        out_shape=vmem((2, PATCH, 2 * PATCH), BF16),
        in_specs=[
            in_hbm, in_hbm, in_hbm, in_hbm,
            pl.BlockSpec(memory_space=pltpu.SMEM),
            pl.BlockSpec(memory_space=pltpu.SMEM),
        ],
        out_specs=pl.BlockSpec(memory_space=vmem),
        scratch_shapes=[
            vmem((2, PATCH, PATCH), F32),
            vmem((2, PATCH, 2 * PATCH), F32),
            vmem((2, PATCH, 2 * PATCH), BF16),
            vmem((2, 2 * PATCH, 2 * PATCH), BF16),
            vmem((PATCH, PATCH), BF16),
            vmem((2, 2, PATCH, PATCH), BF16),
            vmem((5, 8, HALF), jnp.int32),
            vmem((8, 2, PATCH, PATCH), BF16),
            vmem((8, 2, PATCH, PATCH), BF16),
            vmem((16 * PATCH, PATCH), F32),
            vmem((2, PATCH, PATCH), F32),
            vmem((2, 2, PATCH, HALF), F32),
            vmem((2, 2, HALF, HALF), F32),
            vmem((2, 2, HALF, HALF), F32),
            vmem((2, 2, PATCH, HALF), F32),
            vmem((2, HALF, PATCH), F32),
            vmem((PASSES, 2, 2, HALF, HALF), BF16),
            vmem((2, 2, PATCH, HALF), BF16),
            vmem((2, 2, HALF, HALF), BF16),
            vmem((2, HALF, PATCH), BF16),
            vmem((PASSES, 2, 2, HALF, HALF), BF16),
            vmem((2, 2, PATCH, HALF), BF16),
            vmem((2, 2, HALF, HALF), BF16),
            vmem((2, HALF, PATCH), BF16),
            vmem((PATCH, PATCH), BF16),
            vmem((PATCH, PATCH), BF16),
            vmem((PATCH, PATCH), BF16),
            vmem((16, SLAB, PATCH), BF16),
            vmem((2, SLAB, 2 * PATCH), BF16),
            vmem((2, SLAB, 2 * PATCH), BF16),
            vmem((2, SLAB, 2 * PATCH), F32),
            vmem((2, SLAB, 2 * PATCH), BF16),
            dma((5,)), dma, dma((8, 2, 2)), dma((2,)), dma((4,)), dma((2,)), dma((2,)),
            dma((9,)), dma((9,)), dma, dma, dma((2,)), dma, dma,
        ],
        compiler_params=pltpu.CompilerParams(
            collective_id=0, has_side_effects=True, vmem_limit_bytes=56 * 1024 * 1024
        ),
        cost_estimate=pl.CostEstimate(flops=6 * 10**9, bytes_accessed=8 * 2**20, transcendentals=131072),
    )(object_field, probe_modes, patterns, tables, offsets.T, counts)
    return object_field + change.astype(F32)


def solution(mesh):
    return jax.shard_map(
        shards,
        mesh=mesh,
        in_specs=(
            P(None, "tile", None),
            P("mode", None, None, None),
            P("tile", None, None),
            P("tile", None),
            P("tile"),
        ),
        out_specs=P(None, "tile", None),
        check_vma=False,
    )
```

```python
import math

import numpy as np
import ml_dtypes
import jax
import jax.numpy as jnp
from jax import lax
from jax.experimental import pallas as pl
from jax.experimental.pallas import tpu as pltpu
from jax.sharding import PartitionSpec as P

PATCH = 256
HALF = 128
QUARTER = 64
PASSES = 2
STEP_SIZE = 0.9
SLAB = 16
MESH = pl.DeviceIdType.MESH
BF16 = jnp.bfloat16
F32 = jnp.float32

ORDER = ((0, 0), (1, 0), (0, 1), (0, 3), (0, 2), (1, 1), (1, 3), (1, 2))
SENT_ON_AT_HOME = (
    (0, 1, 0), (0, 3, 0), (0, 2, 0), (1, 0, 1), (0, 1, 1), (0, 3, 1),
    (1, 0, 0), (1, 1, 0), (1, 3, 0), (1, 1, 1), (1, 3, 1),
)
SENT_ON_AWAY = ((0, 0, 1), (1, 0, 1), (0, 0, 0), (0, 1, 0), (0, 3, 0), (0, 1, 1), (0, 3, 1))
FAR_FIRST = sorted(
    ((dz, dy) for dz in range(4) for dy in range(4)), key=lambda d: -min(d[0], 4 - d[0]) - min(d[1], 4 - d[1])
)


def make_tables():
    q = np.arange(HALF)
    tables = []
    for s in range(2):
        a = 2 * np.arange(HALF) + s
        angle = (q[:, None] * a[None, :] % PATCH).astype(np.float32) * np.float32(2.0 * math.pi / PATCH)
        factor = np.float32(1.0 / math.sqrt(PATCH))
        real = (np.cos(angle) * factor).astype(ml_dtypes.bfloat16)
        imag = (-np.sin(angle) * factor).astype(ml_dtypes.bfloat16)
        tables.append(np.block([[real, -imag], [imag, real]]))
    tables = np.stack(tables)
    return np.stack([tables, tables.transpose(0, 2, 1)])


def mm(a, b):
    return jnp.dot(a, b, preferred_element_type=F32)


def natural(position):
    return jnp.where(position < HALF, 2 * position, 2 * position - (PATCH - 1))


def kernel(
    obj_hbm, probe_hbm, pat_hbm, tab_hbm, offs_hbm, counts_hbm, out_ref,
    probe, strip, strip_b, ext, pat, tab, info, modes, half, far, init, cur,
    inten, ratio, upd, power, inten_b, upd_b, last_b, power_b, inten_in, upd_in, last_in, power_in,
    place_r, place_c, canvas, slabs, spill, spill_in, own, quot,
    offs_ref, counts_ref, local_sem, gather_send, gather_recv, strip_sem, info_sem, patch_sem, pat_sem,
    pair_send, pair_recv, slab_send, slab_recv, spill_sem, quot_send, quot_recv,
):
    t = lax.axis_index("tile")
    j = lax.axis_index("mode")
    x, z = t // 2, j // 4
    c, y = t - 2 * x, j - 4 * z
    group = z // 2
    owner = c == group
    s_tile = 2 * x + group
    slot = j - 8 * group
    partner = 2 * x + (1 - c)
    up_tile, down_tile = t + 1, t - 1

    load_probe = pltpu.make_async_copy(probe_hbm.at[0], probe, local_sem.at[0])
    load_strip = pltpu.make_async_copy(obj_hbm, strip, local_sem.at[1])
    load_tab = pltpu.make_async_copy(tab_hbm, tab, local_sem.at[2])
    load_pat = pltpu.make_async_copy(pat_hbm.at[slot], pat, local_sem.at[3])
    load_offs = pltpu.make_async_copy(offs_hbm, offs_ref, local_sem.at[5])
    load_counts = pltpu.make_async_copy(counts_hbm, counts_ref, local_sem.at[6])
    load_offs.start()
    load_counts.start()

    @pl.when(owner)
    def _():
        load_probe.start()
        load_pat.start()

    load_strip.start()
    load_tab.start()

    barrier = pltpu.get_barrier_semaphore()

    def greet(tile, mode):
        pl.semaphore_signal(barrier, inc=1, device_id=(tile, mode), device_id_type=MESH)

    for k in range(1, 16):
        greet(t, (j + k) % 16)
    greet(partner, j)
    has_up, has_down = t < 7, t > 0
    to_next_x = (c == 1) & has_up
    to_prev_x = (c == 0) & has_down

    @pl.when(to_next_x)
    def _():
        greet(up_tile, j)

    @pl.when(to_prev_x)
    def _():
        greet(down_tile, j)

    for k in range(8):
        greet(partner, 8 * c + k)

    load_offs.wait()
    load_counts.wait()
    lane = lax.broadcasted_iota(jnp.int32, (8, HALF), 1)
    live = (lax.broadcasted_iota(jnp.int32, (8, HALF), 0) < counts_ref[0]).astype(jnp.int32)
    place = jnp.where(lane == 2, live, 0)
    line = lax.broadcasted_iota(jnp.int32, (8, HALF), 0)
    for i in range(8):
        for p in range(2):
            place = jnp.where((line == i) & (lane == p), offs_ref[p, i], place)
    info[0] = place

    @pl.when(jnp.logical_not(has_down))
    def _():
        info[2] = jnp.zeros((8, HALF), jnp.int32)


    @pl.when(owner)
    def _():
        load_probe.wait()
        rows = lax.broadcasted_iota(jnp.int32, (PATCH, PATCH), 0)
        cols = lax.broadcasted_iota(jnp.int32, (PATCH, PATCH), 1)
        sort_r = jnp.where(cols == natural(rows), 1.0, 0.0).astype(BF16)
        sort_c = jnp.where(rows == natural(cols), 1.0, 0.0).astype(BF16)
        for ri in range(2):
            plane = mm(sort_r, probe[ri].astype(BF16)).astype(BF16)
            plane = mm(plane, sort_c).astype(BF16)
            for s in range(2):
                modes[0, s, ri * HALF:(ri + 1) * HALF, :] = plane[s * HALF:(s + 1) * HALF]

    sends_strip = jnp.logical_not(owner) & has_down

    @pl.when(sends_strip)
    def _():
        load_strip.wait()
        strip_b[...] = strip[...].astype(BF16)

    @pl.when(jnp.logical_not(owner | has_down))
    def _():
        load_strip.wait()

    across = to_next_x | to_prev_x
    pl.semaphore_wait(
        barrier, 16 + jnp.where(across, 1, 0) + jnp.where(owner, 0, 16)
    )

    def to(src, dst, send, recv, tile, mode):
        return pltpu.make_async_remote_copy(
            src_ref=src, dst_ref=dst, send_sem=send, recv_sem=recv,
            device_id=(tile, mode), device_id_type=MESH,
        )

    info_pair = to(info.at[0], info.at[1], info_sem.at[0], info_sem.at[1], partner, j)
    info_next = to(info.at[0], info.at[2], info_sem.at[2], info_sem.at[3], up_tile, j)
    info_pair.start()

    @pl.when(to_next_x)
    def _():
        info_next.start()

    def block(m, s, h):
        return modes.at[m, s, pl.ds(h * HALF, HALF), :]

    def mode_slot(row, home, dy):
        d = (row - 2 * c + 4) % 4
        nearer = 2 * c + jnp.where((d == 1) | (d == 2), 1, 0)
        return jnp.where(home == nearer, ORDER.index((0, dy)), ORDER.index((1, dy)))

    def relay(k, s, h, home, dy, step_z, step_y):
        row = (z + step_z + 4) % 4
        there = mode_slot(row, home, (dy + step_y) % 4)
        to(
            block(k, s, h), block(there, s, h), gather_send, gather_recv.at[there, s, h],
            t, row * 4 + (y + step_y + 4) % 4,
        ).start()

    def take(which, dy, s):
        k = ORDER.index((which, dy))
        d = (z - 2 * c + 4) % 4
        nearer = jnp.where((d == 1) | (d == 2), 1, 0)
        home = 2 * c + (nearer if which == 0 else 1 - nearer)
        dz = (z - home + 4) % 4
        for h in range(2):
            to(
                block(k, s, h), block(k, s, h), gather_send, gather_recv.at[k, s, h], t, j
            ).wait_recv()
            if s == 0 and dy == 0:
                @pl.when(dz == 0)
                def _():
                    for step in (2, 1, -1):
                        relay(k, s, h, home, dy, 0, step)

            if s == 1 and dy == 0:
                @pl.when(dz == 2)
                def _():
                    relay(k, s, h, home, dy, 0, 2)

                for step in (1, -1):
                    relay(k, s, h, home, dy, 0, step)
            if s == 1 and (dy, h) in ((1, 0), (3, 1)):
                @pl.when(dz != 2)
                def _():
                    relay(k, s, h, home, dy, 0, 2 - dy)

            if s == 0 or dy == 0:
                @pl.when(dz == 0)
                def _():
                    if s == 1 or dy == 2:
                        relay(k, s, h, home, dy, 2, 0)
                    relay(k, s, h, home, dy, 1, 0)
                    relay(k, s, h, home, dy, -1, 0)

            if s == 0 and dy != 2:
                @pl.when(dz == (1 if h == 0 else 3))
                def _():
                    relay(k, s, h, home, dy, 1 if h == 0 else -1, 0)

    def finish(k):
        which, dy = ORDER[k]
        for here, done in ((owner, SENT_ON_AT_HOME), (jnp.logical_not(owner), SENT_ON_AWAY)):
            @pl.when(here)
            def _():
                for s in range(2):
                    if (which, dy, s) not in done and not (k == 0 and done is SENT_ON_AT_HOME):
                        take(which, dy, s)

    send_strip = to(
        strip_b, ext.at[:, pl.ds(PATCH, PATCH), :], strip_sem.at[0], strip_sem.at[1], down_tile, j
    )
    pat_pair = to(pat_hbm.at[slot], pat, pat_sem.at[0], pat_sem.at[1], partner, j)

    @pl.when(owner)
    def _():
        for step in (1, -1, 2):
            for h in range(2):
                relay(0, 0, h, z, 0, 0, step)
                relay(0, 1, h, z, 0, step, 0)
        for h in range(2):
            for step in (1, -1):
                relay(0, 0, h, z, 0, step, 0)
                relay(0, 1, h, z, 0, 0, step)

    @pl.when(sends_strip)
    def _():
        send_strip.start()

    @pl.when(t == 7)
    def _():
        ext[:, PATCH:2 * PATCH, :] = jnp.zeros((2, PATCH, 2 * PATCH), BF16)

    @pl.when(owner)
    def _():
        pat_pair.start()
        load_strip.wait()
        high = strip[...].astype(BF16)
        ext[:, 0:PATCH, :] = high
        strip_b[...] = (strip[...] - high.astype(F32)).astype(BF16)

    for here, order in ((owner, SENT_ON_AT_HOME), (jnp.logical_not(owner), SENT_ON_AWAY)):
        @pl.when(here)
        def _():
            for which, dy, s in order[:5] if order is SENT_ON_AT_HOME else order:
                take(which, dy, s)

    load_tab.wait()
    info_pair.wait_recv()

    @pl.when(owner)
    def _():
        info[3] = info[0]

    @pl.when(jnp.logical_not(owner))
    def _():
        info[3] = info[1]

    row = info[3, pl.ds(slot, 1), :]
    first_row, first_col, alive = row[:, 0:1], row[:, 1:2], row[:, 2:3]
    rows = lax.broadcasted_iota(jnp.int32, (PATCH, PATCH), 0)
    cols = lax.broadcasted_iota(jnp.int32, (PATCH, PATCH), 1)

    def wrapped(at):
        return jnp.where(at >= PATCH, at - PATCH, at)

    place_r[...] = jnp.where((rows == wrapped(first_row + natural(cols))) & (alive > 0), 1.0, 0.0).astype(BF16)
    place_c[...] = jnp.where(cols == wrapped(first_col + natural(rows)), 1.0, 0.0).astype(BF16)

    send_patch = to(init, init, patch_sem.at[0], patch_sem.at[1], partner, j)

    @pl.when(owner)
    def _():
        @pl.when(has_up)
        def _():
            send_strip.wait_recv()

        inside = jnp.where(t == 7, PATCH, 2 * PATCH)
        rows = lax.broadcasted_iota(jnp.int32, (PATCH, 2 * PATCH), 0)
        cols = lax.broadcasted_iota(jnp.int32, (PATCH, 2 * PATCH), 1)
        cut_r = jnp.where((cols == first_row + natural(rows)) & (cols < inside), 1.0, 0.0).astype(BF16)
        rows2 = lax.broadcasted_iota(jnp.int32, (2 * PATCH, PATCH), 0)
        cols2 = lax.broadcasted_iota(jnp.int32, (2 * PATCH, PATCH), 1)
        cut_c = jnp.where(rows2 == first_col + natural(cols2), 1.0, 0.0).astype(BF16)
        for ri in range(2):
            high = mm(cut_r, ext[ri]).astype(BF16)
            low = mm(cut_r[:, 0:PATCH], strip_b[ri]).astype(BF16)
            piece = mm(high, cut_c) + mm(low, cut_c)
            for s in range(2):
                init[s, ri * HALF:(ri + 1) * HALF, :] = piece[s * HALF:(s + 1) * HALF]
        send_patch.start()
        for which, dy, s in SENT_ON_AT_HOME[5:]:
            take(which, dy, s)

    @pl.when(owner)
    def _():
        load_pat.wait()
        pat_pair.wait_send()
        send_patch.wait_send()

    @pl.when(jnp.logical_not(owner))
    def _():
        pat_pair.wait_recv()
        send_patch.wait_recv()

    @pl.when(sends_strip)
    def _():
        send_strip.wait_send()


    def far_rows(m, b, r):
        return pl.ds(((2 * m + b) * 2 + r) * HALF, HALF)

    def columns(s):
        return slice(s * HALF, (s + 1) * HALF)

    def beside(parts):
        return jnp.concatenate(parts, axis=1)

    def stacked(parts):
        return jnp.concatenate(parts, axis=0)

    def exit_and_left(m):
        ends = []
        for s in range(2):
            pr = modes[m, s, 0:HALF, :].astype(F32)
            pi = modes[m, s, HALF:PATCH, :].astype(F32)
            cr = init[s, 0:HALF, :]
            ci = init[s, HALF:PATCH, :]
            wave = stacked([(pr * cr - pi * ci).astype(BF16), (pr * ci + pi * cr).astype(BF16)])
            if m == 0:
                power[s] = pr * pr + pi * pi
            else:
                power[s] += pr * pr + pi * pi
            ends.append(mm(tab[0, s], wave))
        for b, part in enumerate((ends[0] + ends[1], ends[0] - ends[1])):
            part = part.astype(BF16)
            for s in range(2):
                for ri in range(2):
                    half[m, s, b * HALF:(b + 1) * HALF, columns(ri)] = part[
                        ri * HALF:(ri + 1) * HALF, columns(s)
                    ]

    def pair_probe(first, s, c2):
        return [
            beside([modes[m, s, columns(ri), columns(c2)] for m in (first, first + 1)]).astype(F32)
            for ri in range(2)
        ]

    def exit_and_left_half(c2):
        for first in range(0, 8, 2):
            ends = []
            for s in range(2):
                pr, pi = pair_probe(first, s, c2)
                cr = beside([cur[c2, s, 0:HALF, :]] * 2)
                ci = beside([cur[c2, s, HALF:PATCH, :]] * 2)
                wave = stacked([(pr * cr - pi * ci).astype(BF16), (pr * ci + pi * cr).astype(BF16)])
                ends.append(mm(tab[0, s], wave))
            for b, part in enumerate((ends[0] + ends[1], ends[0] - ends[1])):
                part = part.astype(BF16)
                for i in range(2):
                    for ri in range(2):
                        half[first + i, c2, b * HALF:(b + 1) * HALF, columns(ri)] = part[
                            ri * HALF:(ri + 1) * HALF, columns(i)
                        ]

    def row_parts(r):
        return slice(r * QUARTER, (r + 1) * QUARTER), slice(HALF + r * QUARTER, HALF + (r + 1) * QUARTER)

    def right_and_power_half(r):
        low, high = row_parts(r)
        sums = [None, None]
        for first in range(0, 8, 2):
            ends = [
                mm(stacked([half[m, s, rows, :] for m in (first, first + 1) for rows in (low, high)]), tab[1, s])
                for s in range(2)
            ]
            for b, part in enumerate((ends[0] + ends[1], ends[0] - ends[1])):
                for i in range(2):
                    mine = part[i * HALF:(i + 1) * HALF]
                    far[far_rows(first + i, b, r), :] = mine
                    re, im = mine[:, 0:HALF], mine[:, HALF:PATCH]
                    term = re * re + im * im
                    sums[b] = term if sums[b] is None else sums[b] + term
        for b in range(2):
            inten[r, b] = sums[b]

    def set_ratio(repeat, r):
        low, high = row_parts(r)
        for b in range(2):
            total = inten[r, b] + inten_in[repeat, r, b].astype(F32)
            measured = stacked([pat[low, columns(b)], pat[high, columns(b)]]).astype(F32)
            ratio[r, b] = jnp.sqrt(measured / jnp.maximum(total, 1.0)) - 1.0

    def change_and_right_half(r):
        low, high = row_parts(r)
        for first in range(0, 8, 2):
            plus, minus = [], []
            for m in (first, first + 1):
                ya = far[far_rows(m, 0, r), :] * beside([ratio[r, 0]] * 2)
                yb = far[far_rows(m, 1, r), :] * beside([ratio[r, 1]] * 2)
                plus.append((ya + yb).astype(BF16))
                minus.append((ya - yb).astype(BF16))
            for s, part in enumerate((plus, minus)):
                near = mm(stacked(part), tab[0, s])
                for i in range(2):
                    lo = near[i * HALF:i * HALF + QUARTER]
                    hi = near[i * HALF + QUARTER:(i + 1) * HALF]
                    for b, mixed in enumerate((lo + hi, lo - hi)):
                        mixed = mixed.astype(BF16)
                        for ri, rows in enumerate((low, high)):
                            half[first + i, b, rows, columns(s)] = mixed[:, columns(ri)]

    def left_and_update_half(c2):
        for s in range(2):
            sums = [None, None]
            for first in range(0, 8, 2):
                near = mm(tab[1, s], beside([half[m, s, :, columns(c2)] for m in (first, first + 1)]))
                nr, ni = near[0:HALF], near[HALF:PATCH]
                pr, pi = pair_probe(first, s, c2)
                for ri, term in enumerate((pr * nr + pi * ni, pr * ni - pi * nr)):
                    term = term[:, 0:HALF] + term[:, HALF:PATCH]
                    sums[ri] = term if sums[ri] is None else sums[ri] + term
            for ri in range(2):
                upd[c2, s, columns(ri), :] = sums[ri]

    def swap(src, dst, which):
        copy = to(src, dst, pair_send.at[which], pair_recv.at[which], partner, j)
        copy.start()
        return copy

    mine = pl.ds(pl.multiple_of(c * HALF, HALF), HALF)
    other = pl.ds(pl.multiple_of((1 - c) * HALF, HALF), HALF)
    for repeat in range(PASSES):
        if repeat == 0:
            for k in range(8):
                finish(k)
                exit_and_left(k)
        copies = []
        for r in range(2):
            right_and_power_half(r)
            inten_b[repeat, r] = inten[r].astype(BF16)
            copies.append(swap(inten_b.at[repeat, r], inten_in.at[repeat, r], 2 * repeat + r))
        if repeat == 0:
            power_b[...] = power[...].astype(BF16)
            power_copy = swap(power_b, power_in, 8)
        for r in range(2):
            copies[r].wait()
            set_ratio(repeat, r)
            change_and_right_half(r)
        copies = []
        for c2 in range(2):
            left_and_update_half(c2)
            if repeat < PASSES - 1:
                upd_b[c2] = upd[c2].astype(BF16)
                copies.append(swap(upd_b.at[c2], upd_in.at[c2], 4 + c2))
            else:
                last_b[c2] = upd[c2, :, other, :].astype(BF16)
                copies.append(swap(last_b.at[c2], last_in.at[c2], 6 + c2))
        if repeat == 0:
            power_copy.wait()
            whole = power[...] + power_in[...].astype(F32)
            whole = jnp.maximum(whole[0], whole[1])
            highest = jnp.max(jnp.max(whole, axis=0, keepdims=True), axis=1, keepdims=True)
            scale = STEP_SIZE / highest
        if repeat < PASSES - 1:
            for c2 in range(2):
                copies[c2].wait()
                for s in range(2):
                    cur[c2, s] = init[s, :, columns(c2)] + scale * (upd[c2, s] + upd_in[c2, s].astype(F32))
                exit_and_left_half(c2)

    moved = []
    for c2 in range(2):
        copies[c2].wait()
        column = []
        for s in range(2):
            change = cur[c2, s, mine, :] - init[s, mine, columns(c2)]
            change += scale * (upd[c2, s, mine, :] + last_in[c2, s].astype(F32))
            column.append(change.astype(BF16))
        moved.append(stacked(column))
    moved = beside(moved)

    placed = mm(place_r[...], moved).astype(BF16)
    canvas[...] = mm(placed, place_c[...]).astype(BF16)

    for dz, dy in FAR_FIRST:
        mode = ((z + dz) % 4) * 4 + (y + dy) % 4
        src = canvas.at[pl.ds(pl.multiple_of(mode * SLAB, SLAB), SLAB), :]
        dst = slabs.at[c * 8 + slot]

        if (dz, dy) == (0, 0):
            @pl.when(owner)
            def _():
                pltpu.make_async_copy(src, dst, slab_recv).start()

            @pl.when(jnp.logical_not(owner))
            def _():
                to(src, dst, slab_send, slab_recv, s_tile, mode).start()
        else:
            to(src, dst, slab_send, slab_recv, s_tile, mode).start()

    @pl.when(to_prev_x)
    def _():
        info_next.wait_recv()

    @pl.when(c == 0)
    def _():
        info[4] = info[2]

    @pl.when(c == 1)
    def _():
        info[4] = info[1]

    at_row = lax.broadcasted_iota(jnp.int32, (SLAB, 2 * PATCH), 0) + j * SLAB
    at_col = lax.broadcasted_iota(jnp.int32, (SLAB, 2 * PATCH), 1)
    from_above = jnp.where(t > 0, 1.0, 0.0)
    cover = jnp.zeros((SLAB, 2 * PATCH), F32)
    for k in range(2):
        here = info[4 * k]
        part = jnp.zeros((SLAB, 2 * PATCH), F32)
        for i in range(8):
            dr = at_row + k * PATCH - here[i:i + 1, 0:1]
            dc = at_col - here[i:i + 1, 1:2]
            inside = (dr >= 0) & (dr < PATCH) & (dc >= 0) & (dc < PATCH) & (here[i:i + 1, 2:3] > 0)
            part += jnp.where(inside, 1.0, 0.0)
        cover += part if k == 0 else part * from_above
    share = 1.0 / jnp.maximum(cover, 1.0)

    at_row = lax.broadcasted_iota(jnp.int32, (SLAB, PATCH), 0) + j * SLAB
    at_col = lax.broadcasted_iota(jnp.int32, (SLAB, PATCH), 1)

    def gathered(which, table, ri):
        parts = [jnp.zeros((SLAB, PATCH), F32) for _ in range(4)]
        for i in range(8):
            value = slabs[which * 16 + ri * 8 + i].astype(F32)
            in_strip = at_row >= info[table, i:i + 1, 0:1]
            in_left = at_col >= info[table, i:i + 1, 1:2]
            left = jnp.where(in_left, value, 0.0)
            right = value - left
            left_own = jnp.where(in_strip, left, 0.0)
            right_own = jnp.where(in_strip, right, 0.0)
            for p, term in enumerate((left_own, right_own, left - left_own, right - right_own)):
                parts[p] += term
        return jnp.concatenate(parts[0:2], axis=1), jnp.concatenate(parts[2:4], axis=1)

    pltpu.make_async_copy(slabs, slabs, slab_recv).wait()
    spill_copy = to(spill, spill_in, spill_sem.at[0], spill_sem.at[1], up_tile, j)
    sums = [gathered(0, 0, ri) for ri in range(2)]
    for ri in range(2):
        spill[ri] = sums[ri][1].astype(BF16)
        own[ri] = sums[ri][0]

    @pl.when(has_up)
    def _():
        spill_copy.start()

    @pl.when(has_down)
    def _():
        spill_copy.wait_recv()
        for ri in range(2):
            own[ri] += spill_in[ri].astype(F32)

    my_rows = out_ref.at[:, pl.ds(pl.multiple_of(j * SLAB, SLAB), SLAB), :]
    for ri in range(2):
        quot[ri] = (own[ri] * share).astype(BF16)
    for dz, dy in FAR_FIRST[:15]:
        to(quot, my_rows, quot_send, quot_recv, t, ((z + dz) % 4) * 4 + (y + dy) % 4).start()
    keep = pltpu.make_async_copy(quot, my_rows, local_sem.at[4])
    keep.start()

    info_pair.wait_send()

    @pl.when(to_next_x)
    def _():
        info_next.wait_send()

    @pl.when(has_up)
    def _():
        spill_copy.wait_send()

    for here, count in ((owner, 45), (jnp.logical_not(owner), 15)):
        @pl.when(here)
        def _():
            rows = far.at[pl.ds(0, count * 64), :]
            pltpu.make_async_copy(rows, rows, gather_send).wait()

    for here, count in ((owner, 15), (jnp.logical_not(owner), 16)):
        @pl.when(here)
        def _():
            rows = slabs.at[pl.ds(0, count)]
            pltpu.make_async_copy(rows, rows, slab_send).wait()

    rows = strip.at[0, pl.ds(0, 15 * SLAB), :]
    pltpu.make_async_copy(rows, rows, quot_send).wait()
    pltpu.make_async_copy(rows, rows, quot_recv).wait()
    keep.wait()


def shards(object_field, probe_modes, patterns, offsets, counts):
    tables = jnp.asarray(make_tables())
    in_hbm = pl.BlockSpec(memory_space=pltpu.HBM)
    vmem = pltpu.VMEM
    dma = pltpu.SemaphoreType.DMA
    change = pl.pallas_call(
        kernel,
        out_shape=vmem((2, PATCH, 2 * PATCH), BF16),
        in_specs=[
            in_hbm, in_hbm, in_hbm, in_hbm,
            in_hbm, in_hbm,
        ],
        out_specs=pl.BlockSpec(memory_space=vmem),
        scratch_shapes=[
            vmem((2, PATCH, PATCH), F32),
            vmem((2, PATCH, 2 * PATCH), F32),
            vmem((2, PATCH, 2 * PATCH), BF16),
            vmem((2, 2 * PATCH, 2 * PATCH), BF16),
            vmem((PATCH, PATCH), BF16),
            vmem((2, 2, PATCH, PATCH), BF16),
            vmem((5, 8, HALF), jnp.int32),
            vmem((8, 2, PATCH, PATCH), BF16),
            vmem((8, 2, PATCH, PATCH), BF16),
            vmem((16 * PATCH, PATCH), F32),
            vmem((2, PATCH, PATCH), F32),
            vmem((2, 2, PATCH, HALF), F32),
            vmem((2, 2, HALF, HALF), F32),
            vmem((2, 2, HALF, HALF), F32),
            vmem((2, 2, PATCH, HALF), F32),
            vmem((2, HALF, PATCH), F32),
            vmem((PASSES, 2, 2, HALF, HALF), BF16),
            vmem((2, 2, PATCH, HALF), BF16),
            vmem((2, 2, HALF, HALF), BF16),
            vmem((2, HALF, PATCH), BF16),
            vmem((PASSES, 2, 2, HALF, HALF), BF16),
            vmem((2, 2, PATCH, HALF), BF16),
            vmem((2, 2, HALF, HALF), BF16),
            vmem((2, HALF, PATCH), BF16),
            vmem((PATCH, PATCH), BF16),
            vmem((PATCH, PATCH), BF16),
            vmem((PATCH, PATCH), BF16),
            vmem((16, SLAB, PATCH), BF16),
            vmem((2, SLAB, 2 * PATCH), BF16),
            vmem((2, SLAB, 2 * PATCH), BF16),
            vmem((2, SLAB, 2 * PATCH), F32),
            vmem((2, SLAB, 2 * PATCH), BF16),
            pltpu.SMEM((2, 8), jnp.int32), pltpu.SMEM((1,), jnp.int32),
            dma((7,)), dma, dma((8, 2, 2)), dma((2,)), dma((4,)), dma((2,)), dma((2,)),
            dma((9,)), dma((9,)), dma, dma, dma((2,)), dma, dma,
        ],
        compiler_params=pltpu.CompilerParams(
            collective_id=0, has_side_effects=True, vmem_limit_bytes=56 * 1024 * 1024
        ),
        cost_estimate=pl.CostEstimate(flops=6 * 10**9, bytes_accessed=8 * 2**20, transcendentals=131072),
    )(object_field, probe_modes, patterns, tables, offsets.T, counts)
    return object_field + change.astype(F32)


def solution(mesh):
    return jax.shard_map(
        shards,
        mesh=mesh,
        in_specs=(
            P(None, "tile", None),
            P("mode", None, None, None),
            P("tile", None, None),
            P("tile", None),
            P("tile"),
        ),
        out_specs=P(None, "tile", None),
        check_vma=False,
    )
```

```python
import math

import numpy as np
import ml_dtypes
import jax
import jax.numpy as jnp
from jax import lax
from jax.experimental import pallas as pl
from jax.experimental.pallas import tpu as pltpu
from jax.sharding import PartitionSpec as P

PATCH = 256
HALF = 128
QUARTER = 64
PASSES = 2
STEP_SIZE = 0.9
SLAB = 16
MESH = pl.DeviceIdType.MESH
BF16 = jnp.bfloat16
F32 = jnp.float32

ORDER = ((0, 0), (1, 0), (0, 1), (0, 3), (0, 2), (1, 1), (1, 3), (1, 2))
SENT_ON_AT_HOME = (
    (0, 1, 0), (0, 3, 0), (0, 2, 0), (1, 0, 1), (0, 1, 1), (0, 3, 1),
    (1, 0, 0), (1, 1, 0), (1, 3, 0), (1, 1, 1), (1, 3, 1),
)
SENT_ON_AWAY = ((0, 0, 1), (1, 0, 1), (0, 0, 0), (0, 1, 0), (0, 3, 0), (0, 1, 1), (0, 3, 1))
FAR_FIRST = sorted(
    ((dz, dy) for dz in range(4) for dy in range(4)), key=lambda d: -min(d[0], 4 - d[0]) - min(d[1], 4 - d[1])
)


def make_tables():
    q = np.arange(HALF)
    tables = []
    for s in range(2):
        a = 2 * np.arange(HALF) + s
        angle = (q[:, None] * a[None, :] % PATCH).astype(np.float32) * np.float32(2.0 * math.pi / PATCH)
        factor = np.float32(1.0 / math.sqrt(PATCH))
        real = (np.cos(angle) * factor).astype(ml_dtypes.bfloat16)
        imag = (-np.sin(angle) * factor).astype(ml_dtypes.bfloat16)
        tables.append(np.block([[real, -imag], [imag, real]]))
    tables = np.stack(tables)
    return np.stack([tables, tables.transpose(0, 2, 1)])


def mm(a, b):
    return jnp.dot(a, b, preferred_element_type=F32)


def natural(position):
    return jnp.where(position < HALF, 2 * position, 2 * position - (PATCH - 1))


def kernel(
    obj_hbm, probe_hbm, pat_hbm, tab_hbm, offs_hbm, counts_hbm, out_ref,
    probe, strip, strip_b, ext, pat, tab, info, modes, half, far, init, cur,
    inten, ratio, upd, power, inten_b, upd_b, last_b, power_b, inten_in, upd_in, last_in, power_in,
    place_r, place_c, canvas, slabs, spill, spill_in, own, quot,
    offs_ref, counts_ref, local_sem, gather_send, gather_recv, strip_sem, info_sem, patch_sem, pat_sem,
    pair_send, pair_recv, slab_send, slab_recv, spill_sem, quot_send, quot_recv, ring_sem, plane_sem,
):
    t = lax.axis_index("tile")
    j = lax.axis_index("mode")
    x, z = t // 2, j // 4
    c, y = t - 2 * x, j - 4 * z
    group = z // 2
    owner = c == group
    s_tile = 2 * x + group
    slot = j - 8 * group
    partner = 2 * x + (1 - c)
    up_tile, down_tile = t + 1, t - 1

    load_probe = pltpu.make_async_copy(probe_hbm.at[0], probe, local_sem.at[0])
    load_strip = pltpu.make_async_copy(obj_hbm, strip, local_sem.at[1])
    load_tab = pltpu.make_async_copy(tab_hbm, tab, local_sem.at[2])
    load_pat = pltpu.make_async_copy(pat_hbm.at[slot], pat, local_sem.at[3])
    load_offs = pltpu.make_async_copy(offs_hbm, offs_ref, local_sem.at[5])
    load_counts = pltpu.make_async_copy(counts_hbm, counts_ref, local_sem.at[6])
    load_offs.start()
    load_counts.start()

    @pl.when(owner)
    def _():
        load_probe.start()
        load_pat.start()

    load_strip.start()
    load_tab.start()

    barrier = pltpu.get_barrier_semaphore()

    def greet(tile, mode):
        pl.semaphore_signal(barrier, inc=1, device_id=(tile, mode), device_id_type=MESH)

    for k in range(1, 4):
        greet(t, 4 * z + (y + k) % 4)
        greet(t, 4 * ((z + k) % 4) + y)
    greet(partner, j)
    has_up, has_down = t < 7, t > 0
    to_next_x = (c == 1) & has_up
    to_prev_x = (c == 0) & has_down

    @pl.when(to_next_x)
    def _():
        greet(up_tile, j)

    @pl.when(to_prev_x)
    def _():
        greet(down_tile, j)

    load_offs.wait()
    load_counts.wait()
    lane = lax.broadcasted_iota(jnp.int32, (8, HALF), 1)
    live = (lax.broadcasted_iota(jnp.int32, (8, HALF), 0) < counts_ref[0]).astype(jnp.int32)
    place = jnp.where(lane == 2, live, 0)
    line = lax.broadcasted_iota(jnp.int32, (8, HALF), 0)
    for i in range(8):
        for p in range(2):
            place = jnp.where((line == i) & (lane == p), offs_ref[p, i], place)
    info[0] = place

    @pl.when(jnp.logical_not(has_down))
    def _():
        info[2] = jnp.zeros((8, HALF), jnp.int32)


    @pl.when(owner)
    def _():
        load_probe.wait()
        rows = lax.broadcasted_iota(jnp.int32, (PATCH, PATCH), 0)
        cols = lax.broadcasted_iota(jnp.int32, (PATCH, PATCH), 1)
        sort_r = jnp.where(cols == natural(rows), 1.0, 0.0).astype(BF16)
        sort_c = jnp.where(rows == natural(cols), 1.0, 0.0).astype(BF16)
        for ri in range(2):
            plane = mm(sort_r, probe[ri].astype(BF16)).astype(BF16)
            plane = mm(plane, sort_c).astype(BF16)
            for s in range(2):
                modes[0, s, ri * HALF:(ri + 1) * HALF, :] = plane[s * HALF:(s + 1) * HALF]

    sends_strip = jnp.logical_not(owner) & has_down

    @pl.when(sends_strip)
    def _():
        load_strip.wait()
        strip_b[...] = strip[...].astype(BF16)

    @pl.when(jnp.logical_not(owner | has_down))
    def _():
        load_strip.wait()

    across = to_next_x | to_prev_x
    pl.semaphore_wait(barrier, 7 + jnp.where(across, 1, 0))

    def to(src, dst, send, recv, tile, mode):
        return pltpu.make_async_remote_copy(
            src_ref=src, dst_ref=dst, send_sem=send, recv_sem=recv,
            device_id=(tile, mode), device_id_type=MESH,
        )

    info_pair = to(info.at[0], info.at[1], info_sem.at[0], info_sem.at[1], partner, j)
    info_next = to(info.at[0], info.at[2], info_sem.at[2], info_sem.at[3], up_tile, j)
    info_pair.start()

    @pl.when(to_next_x)
    def _():
        info_next.start()

    def block(m, s, h):
        return modes.at[m, s, pl.ds(h * HALF, HALF), :]

    def mode_slot(row, home, dy):
        d = (row - 2 * c + 4) % 4
        nearer = 2 * c + jnp.where((d == 1) | (d == 2), 1, 0)
        return jnp.where(home == nearer, ORDER.index((0, dy)), ORDER.index((1, dy)))

    def relay(k, s, h, home, dy, step_z, step_y):
        row = (z + step_z + 4) % 4
        there = mode_slot(row, home, (dy + step_y) % 4)
        to(
            block(k, s, h), block(there, s, h), gather_send, gather_recv.at[there, s, h],
            t, row * 4 + (y + step_y + 4) % 4,
        ).start()

    def take(which, dy, s):
        k = ORDER.index((which, dy))
        d = (z - 2 * c + 4) % 4
        nearer = jnp.where((d == 1) | (d == 2), 1, 0)
        home = 2 * c + (nearer if which == 0 else 1 - nearer)
        dz = (z - home + 4) % 4
        for h in range(2):
            to(
                block(k, s, h), block(k, s, h), gather_send, gather_recv.at[k, s, h], t, j
            ).wait_recv()
            if s == 0 and dy == 0:
                @pl.when(dz == 0)
                def _():
                    for step in (2, 1, -1):
                        relay(k, s, h, home, dy, 0, step)

            if s == 1 and dy == 0:
                @pl.when(dz == 2)
                def _():
                    relay(k, s, h, home, dy, 0, 2)

                for step in (1, -1):
                    relay(k, s, h, home, dy, 0, step)
            if s == 1 and (dy, h) in ((1, 0), (3, 1)):
                @pl.when(dz != 2)
                def _():
                    relay(k, s, h, home, dy, 0, 2 - dy)

            if s == 0 or dy == 0:
                @pl.when(dz == 0)
                def _():
                    if s == 1 or dy == 2:
                        relay(k, s, h, home, dy, 2, 0)
                    relay(k, s, h, home, dy, 1, 0)
                    relay(k, s, h, home, dy, -1, 0)

            if s == 0 and dy != 2:
                @pl.when(dz == (1 if h == 0 else 3))
                def _():
                    relay(k, s, h, home, dy, 1 if h == 0 else -1, 0)

    def finish(k):
        which, dy = ORDER[k]
        for here, done in ((owner, SENT_ON_AT_HOME), (jnp.logical_not(owner), SENT_ON_AWAY)):
            @pl.when(here)
            def _():
                for s in range(2):
                    if (which, dy, s) not in done and not (k == 0 and done is SENT_ON_AT_HOME):
                        take(which, dy, s)

    send_strip = to(
        strip_b, ext.at[:, pl.ds(PATCH, PATCH), :], strip_sem.at[0], strip_sem.at[1], down_tile, j
    )
    pat_pair = to(pat_hbm.at[slot], pat, pat_sem.at[0], pat_sem.at[1], partner, j)

    @pl.when(owner)
    def _():
        for step in (1, -1, 2):
            for h in range(2):
                relay(0, 0, h, z, 0, 0, step)
                relay(0, 1, h, z, 0, step, 0)
        for h in range(2):
            for step in (1, -1):
                relay(0, 0, h, z, 0, step, 0)
                relay(0, 1, h, z, 0, 0, step)

    @pl.when(sends_strip)
    def _():
        send_strip.start()

    for k in range(1, 4):
        pl.semaphore_signal(ring_sem, inc=1, device_id=(t, 4 * ((z + k) % 4) + y), device_id_type=MESH)

    @pl.when(t == 7)
    def _():
        ext[:, PATCH:2 * PATCH, :] = jnp.zeros((2, PATCH, 2 * PATCH), BF16)

    @pl.when(owner)
    def _():
        pat_pair.start()
        load_strip.wait()
        high = strip[...].astype(BF16)
        ext[:, 0:PATCH, :] = high
        strip_b[...] = (strip[...] - high.astype(F32)).astype(BF16)

    for here, order in ((owner, SENT_ON_AT_HOME), (jnp.logical_not(owner), SENT_ON_AWAY)):
        @pl.when(here)
        def _():
            for which, dy, s in order[:5] if order is SENT_ON_AT_HOME else order:
                take(which, dy, s)

    load_tab.wait()
    info_pair.wait_recv()

    @pl.when(owner)
    def _():
        info[3] = info[0]

    @pl.when(jnp.logical_not(owner))
    def _():
        info[3] = info[1]

    row = info[3, pl.ds(slot, 1), :]
    first_row, first_col, alive = row[:, 0:1], row[:, 1:2], row[:, 2:3]
    rows = lax.broadcasted_iota(jnp.int32, (PATCH, PATCH), 0)
    cols = lax.broadcasted_iota(jnp.int32, (PATCH, PATCH), 1)

    def wrapped(at):
        return jnp.where(at >= PATCH, at - PATCH, at)

    place_r[...] = jnp.where((rows == wrapped(first_row + natural(cols))) & (alive > 0), 1.0, 0.0).astype(BF16)
    place_c[...] = jnp.where(cols == wrapped(first_col + natural(rows)), 1.0, 0.0).astype(BF16)

    send_patch = to(init, init, patch_sem.at[0], patch_sem.at[1], partner, j)

    @pl.when(owner)
    def _():
        @pl.when(has_up)
        def _():
            send_strip.wait_recv()

        inside = jnp.where(t == 7, PATCH, 2 * PATCH)
        rows = lax.broadcasted_iota(jnp.int32, (PATCH, 2 * PATCH), 0)
        cols = lax.broadcasted_iota(jnp.int32, (PATCH, 2 * PATCH), 1)
        cut_r = jnp.where((cols == first_row + natural(rows)) & (cols < inside), 1.0, 0.0).astype(BF16)
        rows2 = lax.broadcasted_iota(jnp.int32, (2 * PATCH, PATCH), 0)
        cols2 = lax.broadcasted_iota(jnp.int32, (2 * PATCH, PATCH), 1)
        cut_c = jnp.where(rows2 == first_col + natural(cols2), 1.0, 0.0).astype(BF16)
        for ri in range(2):
            high = mm(cut_r, ext[ri]).astype(BF16)
            low = mm(cut_r[:, 0:PATCH], strip_b[ri]).astype(BF16)
            piece = mm(high, cut_c) + mm(low, cut_c)
            for s in range(2):
                init[s, ri * HALF:(ri + 1) * HALF, :] = piece[s * HALF:(s + 1) * HALF]
        send_patch.start()
        for which, dy, s in SENT_ON_AT_HOME[5:]:
            take(which, dy, s)

    @pl.when(owner)
    def _():
        load_pat.wait()
        pat_pair.wait_send()
        send_patch.wait_send()

    @pl.when(jnp.logical_not(owner))
    def _():
        pat_pair.wait_recv()
        send_patch.wait_recv()

    @pl.when(sends_strip)
    def _():
        send_strip.wait_send()


    def far_rows(m, b, r):
        return pl.ds(((2 * m + b) * 2 + r) * HALF, HALF)

    def columns(s):
        return slice(s * HALF, (s + 1) * HALF)

    def beside(parts):
        return jnp.concatenate(parts, axis=1)

    def stacked(parts):
        return jnp.concatenate(parts, axis=0)

    def exit_and_left(m):
        ends = []
        for s in range(2):
            pr = modes[m, s, 0:HALF, :].astype(F32)
            pi = modes[m, s, HALF:PATCH, :].astype(F32)
            cr = init[s, 0:HALF, :]
            ci = init[s, HALF:PATCH, :]
            wave = stacked([(pr * cr - pi * ci).astype(BF16), (pr * ci + pi * cr).astype(BF16)])
            if m == 0:
                power[s] = pr * pr + pi * pi
            else:
                power[s] += pr * pr + pi * pi
            ends.append(mm(tab[0, s], wave))
        for b, part in enumerate((ends[0] + ends[1], ends[0] - ends[1])):
            part = part.astype(BF16)
            for s in range(2):
                for ri in range(2):
                    half[m, s, b * HALF:(b + 1) * HALF, columns(ri)] = part[
                        ri * HALF:(ri + 1) * HALF, columns(s)
                    ]

    def pair_probe(first, s, c2):
        return [
            beside([modes[m, s, columns(ri), columns(c2)] for m in (first, first + 1)]).astype(F32)
            for ri in range(2)
        ]

    def exit_and_left_half(c2):
        for first in range(0, 8, 2):
            ends = []
            for s in range(2):
                pr, pi = pair_probe(first, s, c2)
                cr = beside([cur[c2, s, 0:HALF, :]] * 2)
                ci = beside([cur[c2, s, HALF:PATCH, :]] * 2)
                wave = stacked([(pr * cr - pi * ci).astype(BF16), (pr * ci + pi * cr).astype(BF16)])
                ends.append(mm(tab[0, s], wave))
            for b, part in enumerate((ends[0] + ends[1], ends[0] - ends[1])):
                part = part.astype(BF16)
                for i in range(2):
                    for ri in range(2):
                        half[first + i, c2, b * HALF:(b + 1) * HALF, columns(ri)] = part[
                            ri * HALF:(ri + 1) * HALF, columns(i)
                        ]

    def row_parts(r):
        return slice(r * QUARTER, (r + 1) * QUARTER), slice(HALF + r * QUARTER, HALF + (r + 1) * QUARTER)

    def right_and_power_half(r):
        low, high = row_parts(r)
        sums = [None, None]
        for first in range(0, 8, 2):
            ends = [
                mm(stacked([half[m, s, rows, :] for m in (first, first + 1) for rows in (low, high)]), tab[1, s])
                for s in range(2)
            ]
            for b, part in enumerate((ends[0] + ends[1], ends[0] - ends[1])):
                for i in range(2):
                    mine = part[i * HALF:(i + 1) * HALF]
                    far[far_rows(first + i, b, r), :] = mine
                    re, im = mine[:, 0:HALF], mine[:, HALF:PATCH]
                    term = re * re + im * im
                    sums[b] = term if sums[b] is None else sums[b] + term
        for b in range(2):
            inten[r, b] = sums[b]

    def set_ratio(repeat, r):
        low, high = row_parts(r)
        for b in range(2):
            total = inten[r, b] + inten_in[repeat, r, b].astype(F32)
            measured = stacked([pat[low, columns(b)], pat[high, columns(b)]]).astype(F32)
            ratio[r, b] = jnp.sqrt(measured / jnp.maximum(total, 1.0)) - 1.0

    def change_and_right_half(r):
        low, high = row_parts(r)
        for first in range(0, 8, 2):
            plus, minus = [], []
            for m in (first, first + 1):
                ya = far[far_rows(m, 0, r), :] * beside([ratio[r, 0]] * 2)
                yb = far[far_rows(m, 1, r), :] * beside([ratio[r, 1]] * 2)
                plus.append((ya + yb).astype(BF16))
                minus.append((ya - yb).astype(BF16))
            for s, part in enumerate((plus, minus)):
                near = mm(stacked(part), tab[0, s])
                for i in range(2):
                    lo = near[i * HALF:i * HALF + QUARTER]
                    hi = near[i * HALF + QUARTER:(i + 1) * HALF]
                    for b, mixed in enumerate((lo + hi, lo - hi)):
                        mixed = mixed.astype(BF16)
                        for ri, rows in enumerate((low, high)):
                            half[first + i, b, rows, columns(s)] = mixed[:, columns(ri)]

    def left_and_update_half(c2):
        for s in range(2):
            sums = [None, None]
            for first in range(0, 8, 2):
                near = mm(tab[1, s], beside([half[m, s, :, columns(c2)] for m in (first, first + 1)]))
                nr, ni = near[0:HALF], near[HALF:PATCH]
                pr, pi = pair_probe(first, s, c2)
                for ri, term in enumerate((pr * nr + pi * ni, pr * ni - pi * nr)):
                    term = term[:, 0:HALF] + term[:, HALF:PATCH]
                    sums[ri] = term if sums[ri] is None else sums[ri] + term
            for ri in range(2):
                upd[c2, s, columns(ri), :] = sums[ri]

    def swap(src, dst, which):
        copy = to(src, dst, pair_send.at[which], pair_recv.at[which], partner, j)
        copy.start()
        return copy

    mine = pl.ds(pl.multiple_of(c * HALF, HALF), HALF)
    other = pl.ds(pl.multiple_of((1 - c) * HALF, HALF), HALF)
    for repeat in range(PASSES):
        if repeat == 0:
            for k in range(8):
                finish(k)
                exit_and_left(k)
        copies = []
        for r in range(2):
            right_and_power_half(r)
            inten_b[repeat, r] = inten[r].astype(BF16)
            copies.append(swap(inten_b.at[repeat, r], inten_in.at[repeat, r], 2 * repeat + r))
        if repeat == 0:
            power_b[...] = power[...].astype(BF16)
            power_copy = swap(power_b, power_in, 8)
        for r in range(2):
            copies[r].wait()
            set_ratio(repeat, r)
            change_and_right_half(r)
        copies = []
        for c2 in range(2):
            left_and_update_half(c2)
            if repeat < PASSES - 1:
                upd_b[c2] = upd[c2].astype(BF16)
                copies.append(swap(upd_b.at[c2], upd_in.at[c2], 4 + c2))
            else:
                last_b[c2] = upd[c2, :, other, :].astype(BF16)
                copies.append(swap(last_b.at[c2], last_in.at[c2], 6 + c2))
        if repeat == 0:
            power_copy.wait()
            whole = power[...] + power_in[...].astype(F32)
            whole = jnp.maximum(whole[0], whole[1])
            highest = jnp.max(jnp.max(whole, axis=0, keepdims=True), axis=1, keepdims=True)
            scale = STEP_SIZE / highest
        if repeat < PASSES - 1:
            for c2 in range(2):
                copies[c2].wait()
                for s in range(2):
                    cur[c2, s] = init[s, :, columns(c2)] + scale * (upd[c2, s] + upd_in[c2, s].astype(F32))
                exit_and_left_half(c2)

    pl.semaphore_wait(ring_sem, 3)
    pl.semaphore_signal(plane_sem, inc=1, device_id=(partner, j), device_id_type=MESH)
    pl.semaphore_wait(plane_sem, 1)

    moved = []
    for c2 in range(2):
        copies[c2].wait()
        column = []
        for s in range(2):
            change = cur[c2, s, mine, :] - init[s, mine, columns(c2)]
            change += scale * (upd[c2, s, mine, :] + last_in[c2, s].astype(F32))
            column.append(change.astype(BF16))
        moved.append(stacked(column))
    moved = beside(moved)

    placed = mm(place_r[...], moved).astype(BF16)
    canvas[...] = mm(placed, place_c[...]).astype(BF16)

    for dz, dy in FAR_FIRST:
        mode = ((z + dz) % 4) * 4 + (y + dy) % 4
        src = canvas.at[pl.ds(pl.multiple_of(mode * SLAB, SLAB), SLAB), :]
        dst = slabs.at[c * 8 + slot]

        if (dz, dy) == (0, 0):
            @pl.when(owner)
            def _():
                pltpu.make_async_copy(src, dst, slab_recv).start()

            @pl.when(jnp.logical_not(owner))
            def _():
                to(src, dst, slab_send, slab_recv, s_tile, mode).start()
        else:
            to(src, dst, slab_send, slab_recv, s_tile, mode).start()

    @pl.when(to_prev_x)
    def _():
        info_next.wait_recv()

    @pl.when(c == 0)
    def _():
        info[4] = info[2]

    @pl.when(c == 1)
    def _():
        info[4] = info[1]

    at_row = lax.broadcasted_iota(jnp.int32, (SLAB, 2 * PATCH), 0) + j * SLAB
    at_col = lax.broadcasted_iota(jnp.int32, (SLAB, 2 * PATCH), 1)
    from_above = jnp.where(t > 0, 1.0, 0.0)
    cover = jnp.zeros((SLAB, 2 * PATCH), F32)
    for k in range(2):
        here = info[4 * k]
        part = jnp.zeros((SLAB, 2 * PATCH), F32)
        for i in range(8):
            dr = at_row + k * PATCH - here[i:i + 1, 0:1]
            dc = at_col - here[i:i + 1, 1:2]
            inside = (dr >= 0) & (dr < PATCH) & (dc >= 0) & (dc < PATCH) & (here[i:i + 1, 2:3] > 0)
            part += jnp.where(inside, 1.0, 0.0)
        cover += part if k == 0 else part * from_above
    share = 1.0 / jnp.maximum(cover, 1.0)

    at_row = lax.broadcasted_iota(jnp.int32, (SLAB, PATCH), 0) + j * SLAB
    at_col = lax.broadcasted_iota(jnp.int32, (SLAB, PATCH), 1)

    def gathered(which, table, ri):
        parts = [jnp.zeros((SLAB, PATCH), F32) for _ in range(4)]
        for i in range(8):
            value = slabs[which * 16 + ri * 8 + i].astype(F32)
            in_strip = at_row >= info[table, i:i + 1, 0:1]
            in_left = at_col >= info[table, i:i + 1, 1:2]
            left = jnp.where(in_left, value, 0.0)
            right = value - left
            left_own = jnp.where(in_strip, left, 0.0)
            right_own = jnp.where(in_strip, right, 0.0)
            for p, term in enumerate((left_own, right_own, left - left_own, right - right_own)):
                parts[p] += term
        return jnp.concatenate(parts[0:2], axis=1), jnp.concatenate(parts[2:4], axis=1)

    pltpu.make_async_copy(slabs, slabs, slab_recv).wait()
    spill_copy = to(spill, spill_in, spill_sem.at[0], spill_sem.at[1], up_tile, j)
    sums = [gathered(0, 0, ri) for ri in range(2)]
    for ri in range(2):
        spill[ri] = sums[ri][1].astype(BF16)
        own[ri] = sums[ri][0]

    @pl.when(has_up)
    def _():
        spill_copy.start()

    @pl.when(has_down)
    def _():
        spill_copy.wait_recv()
        for ri in range(2):
            own[ri] += spill_in[ri].astype(F32)

    my_rows = out_ref.at[:, pl.ds(pl.multiple_of(j * SLAB, SLAB), SLAB), :]
    for ri in range(2):
        quot[ri] = (own[ri] * share).astype(BF16)
    for dz, dy in FAR_FIRST[:15]:
        to(quot, my_rows, quot_send, quot_recv, t, ((z + dz) % 4) * 4 + (y + dy) % 4).start()
    keep = pltpu.make_async_copy(quot, my_rows, local_sem.at[4])
    keep.start()

    info_pair.wait_send()

    @pl.when(to_next_x)
    def _():
        info_next.wait_send()

    @pl.when(has_up)
    def _():
        spill_copy.wait_send()

    for here, count in ((owner, 45), (jnp.logical_not(owner), 15)):
        @pl.when(here)
        def _():
            rows = far.at[pl.ds(0, count * 64), :]
            pltpu.make_async_copy(rows, rows, gather_send).wait()

    for here, count in ((owner, 15), (jnp.logical_not(owner), 16)):
        @pl.when(here)
        def _():
            rows = slabs.at[pl.ds(0, count)]
            pltpu.make_async_copy(rows, rows, slab_send).wait()

    rows = strip.at[0, pl.ds(0, 15 * SLAB), :]
    pltpu.make_async_copy(rows, rows, quot_send).wait()
    pltpu.make_async_copy(rows, rows, quot_recv).wait()
    keep.wait()


def shards(object_field, probe_modes, patterns, offsets, counts):
    tables = jnp.asarray(make_tables())
    in_hbm = pl.BlockSpec(memory_space=pltpu.HBM)
    vmem = pltpu.VMEM
    dma = pltpu.SemaphoreType.DMA
    change = pl.pallas_call(
        kernel,
        out_shape=vmem((2, PATCH, 2 * PATCH), BF16),
        in_specs=[
            in_hbm, in_hbm, in_hbm, in_hbm,
            in_hbm, in_hbm,
        ],
        out_specs=pl.BlockSpec(memory_space=vmem),
        scratch_shapes=[
            vmem((2, PATCH, PATCH), F32),
            vmem((2, PATCH, 2 * PATCH), F32),
            vmem((2, PATCH, 2 * PATCH), BF16),
            vmem((2, 2 * PATCH, 2 * PATCH), BF16),
            vmem((PATCH, PATCH), BF16),
            vmem((2, 2, PATCH, PATCH), BF16),
            vmem((5, 8, HALF), jnp.int32),
            vmem((8, 2, PATCH, PATCH), BF16),
            vmem((8, 2, PATCH, PATCH), BF16),
            vmem((16 * PATCH, PATCH), F32),
            vmem((2, PATCH, PATCH), F32),
            vmem((2, 2, PATCH, HALF), F32),
            vmem((2, 2, HALF, HALF), F32),
            vmem((2, 2, HALF, HALF), F32),
            vmem((2, 2, PATCH, HALF), F32),
            vmem((2, HALF, PATCH), F32),
            vmem((PASSES, 2, 2, HALF, HALF), BF16),
            vmem((2, 2, PATCH, HALF), BF16),
            vmem((2, 2, HALF, HALF), BF16),
            vmem((2, HALF, PATCH), BF16),
            vmem((PASSES, 2, 2, HALF, HALF), BF16),
            vmem((2, 2, PATCH, HALF), BF16),
            vmem((2, 2, HALF, HALF), BF16),
            vmem((2, HALF, PATCH), BF16),
            vmem((PATCH, PATCH), BF16),
            vmem((PATCH, PATCH), BF16),
            vmem((PATCH, PATCH), BF16),
            vmem((16, SLAB, PATCH), BF16),
            vmem((2, SLAB, 2 * PATCH), BF16),
            vmem((2, SLAB, 2 * PATCH), BF16),
            vmem((2, SLAB, 2 * PATCH), F32),
            vmem((2, SLAB, 2 * PATCH), BF16),
            pltpu.SMEM((2, 8), jnp.int32), pltpu.SMEM((1,), jnp.int32),
            dma((7,)), dma, dma((8, 2, 2)), dma((2,)), dma((4,)), dma((2,)), dma((2,)),
            dma((9,)), dma((9,)), dma, dma, dma((2,)), dma, dma,
            pltpu.SemaphoreType.REGULAR, pltpu.SemaphoreType.REGULAR,
        ],
        compiler_params=pltpu.CompilerParams(
            collective_id=0, has_side_effects=True, vmem_limit_bytes=56 * 1024 * 1024
        ),
        cost_estimate=pl.CostEstimate(flops=6 * 10**9, bytes_accessed=8 * 2**20, transcendentals=131072),
    )(object_field, probe_modes, patterns, tables, offsets.T, counts)
    return object_field + change.astype(F32)


def solution(mesh):
    return jax.shard_map(
        shards,
        mesh=mesh,
        in_specs=(
            P(None, "tile", None),
            P("mode", None, None, None),
            P("tile", None, None),
            P("tile", None),
            P("tile"),
        ),
        out_specs=P(None, "tile", None),
        check_vma=False,
    )
```

```python
import math

import numpy as np
import ml_dtypes
import jax
import jax.numpy as jnp
from jax import lax
from jax.experimental import pallas as pl
from jax.experimental.pallas import tpu as pltpu
from jax.sharding import PartitionSpec as P

PATCH = 256
HALF = 128
QUARTER = 64
PASSES = 2
STEP_SIZE = 0.9
SLAB = 16
MESH = pl.DeviceIdType.MESH
BF16 = jnp.bfloat16
F32 = jnp.float32

ORDER = ((0, 0), (1, 0), (0, 1), (0, 3), (0, 2), (1, 1), (1, 3), (1, 2))
SENT_ON_AT_HOME = (
    (0, 1, 0), (0, 3, 0), (0, 2, 0), (1, 0, 1), (0, 1, 1), (0, 3, 1),
    (1, 0, 0), (1, 1, 0), (1, 3, 0), (1, 1, 1), (1, 3, 1), (1, 2, 0),
)
SENT_ON_AWAY = ((0, 0, 1), (1, 0, 1), (0, 0, 0), (0, 1, 0), (0, 3, 0), (0, 1, 1), (0, 3, 1), (0, 2, 0))
FAR_FIRST = sorted(
    ((dz, dy) for dz in range(4) for dy in range(4)), key=lambda d: -min(d[0], 4 - d[0]) - min(d[1], 4 - d[1])
)


def make_tables():
    q = np.arange(HALF)
    tables = []
    for s in range(2):
        a = 2 * np.arange(HALF) + s
        angle = (q[:, None] * a[None, :] % PATCH).astype(np.float32) * np.float32(2.0 * math.pi / PATCH)
        factor = np.float32(1.0 / math.sqrt(PATCH))
        real = (np.cos(angle) * factor).astype(ml_dtypes.bfloat16)
        imag = (-np.sin(angle) * factor).astype(ml_dtypes.bfloat16)
        tables.append(np.block([[real, -imag], [imag, real]]))
    tables = np.stack(tables)
    return np.stack([tables, tables.transpose(0, 2, 1)])


def mm(a, b):
    return jnp.dot(a, b, preferred_element_type=F32)


def natural(position):
    return jnp.where(position < HALF, 2 * position, 2 * position - (PATCH - 1))


def kernel(
    obj_hbm, probe_hbm, pat_hbm, tab_hbm, offs_hbm, counts_hbm, out_ref,
    probe, strip, strip_b, ext, pat, tab, info, modes, half, far, init, cur,
    inten, root, ratio, upd, power, inten_b, upd_b, last_b, power_b, inten_in, upd_in, last_in, power_in,
    place_r, place_c, canvas, slabs, masks, spill, spill_in, own, quot,
    offs_ref, counts_ref, local_sem, gather_send, gather_recv, strip_sem, info_sem, patch_sem, pat_sem,
    pair_send, pair_recv, slab_send, slab_recv, spill_sem, quot_send, quot_recv, ring_sem, plane_sem,
):
    t = lax.axis_index("tile")
    j = lax.axis_index("mode")
    x, z = t // 2, j // 4
    c, y = t - 2 * x, j - 4 * z
    group = z // 2
    owner = c == group
    s_tile = 2 * x + group
    slot = j - 8 * group
    partner = 2 * x + (1 - c)
    up_tile, down_tile = t + 1, t - 1

    load_probe = pltpu.make_async_copy(probe_hbm.at[0], probe, local_sem.at[0])
    load_strip = pltpu.make_async_copy(obj_hbm, strip, local_sem.at[1])
    load_tab = pltpu.make_async_copy(tab_hbm, tab, local_sem.at[2])
    load_pat = pltpu.make_async_copy(pat_hbm.at[slot], pat, local_sem.at[3])
    @pl.when(owner)
    def _():
        load_probe.start()

    barrier = pltpu.get_barrier_semaphore()

    def greet(tile, mode):
        pl.semaphore_signal(barrier, inc=1, device_id=(tile, mode), device_id_type=MESH)

    for k in range(1, 4):
        greet(t, 4 * z + (y + k) % 4)
        greet(t, 4 * ((z + k) % 4) + y)
    greet(partner, j)
    has_up, has_down = t < 7, t > 0
    to_next_x = (c == 1) & has_up
    to_prev_x = (c == 0) & has_down

    @pl.when(to_next_x)
    def _():
        greet(up_tile, j)

    @pl.when(to_prev_x)
    def _():
        greet(down_tile, j)

    load_offs = pltpu.make_async_copy(offs_hbm, offs_ref, local_sem.at[5])
    load_counts = pltpu.make_async_copy(counts_hbm, counts_ref, local_sem.at[6])
    load_offs.start()
    load_counts.start()

    @pl.when(owner)
    def _():
        load_pat.start()

    load_strip.start()
    load_tab.start()

    @pl.when(owner)
    def _():
        load_probe.wait()
        rows = lax.broadcasted_iota(jnp.int32, (PATCH, PATCH), 0)
        cols = lax.broadcasted_iota(jnp.int32, (PATCH, PATCH), 1)
        sort_r = jnp.where(cols == natural(rows), 1.0, 0.0).astype(BF16)
        sort_c = jnp.where(rows == natural(cols), 1.0, 0.0).astype(BF16)
        for ri in range(2):
            plane = mm(sort_r, probe[ri].astype(BF16)).astype(BF16)
            plane = mm(plane, sort_c).astype(BF16)
            for s in range(2):
                modes[0, s, ri * HALF:(ri + 1) * HALF, :] = plane[s * HALF:(s + 1) * HALF]

    sends_strip = jnp.logical_not(owner) & has_down

    @pl.when(sends_strip)
    def _():
        load_strip.wait()
        strip_b[...] = strip[...].astype(BF16)

    @pl.when(jnp.logical_not(owner | has_down))
    def _():
        load_strip.wait()

    across = to_next_x | to_prev_x
    pl.semaphore_wait(barrier, 7 + jnp.where(across, 1, 0))

    def to(src, dst, send, recv, tile, mode):
        return pltpu.make_async_remote_copy(
            src_ref=src, dst_ref=dst, send_sem=send, recv_sem=recv,
            device_id=(tile, mode), device_id_type=MESH,
        )

    def block(m, s, h):
        return modes.at[m, s, pl.ds(h * HALF, HALF), :]

    def mode_slot(row, home, dy):
        d = (row - 2 * c + 4) % 4
        nearer = 2 * c + jnp.where((d == 1) | (d == 2), 1, 0)
        return jnp.where(home == nearer, ORDER.index((0, dy)), ORDER.index((1, dy)))

    def relay(k, s, h, home, dy, step_z, step_y):
        row = (z + step_z + 4) % 4
        there = mode_slot(row, home, (dy + step_y) % 4)
        to(
            block(k, s, h), block(there, s, h), gather_send, gather_recv.at[there, s, h],
            t, row * 4 + (y + step_y + 4) % 4,
        ).start()

    def take(which, dy, s):
        k = ORDER.index((which, dy))
        d = (z - 2 * c + 4) % 4
        nearer = jnp.where((d == 1) | (d == 2), 1, 0)
        home = 2 * c + (nearer if which == 0 else 1 - nearer)
        dz = (z - home + 4) % 4
        for h in range(2):
            to(
                block(k, s, h), block(k, s, h), gather_send, gather_recv.at[k, s, h], t, j
            ).wait_recv()
            if s == 0 and dy == 0:
                @pl.when(dz == 0)
                def _():
                    for step in (2, 1, -1):
                        relay(k, s, h, home, dy, 0, step)

            if s == 1 and dy == 0:
                @pl.when(dz == 2)
                def _():
                    relay(k, s, h, home, dy, 0, 2)

                for step in (1, -1):
                    relay(k, s, h, home, dy, 0, step)
            if s == 1 and (dy, h) in ((1, 0), (3, 1)):
                @pl.when(dz != 2)
                def _():
                    relay(k, s, h, home, dy, 0, 2 - dy)

            if s == 0 or dy == 0:
                @pl.when(dz == 0)
                def _():
                    if s == 1:
                        relay(k, s, h, home, dy, 2, 0)
                    relay(k, s, h, home, dy, 1, 0)
                    relay(k, s, h, home, dy, -1, 0)

            if s == 0:
                @pl.when(dz == (1 if h == 0 else 3))
                def _():
                    relay(k, s, h, home, dy, 1 if h == 0 else -1, 0)

    def finish(k):
        which, dy = ORDER[k]
        for here, done in ((owner, SENT_ON_AT_HOME), (jnp.logical_not(owner), SENT_ON_AWAY)):
            @pl.when(here)
            def _():
                for s in range(2):
                    if (which, dy, s) not in done and not (k == 0 and done is SENT_ON_AT_HOME):
                        take(which, dy, s)

    send_strip = to(
        strip_b, ext.at[:, pl.ds(PATCH, PATCH), :], strip_sem.at[0], strip_sem.at[1], down_tile, j
    )
    pat_pair = to(pat_hbm.at[slot], pat, pat_sem.at[0], pat_sem.at[1], partner, j)

    @pl.when(owner)
    def _():
        for step in (1, -1, 2):
            for h in range(2):
                relay(0, 0, h, z, 0, 0, step)
                relay(0, 1, h, z, 0, step, 0)
        for h in range(2):
            for step in (1, -1):
                relay(0, 0, h, z, 0, step, 0)
                relay(0, 1, h, z, 0, 0, step)

    @pl.when(sends_strip)
    def _():
        send_strip.start()

    load_offs.wait()
    load_counts.wait()
    lane = lax.broadcasted_iota(jnp.int32, (8, HALF), 1)
    live = (lax.broadcasted_iota(jnp.int32, (8, HALF), 0) < counts_ref[0]).astype(jnp.int32)
    place = jnp.where(lane == 2, live, 0)
    line = lax.broadcasted_iota(jnp.int32, (8, HALF), 0)
    for i in range(8):
        for p in range(2):
            place = jnp.where((line == i) & (lane == p), offs_ref[p, i], place)
    info[0] = place

    @pl.when(jnp.logical_not(has_down))
    def _():
        info[2] = jnp.zeros((8, HALF), jnp.int32)


    info_pair = to(info.at[0], info.at[1], info_sem.at[0], info_sem.at[1], partner, j)
    info_next = to(info.at[0], info.at[2], info_sem.at[2], info_sem.at[3], up_tile, j)
    info_pair.start()

    @pl.when(to_next_x)
    def _():
        info_next.start()

    for k in range(1, 4):
        pl.semaphore_signal(ring_sem, inc=1, device_id=(t, 4 * ((z + k) % 4) + y), device_id_type=MESH)

    @pl.when(t == 7)
    def _():
        ext[:, PATCH:2 * PATCH, :] = jnp.zeros((2, PATCH, 2 * PATCH), BF16)

    @pl.when(owner)
    def _():
        pat_pair.start()
        load_strip.wait()
        high = strip[...].astype(BF16)
        ext[:, 0:PATCH, :] = high
        strip_b[...] = (strip[...] - high.astype(F32)).astype(BF16)

    for here, order in ((owner, SENT_ON_AT_HOME), (jnp.logical_not(owner), SENT_ON_AWAY)):
        @pl.when(here)
        def _():
            for which, dy, s in order[:8] if order is SENT_ON_AT_HOME else order:
                take(which, dy, s)

    load_tab.wait()
    info_pair.wait_recv()

    @pl.when(owner)
    def _():
        info[3] = info[0]

    @pl.when(jnp.logical_not(owner))
    def _():
        info[3] = info[1]

    row = info[3, pl.ds(slot, 1), :]
    first_row, first_col, alive = row[:, 0:1], row[:, 1:2], row[:, 2:3]
    rows = lax.broadcasted_iota(jnp.int32, (PATCH, PATCH), 0)
    cols = lax.broadcasted_iota(jnp.int32, (PATCH, PATCH), 1)

    def wrapped(at):
        return jnp.where(at >= PATCH, at - PATCH, at)

    place_r[...] = jnp.where((rows == wrapped(first_row + natural(cols))) & (alive > 0), 1.0, 0.0).astype(BF16)
    place_c[...] = jnp.where(cols == wrapped(first_col + natural(rows)), 1.0, 0.0).astype(BF16)

    send_patch = to(init, init, patch_sem.at[0], patch_sem.at[1], partner, j)

    @pl.when(owner)
    def _():
        @pl.when(has_up)
        def _():
            send_strip.wait_recv()

        inside = jnp.where(t == 7, PATCH, 2 * PATCH)
        rows = lax.broadcasted_iota(jnp.int32, (PATCH, 2 * PATCH), 0)
        cols = lax.broadcasted_iota(jnp.int32, (PATCH, 2 * PATCH), 1)
        cut_r = jnp.where((cols == first_row + natural(rows)) & (cols < inside), 1.0, 0.0).astype(BF16)
        rows2 = lax.broadcasted_iota(jnp.int32, (2 * PATCH, PATCH), 0)
        cols2 = lax.broadcasted_iota(jnp.int32, (2 * PATCH, PATCH), 1)
        cut_c = jnp.where(rows2 == first_col + natural(cols2), 1.0, 0.0).astype(BF16)
        for ri in range(2):
            high = mm(cut_r, ext[ri]).astype(BF16)
            low = mm(cut_r[:, 0:PATCH], strip_b[ri]).astype(BF16)
            piece = mm(high, cut_c) + mm(low, cut_c)
            for s in range(2):
                init[s, ri * HALF:(ri + 1) * HALF, :] = piece[s * HALF:(s + 1) * HALF]
        send_patch.start()
        for which, dy, s in SENT_ON_AT_HOME[8:]:
            take(which, dy, s)

    @pl.when(owner)
    def _():
        load_pat.wait()
        pat_pair.wait_send()
        send_patch.wait_send()

    @pl.when(jnp.logical_not(owner))
    def _():
        pat_pair.wait_recv()
        send_patch.wait_recv()

    @pl.when(sends_strip)
    def _():
        send_strip.wait_send()


    def far_rows(m, b, r):
        return pl.ds(((2 * m + b) * 2 + r) * HALF, HALF)

    def columns(s):
        return slice(s * HALF, (s + 1) * HALF)

    def beside(parts):
        return jnp.concatenate(parts, axis=1)

    def stacked(parts):
        return jnp.concatenate(parts, axis=0)

    def exit_and_left(m):
        ends = []
        for s in range(2):
            pr = modes[m, s, 0:HALF, :].astype(F32)
            pi = modes[m, s, HALF:PATCH, :].astype(F32)
            cr = init[s, 0:HALF, :]
            ci = init[s, HALF:PATCH, :]
            wave = stacked([(pr * cr - pi * ci).astype(BF16), (pr * ci + pi * cr).astype(BF16)])
            if m == 0:
                power[s] = pr * pr + pi * pi
            else:
                power[s] += pr * pr + pi * pi
            ends.append(mm(tab[0, s], wave))
        for b, part in enumerate((ends[0] + ends[1], ends[0] - ends[1])):
            part = part.astype(BF16)
            for s in range(2):
                for ri in range(2):
                    half[m, s, b * HALF:(b + 1) * HALF, columns(ri)] = part[
                        ri * HALF:(ri + 1) * HALF, columns(s)
                    ]

    def pair_probe(first, s, c2):
        return [
            beside([modes[m, s, columns(ri), columns(c2)] for m in (first, first + 1)]).astype(F32)
            for ri in range(2)
        ]

    def exit_and_left_half(c2):
        for first in range(0, 8, 2):
            ends = []
            for s in range(2):
                pr, pi = pair_probe(first, s, c2)
                cr = beside([cur[c2, s, 0:HALF, :]] * 2)
                ci = beside([cur[c2, s, HALF:PATCH, :]] * 2)
                wave = stacked([(pr * cr - pi * ci).astype(BF16), (pr * ci + pi * cr).astype(BF16)])
                ends.append(mm(tab[0, s], wave))
            for b, part in enumerate((ends[0] + ends[1], ends[0] - ends[1])):
                part = part.astype(BF16)
                for i in range(2):
                    for ri in range(2):
                        half[first + i, c2, b * HALF:(b + 1) * HALF, columns(ri)] = part[
                            ri * HALF:(ri + 1) * HALF, columns(i)
                        ]

    def row_parts(r):
        return slice(r * QUARTER, (r + 1) * QUARTER), slice(HALF + r * QUARTER, HALF + (r + 1) * QUARTER)

    def right_and_power_half(r):
        low, high = row_parts(r)
        sums = [None, None]
        for first in range(0, 8, 2):
            ends = [
                mm(stacked([half[m, s, rows, :] for m in (first, first + 1) for rows in (low, high)]), tab[1, s])
                for s in range(2)
            ]
            for b, part in enumerate((ends[0] + ends[1], ends[0] - ends[1])):
                for i in range(2):
                    mine = part[i * HALF:(i + 1) * HALF]
                    far[far_rows(first + i, b, r), :] = mine
                    re, im = mine[:, 0:HALF], mine[:, HALF:PATCH]
                    term = re * re + im * im
                    sums[b] = term if sums[b] is None else sums[b] + term
        for b in range(2):
            inten[r, b] = sums[b]

    def set_ratio(repeat, r):
        low, high = row_parts(r)
        for b in range(2):
            total = inten[r, b] + inten_in[repeat, r, b].astype(F32)
            ratio[r, b] = root[r, b] * lax.rsqrt(jnp.maximum(total, 1.0)) - 1.0

    def change_and_right_half(r):
        low, high = row_parts(r)
        for first in range(0, 8, 2):
            plus, minus = [], []
            for m in (first, first + 1):
                ya = far[far_rows(m, 0, r), :] * beside([ratio[r, 0]] * 2)
                yb = far[far_rows(m, 1, r), :] * beside([ratio[r, 1]] * 2)
                plus.append((ya + yb).astype(BF16))
                minus.append((ya - yb).astype(BF16))
            for s, part in enumerate((plus, minus)):
                near = mm(stacked(part), tab[0, s])
                for i in range(2):
                    lo = near[i * HALF:i * HALF + QUARTER]
                    hi = near[i * HALF + QUARTER:(i + 1) * HALF]
                    for b, mixed in enumerate((lo + hi, lo - hi)):
                        mixed = mixed.astype(BF16)
                        for ri, rows in enumerate((low, high)):
                            half[first + i, b, rows, columns(s)] = mixed[:, columns(ri)]

    def left_and_update_half(c2):
        for s in range(2):
            sums = [None, None]
            for first in range(0, 8, 2):
                near = mm(tab[1, s], beside([half[m, s, :, columns(c2)] for m in (first, first + 1)]))
                nr, ni = near[0:HALF], near[HALF:PATCH]
                pr, pi = pair_probe(first, s, c2)
                for ri, term in enumerate((pr * nr + pi * ni, pr * ni - pi * nr)):
                    term = term[:, 0:HALF] + term[:, HALF:PATCH]
                    sums[ri] = term if sums[ri] is None else sums[ri] + term
            for ri in range(2):
                upd[c2, s, columns(ri), :] = sums[ri]

    def swap(src, dst, which):
        copy = to(src, dst, pair_send.at[which], pair_recv.at[which], partner, j)
        copy.start()
        return copy

    for r in range(2):
        low, high = row_parts(r)
        for b in range(2):
            root[r, b] = jnp.sqrt(stacked([pat[low, columns(b)], pat[high, columns(b)]]).astype(F32))

    mine = pl.ds(pl.multiple_of(c * HALF, HALF), HALF)
    other = pl.ds(pl.multiple_of((1 - c) * HALF, HALF), HALF)
    for repeat in range(PASSES):
        if repeat == 0:
            for k in range(8):
                finish(k)
                exit_and_left(k)
        copies = []
        for r in range(2):
            right_and_power_half(r)
            inten_b[repeat, r] = inten[r].astype(BF16)
            copies.append(swap(inten_b.at[repeat, r], inten_in.at[repeat, r], 2 * repeat + r))
        if repeat == 0:
            power_b[...] = power[...].astype(BF16)
            power_copy = swap(power_b, power_in, 8)
        for r in range(2):
            copies[r].wait()
            set_ratio(repeat, r)
            change_and_right_half(r)
        copies = []
        for c2 in range(2):
            left_and_update_half(c2)
            if repeat < PASSES - 1:
                upd_b[c2] = upd[c2].astype(BF16)
                copies.append(swap(upd_b.at[c2], upd_in.at[c2], 4 + c2))
            else:
                last_b[c2] = upd[c2, :, other, :].astype(BF16)
                copies.append(swap(last_b.at[c2], last_in.at[c2], 6 + c2))
        if repeat == 0:
            power_copy.wait()
            whole = power[...] + power_in[...].astype(F32)
            whole = jnp.maximum(whole[0], whole[1])
            highest = jnp.max(jnp.max(whole, axis=0, keepdims=True), axis=1, keepdims=True)
            scale = STEP_SIZE / highest
        if repeat < PASSES - 1:
            for c2 in range(2):
                copies[c2].wait()
                for s in range(2):
                    cur[c2, s] = init[s, :, columns(c2)] + scale * (upd[c2, s] + upd_in[c2, s].astype(F32))
                exit_and_left_half(c2)

    pl.semaphore_wait(ring_sem, 3)
    pl.semaphore_signal(plane_sem, inc=1, device_id=(partner, j), device_id_type=MESH)
    pl.semaphore_wait(plane_sem, 1)

    moved = []
    for c2 in range(2):
        copies[c2].wait()
        column = []
        for s in range(2):
            change = cur[c2, s, mine, :] - init[s, mine, columns(c2)]
            change += scale * (upd[c2, s, mine, :] + last_in[c2, s].astype(F32))
            column.append(change.astype(BF16))
        moved.append(stacked(column))
    moved = beside(moved)

    placed = mm(place_r[...], moved).astype(BF16)
    canvas[...] = mm(placed, place_c[...]).astype(BF16)

    for dz, dy in FAR_FIRST:
        mode = ((z + dz) % 4) * 4 + (y + dy) % 4
        src = canvas.at[pl.ds(pl.multiple_of(mode * SLAB, SLAB), SLAB), :]
        dst = slabs.at[c * 8 + slot]

        if (dz, dy) == (0, 0):
            @pl.when(owner)
            def _():
                pltpu.make_async_copy(src, dst, slab_recv).start()

            @pl.when(jnp.logical_not(owner))
            def _():
                to(src, dst, slab_send, slab_recv, s_tile, mode).start()
        else:
            to(src, dst, slab_send, slab_recv, s_tile, mode).start()

    @pl.when(to_prev_x)
    def _():
        info_next.wait_recv()

    @pl.when(c == 0)
    def _():
        info[4] = info[2]

    @pl.when(c == 1)
    def _():
        info[4] = info[1]

    at_row = lax.broadcasted_iota(jnp.int32, (SLAB, 2 * PATCH), 0) + j * SLAB
    at_col = lax.broadcasted_iota(jnp.int32, (SLAB, 2 * PATCH), 1)
    from_above = jnp.where(t > 0, 1.0, 0.0)
    cover = jnp.zeros((SLAB, 2 * PATCH), F32)
    for k in range(2):
        here = info[4 * k]
        part = jnp.zeros((SLAB, 2 * PATCH), F32)
        for i in range(8):
            dr = at_row + k * PATCH - here[i:i + 1, 0:1]
            dc = at_col - here[i:i + 1, 1:2]
            inside = (dr >= 0) & (dr < PATCH) & (dc >= 0) & (dc < PATCH) & (here[i:i + 1, 2:3] > 0)
            part += jnp.where(inside, 1.0, 0.0)
        cover += part if k == 0 else part * from_above
    share = 1.0 / jnp.maximum(cover, 1.0)

    at_row = lax.broadcasted_iota(jnp.int32, (SLAB, PATCH), 0) + j * SLAB
    at_col = lax.broadcasted_iota(jnp.int32, (SLAB, PATCH), 1)

    for i in range(8):
        in_strip = at_row >= info[0, i:i + 1, 0:1]
        in_left = at_col >= info[0, i:i + 1, 1:2]
        for p, (kept, left) in enumerate(((True, True), (True, False), (False, True), (False, False))):
            wanted = (in_strip if kept else jnp.logical_not(in_strip)) & (in_left if left else jnp.logical_not(in_left))
            masks[p, i] = jnp.where(wanted, 1.0, 0.0)

    def gathered(ri, past_end):
        sums = [0.0, 0.0]
        for i in range(8):
            value = slabs[ri * 8 + i].astype(F32)
            for p in range(2):
                sums[p] += value * masks[2 * past_end + p, i]
        return jnp.concatenate(sums, axis=1)

    pltpu.make_async_copy(slabs, slabs, slab_recv).wait()
    spill_copy = to(spill, spill_in, spill_sem.at[0], spill_sem.at[1], up_tile, j)

    @pl.when(has_up)
    def _():
        for ri in range(2):
            spill[ri] = gathered(ri, 1).astype(BF16)
        spill_copy.start()

    for ri in range(2):
        own[ri] = gathered(ri, 0)

    @pl.when(has_down)
    def _():
        spill_copy.wait_recv()
        for ri in range(2):
            own[ri] += spill_in[ri].astype(F32)

    my_rows = out_ref.at[:, pl.ds(pl.multiple_of(j * SLAB, SLAB), SLAB), :]
    for ri in range(2):
        quot[ri] = (own[ri] * share).astype(BF16)
    for dz, dy in FAR_FIRST[:15]:
        to(quot, my_rows, quot_send, quot_recv, t, ((z + dz) % 4) * 4 + (y + dy) % 4).start()
    keep = pltpu.make_async_copy(quot, my_rows, local_sem.at[4])
    keep.start()

    info_pair.wait_send()

    @pl.when(to_next_x)
    def _():
        info_next.wait_send()

    @pl.when(has_up)
    def _():
        spill_copy.wait_send()

    for here, count in ((owner, 44), (jnp.logical_not(owner), 16)):
        @pl.when(here)
        def _():
            rows = far.at[pl.ds(0, count * 64), :]
            pltpu.make_async_copy(rows, rows, gather_send).wait()

    for here, count in ((owner, 15), (jnp.logical_not(owner), 16)):
        @pl.when(here)
        def _():
            rows = slabs.at[pl.ds(0, count)]
            pltpu.make_async_copy(rows, rows, slab_send).wait()

    rows = strip.at[0, pl.ds(0, 15 * SLAB), :]
    pltpu.make_async_copy(rows, rows, quot_send).wait()
    pltpu.make_async_copy(rows, rows, quot_recv).wait()
    keep.wait()


def shards(object_field, probe_modes, patterns, offsets, counts):
    tables = jnp.asarray(make_tables())
    in_hbm = pl.BlockSpec(memory_space=pltpu.HBM)
    vmem = pltpu.VMEM
    dma = pltpu.SemaphoreType.DMA
    change = pl.pallas_call(
        kernel,
        out_shape=vmem((2, PATCH, 2 * PATCH), BF16),
        in_specs=[
            in_hbm, in_hbm, in_hbm, in_hbm,
            in_hbm, in_hbm,
        ],
        out_specs=pl.BlockSpec(memory_space=vmem),
        scratch_shapes=[
            vmem((2, PATCH, PATCH), F32),
            vmem((2, PATCH, 2 * PATCH), F32),
            vmem((2, PATCH, 2 * PATCH), BF16),
            vmem((2, 2 * PATCH, 2 * PATCH), BF16),
            vmem((PATCH, PATCH), BF16),
            vmem((2, 2, PATCH, PATCH), BF16),
            vmem((5, 8, HALF), jnp.int32),
            vmem((8, 2, PATCH, PATCH), BF16),
            vmem((8, 2, PATCH, PATCH), BF16),
            vmem((16 * PATCH, PATCH), F32),
            vmem((2, PATCH, PATCH), F32),
            vmem((2, 2, PATCH, HALF), F32),
            vmem((2, 2, HALF, HALF), F32),
            vmem((2, 2, HALF, HALF), F32),
            vmem((2, 2, HALF, HALF), F32),
            vmem((2, 2, PATCH, HALF), F32),
            vmem((2, HALF, PATCH), F32),
            vmem((PASSES, 2, 2, HALF, HALF), BF16),
            vmem((2, 2, PATCH, HALF), BF16),
            vmem((2, 2, HALF, HALF), BF16),
            vmem((2, HALF, PATCH), BF16),
            vmem((PASSES, 2, 2, HALF, HALF), BF16),
            vmem((2, 2, PATCH, HALF), BF16),
            vmem((2, 2, HALF, HALF), BF16),
            vmem((2, HALF, PATCH), BF16),
            vmem((PATCH, PATCH), BF16),
            vmem((PATCH, PATCH), BF16),
            vmem((PATCH, PATCH), BF16),
            vmem((16, SLAB, PATCH), BF16),
            vmem((4, 8, SLAB, PATCH), F32),
            vmem((2, SLAB, 2 * PATCH), BF16),
            vmem((2, SLAB, 2 * PATCH), BF16),
            vmem((2, SLAB, 2 * PATCH), F32),
            vmem((2, SLAB, 2 * PATCH), BF16),
            pltpu.SMEM((2, 8), jnp.int32), pltpu.SMEM((1,), jnp.int32),
            dma((7,)), dma, dma((8, 2, 2)), dma((2,)), dma((4,)), dma((2,)), dma((2,)),
            dma((9,)), dma((9,)), dma, dma, dma((2,)), dma, dma,
            pltpu.SemaphoreType.REGULAR, pltpu.SemaphoreType.REGULAR,
        ],
        compiler_params=pltpu.CompilerParams(
            collective_id=0, has_side_effects=True, vmem_limit_bytes=56 * 1024 * 1024
        ),
        cost_estimate=pl.CostEstimate(flops=6 * 10**9, bytes_accessed=8 * 2**20, transcendentals=131072),
    )(object_field, probe_modes, patterns, tables, offsets.T, counts)
    return object_field + change.astype(F32)


def solution(mesh):
    return jax.shard_map(
        shards,
        mesh=mesh,
        in_specs=(
            P(None, "tile", None),
            P("mode", None, None, None),
            P("tile", None, None),
            P("tile", None),
            P("tile"),
        ),
        out_specs=P(None, "tile", None),
        check_vma=False,
    )
```

```python
import math

import numpy as np
import ml_dtypes
import jax
import jax.numpy as jnp
from jax import lax
from jax.experimental import pallas as pl
from jax.experimental.pallas import tpu as pltpu
from jax.sharding import PartitionSpec as P

PATCH = 256
HALF = 128
QUARTER = 64
PASSES = 2
STEP_SIZE = 0.9
SLAB = 16
MESH = pl.DeviceIdType.MESH
BF16 = jnp.bfloat16
F32 = jnp.float32

ORDER = ((0, 0), (1, 0), (0, 1), (0, 3), (0, 2), (1, 1), (1, 3), (1, 2))
SENT_ON_AT_HOME = (
    (0, 1, 0), (0, 3, 0), (0, 2, 0), (1, 0, 1), (0, 1, 1), (0, 3, 1),
    (1, 0, 0), (1, 1, 0), (1, 3, 0), (1, 1, 1), (1, 3, 1), (1, 2, 0),
)
SENT_ON_AWAY = ((0, 0, 1), (1, 0, 1), (0, 0, 0), (0, 1, 0), (0, 3, 0), (0, 1, 1), (0, 3, 1), (0, 2, 0))
FAR_FIRST = sorted(
    ((dz, dy) for dz in range(4) for dy in range(4)), key=lambda d: -min(d[0], 4 - d[0]) - min(d[1], 4 - d[1])
)


def make_tables():
    q = np.arange(HALF)
    tables = []
    for s in range(2):
        a = 2 * np.arange(HALF) + s
        angle = (q[:, None] * a[None, :] % PATCH).astype(np.float32) * np.float32(2.0 * math.pi / PATCH)
        factor = np.float32(1.0 / math.sqrt(PATCH))
        real = (np.cos(angle) * factor).astype(ml_dtypes.bfloat16)
        imag = (-np.sin(angle) * factor).astype(ml_dtypes.bfloat16)
        tables.append(np.block([[real, -imag], [imag, real]]))
    tables = np.stack(tables)
    return np.stack([tables, tables.transpose(0, 2, 1)])


def mm(a, b):
    return jnp.dot(a, b, preferred_element_type=F32)


def natural(position):
    return jnp.where(position < HALF, 2 * position, 2 * position - (PATCH - 1))


def kernel(
    obj_hbm, probe_hbm, pat_hbm, tab_hbm, offs_hbm, counts_hbm, out_ref,
    probe, strip, strip_b, ext, pat, tab, info, modes, half, far, init, cur,
    inten, root, ratio, upd, power, inten_b, upd_b, last_b, power_b, inten_in, upd_in, last_in, power_in,
    place_r, place_c, canvas, slabs, masks, spill, spill_in, own, quot,
    offs_ref, counts_ref, local_sem, gather_send, gather_recv, strip_sem, info_sem, patch_sem, pat_sem,
    pair_send, pair_recv, slab_send, slab_recv, spill_sem, quot_send, quot_recv, ring_sem, plane_sem,
):
    t = lax.axis_index("tile")
    j = lax.axis_index("mode")
    x, z = t // 2, j // 4
    c, y = t - 2 * x, j - 4 * z
    group = z // 2
    owner = c == group
    s_tile = 2 * x + group
    slot = j - 8 * group
    partner = 2 * x + (1 - c)
    up_tile, down_tile = t + 1, t - 1

    load_probe = pltpu.make_async_copy(probe_hbm.at[0], probe, local_sem.at[0])
    load_strip = pltpu.make_async_copy(obj_hbm, strip, local_sem.at[1])
    load_tab = pltpu.make_async_copy(tab_hbm, tab, local_sem.at[2])
    load_pat = pltpu.make_async_copy(pat_hbm.at[slot], pat, local_sem.at[3])
    @pl.when(owner)
    def _():
        load_probe.start()

    barrier = pltpu.get_barrier_semaphore()

    def greet(tile, mode):
        pl.semaphore_signal(barrier, inc=1, device_id=(tile, mode), device_id_type=MESH)

    for k in range(1, 4):
        greet(t, 4 * z + (y + k) % 4)
        greet(t, 4 * ((z + k) % 4) + y)
    greet(partner, j)
    has_up, has_down = t < 7, t > 0
    to_next_x = (c == 1) & has_up
    to_prev_x = (c == 0) & has_down

    @pl.when(to_next_x)
    def _():
        greet(up_tile, j)

    @pl.when(to_prev_x)
    def _():
        greet(down_tile, j)

    load_offs = pltpu.make_async_copy(offs_hbm, offs_ref, local_sem.at[5])
    load_counts = pltpu.make_async_copy(counts_hbm, counts_ref, local_sem.at[6])
    load_offs.start()
    load_counts.start()

    @pl.when(owner)
    def _():
        load_pat.start()

    load_strip.start()
    load_tab.start()

    @pl.when(owner)
    def _():
        load_probe.wait()
        rows = lax.broadcasted_iota(jnp.int32, (PATCH, PATCH), 0)
        cols = lax.broadcasted_iota(jnp.int32, (PATCH, PATCH), 1)
        sort_r = jnp.where(cols == natural(rows), 1.0, 0.0).astype(BF16)
        sort_c = jnp.where(rows == natural(cols), 1.0, 0.0).astype(BF16)
        for ri in range(2):
            plane = mm(sort_r, probe[ri].astype(BF16)).astype(BF16)
            plane = mm(plane, sort_c).astype(BF16)
            for s in range(2):
                modes[0, s, ri * HALF:(ri + 1) * HALF, :] = plane[s * HALF:(s + 1) * HALF]

    sends_strip = jnp.logical_not(owner) & has_down

    @pl.when(sends_strip)
    def _():
        load_strip.wait()
        strip_b[...] = strip[...].astype(BF16)

    @pl.when(jnp.logical_not(owner | has_down))
    def _():
        load_strip.wait()

    across = to_next_x | to_prev_x
    pl.semaphore_wait(barrier, 7 + jnp.where(across, 1, 0))

    def to(src, dst, send, recv, tile, mode):
        return pltpu.make_async_remote_copy(
            src_ref=src, dst_ref=dst, send_sem=send, recv_sem=recv,
            device_id=(tile, mode), device_id_type=MESH,
        )

    def block(m, s, h):
        return modes.at[m, s, pl.ds(h * HALF, HALF), :]

    def mode_slot(row, home, dy):
        d = (row - 2 * c + 4) % 4
        nearer = 2 * c + jnp.where((d == 1) | (d == 2), 1, 0)
        return jnp.where(home == nearer, ORDER.index((0, dy)), ORDER.index((1, dy)))

    def relay(k, s, h, home, dy, step_z, step_y):
        row = (z + step_z + 4) % 4
        there = mode_slot(row, home, (dy + step_y) % 4)
        to(
            block(k, s, h), block(there, s, h), gather_send, gather_recv.at[there, s, h],
            t, row * 4 + (y + step_y + 4) % 4,
        ).start()

    def take(which, dy, s):
        k = ORDER.index((which, dy))
        d = (z - 2 * c + 4) % 4
        nearer = jnp.where((d == 1) | (d == 2), 1, 0)
        home = 2 * c + (nearer if which == 0 else 1 - nearer)
        dz = (z - home + 4) % 4
        for h in range(2):
            to(
                block(k, s, h), block(k, s, h), gather_send, gather_recv.at[k, s, h], t, j
            ).wait_recv()
            if s == 0 and dy == 0:
                @pl.when(dz == 0)
                def _():
                    for step in (2, 1, -1):
                        relay(k, s, h, home, dy, 0, step)

            if s == 1 and dy == 0:
                @pl.when(dz == 2)
                def _():
                    relay(k, s, h, home, dy, 0, 2)

                for step in (1, -1):
                    relay(k, s, h, home, dy, 0, step)
            if s == 1 and (dy, h) in ((1, 0), (3, 1)):
                @pl.when(dz != 2)
                def _():
                    relay(k, s, h, home, dy, 0, 2 - dy)

            if s == 0 or dy == 0:
                @pl.when(dz == 0)
                def _():
                    if s == 1:
                        relay(k, s, h, home, dy, 2, 0)
                    relay(k, s, h, home, dy, 1, 0)
                    relay(k, s, h, home, dy, -1, 0)

            if s == 0:
                @pl.when(dz == (1 if h == 0 else 3))
                def _():
                    relay(k, s, h, home, dy, 1 if h == 0 else -1, 0)

    def finish(k):
        which, dy = ORDER[k]
        for here, done in ((owner, SENT_ON_AT_HOME), (jnp.logical_not(owner), SENT_ON_AWAY)):
            @pl.when(here)
            def _():
                for s in range(2):
                    if (which, dy, s) not in done and not (k == 0 and done is SENT_ON_AT_HOME):
                        take(which, dy, s)

    send_strip = to(
        strip_b, ext.at[:, pl.ds(PATCH, PATCH), :], strip_sem.at[0], strip_sem.at[1], down_tile, j
    )
    pat_pair = to(pat_hbm.at[slot], pat, pat_sem.at[0], pat_sem.at[1], partner, j)

    @pl.when(owner)
    def _():
        for step in (1, -1, 2):
            for h in range(2):
                relay(0, 0, h, z, 0, 0, step)
                relay(0, 1, h, z, 0, step, 0)
        for h in range(2):
            for step in (1, -1):
                relay(0, 0, h, z, 0, step, 0)
                relay(0, 1, h, z, 0, 0, step)

    @pl.when(sends_strip)
    def _():
        send_strip.start()

    load_offs.wait()
    load_counts.wait()
    lane = lax.broadcasted_iota(jnp.int32, (8, HALF), 1)
    live = (lax.broadcasted_iota(jnp.int32, (8, HALF), 0) < counts_ref[0]).astype(jnp.int32)
    place = jnp.where(lane == 2, live, 0)
    line = lax.broadcasted_iota(jnp.int32, (8, HALF), 0)
    for i in range(8):
        for p in range(2):
            place = jnp.where((line == i) & (lane == p), offs_ref[p, i], place)
    info[0] = place

    @pl.when(jnp.logical_not(has_down))
    def _():
        info[2] = jnp.zeros((8, HALF), jnp.int32)


    info_pair = to(info.at[0], info.at[1], info_sem.at[0], info_sem.at[1], partner, j)
    info_next = to(info.at[0], info.at[2], info_sem.at[2], info_sem.at[3], up_tile, j)
    info_pair.start()

    @pl.when(to_next_x)
    def _():
        info_next.start()

    for k in range(1, 4):
        pl.semaphore_signal(ring_sem, inc=1, device_id=(t, 4 * ((z + k) % 4) + y), device_id_type=MESH)

    @pl.when(t == 7)
    def _():
        ext[:, PATCH:2 * PATCH, :] = jnp.zeros((2, PATCH, 2 * PATCH), BF16)

    @pl.when(owner)
    def _():
        pat_pair.start()
        load_strip.wait()
        high = strip[...].astype(BF16)
        ext[:, 0:PATCH, :] = high
        strip_b[...] = (strip[...] - high.astype(F32)).astype(BF16)

    for here, order in ((owner, SENT_ON_AT_HOME), (jnp.logical_not(owner), SENT_ON_AWAY)):
        @pl.when(here)
        def _():
            for which, dy, s in order[:8] if order is SENT_ON_AT_HOME else order:
                take(which, dy, s)

    load_tab.wait()
    info_pair.wait_recv()

    @pl.when(owner)
    def _():
        info[3] = info[0]

    @pl.when(jnp.logical_not(owner))
    def _():
        info[3] = info[1]

    row = info[3, pl.ds(slot, 1), :]
    first_row, first_col, alive = row[:, 0:1], row[:, 1:2], row[:, 2:3]
    rows = lax.broadcasted_iota(jnp.int32, (PATCH, PATCH), 0)
    cols = lax.broadcasted_iota(jnp.int32, (PATCH, PATCH), 1)

    def wrapped(at):
        return jnp.where(at >= PATCH, at - PATCH, at)

    place_r[...] = jnp.where((rows == wrapped(first_row + natural(cols))) & (alive > 0), 1.0, 0.0).astype(BF16)
    place_c[...] = jnp.where(cols == wrapped(first_col + natural(rows)), 1.0, 0.0).astype(BF16)

    send_patch = to(init, init, patch_sem.at[0], patch_sem.at[1], partner, j)

    @pl.when(owner)
    def _():
        @pl.when(has_up)
        def _():
            send_strip.wait_recv()

        inside = jnp.where(t == 7, PATCH, 2 * PATCH)
        rows = lax.broadcasted_iota(jnp.int32, (PATCH, 2 * PATCH), 0)
        cols = lax.broadcasted_iota(jnp.int32, (PATCH, 2 * PATCH), 1)
        cut_r = jnp.where((cols == first_row + natural(rows)) & (cols < inside), 1.0, 0.0).astype(BF16)
        rows2 = lax.broadcasted_iota(jnp.int32, (2 * PATCH, PATCH), 0)
        cols2 = lax.broadcasted_iota(jnp.int32, (2 * PATCH, PATCH), 1)
        cut_c = jnp.where(rows2 == first_col + natural(cols2), 1.0, 0.0).astype(BF16)
        for ri in range(2):
            high = mm(cut_r, ext[ri]).astype(BF16)
            low = mm(cut_r[:, 0:PATCH], strip_b[ri]).astype(BF16)
            piece = mm(high, cut_c) + mm(low, cut_c)
            for s in range(2):
                init[s, ri * HALF:(ri + 1) * HALF, :] = piece[s * HALF:(s + 1) * HALF]
        send_patch.start()
        for which, dy, s in SENT_ON_AT_HOME[8:]:
            take(which, dy, s)

    @pl.when(owner)
    def _():
        load_pat.wait()
        pat_pair.wait_send()
        send_patch.wait_send()

    @pl.when(jnp.logical_not(owner))
    def _():
        pat_pair.wait_recv()
        send_patch.wait_recv()

    @pl.when(sends_strip)
    def _():
        send_strip.wait_send()


    def far_rows(m, b, r):
        return pl.ds(((2 * m + b) * 2 + r) * HALF, HALF)

    def columns(s):
        return slice(s * HALF, (s + 1) * HALF)

    def beside(parts):
        return jnp.concatenate(parts, axis=1)

    def stacked(parts):
        return jnp.concatenate(parts, axis=0)

    def exit_and_left(m):
        ends = []
        for s in range(2):
            pr = modes[m, s, 0:HALF, :].astype(F32)
            pi = modes[m, s, HALF:PATCH, :].astype(F32)
            cr = init[s, 0:HALF, :]
            ci = init[s, HALF:PATCH, :]
            wave = stacked([(pr * cr - pi * ci).astype(BF16), (pr * ci + pi * cr).astype(BF16)])
            if m == 0:
                power[s] = pr * pr + pi * pi
            else:
                power[s] += pr * pr + pi * pi
            ends.append(mm(tab[0, s], wave))
        for b, part in enumerate((ends[0] + ends[1], ends[0] - ends[1])):
            part = part.astype(BF16)
            for s in range(2):
                for ri in range(2):
                    half[m, s, b * HALF:(b + 1) * HALF, columns(ri)] = part[
                        ri * HALF:(ri + 1) * HALF, columns(s)
                    ]

    def pair_probe(first, s, c2):
        return [
            beside([modes[m, s, columns(ri), columns(c2)] for m in (first, first + 1)]).astype(F32)
            for ri in range(2)
        ]

    def exit_and_left_half(c2):
        for first in range(0, 8, 2):
            ends = []
            for s in range(2):
                pr, pi = pair_probe(first, s, c2)
                cr = beside([cur[c2, s, 0:HALF, :]] * 2)
                ci = beside([cur[c2, s, HALF:PATCH, :]] * 2)
                wave = stacked([(pr * cr - pi * ci).astype(BF16), (pr * ci + pi * cr).astype(BF16)])
                ends.append(mm(tab[0, s], wave))
            for b, part in enumerate((ends[0] + ends[1], ends[0] - ends[1])):
                part = part.astype(BF16)
                for i in range(2):
                    for ri in range(2):
                        half[first + i, c2, b * HALF:(b + 1) * HALF, columns(ri)] = part[
                            ri * HALF:(ri + 1) * HALF, columns(i)
                        ]

    def row_parts(r):
        return slice(r * QUARTER, (r + 1) * QUARTER), slice(HALF + r * QUARTER, HALF + (r + 1) * QUARTER)

    def right_and_power_half(r):
        low, high = row_parts(r)
        sums = [None, None]
        for first in range(0, 8, 2):
            ends = [
                mm(stacked([half[m, s, rows, :] for m in (first, first + 1) for rows in (low, high)]), tab[1, s])
                for s in range(2)
            ]
            for b, part in enumerate((ends[0] + ends[1], ends[0] - ends[1])):
                for i in range(2):
                    mine = part[i * HALF:(i + 1) * HALF]
                    far[far_rows(first + i, b, r), :] = mine
                    re, im = mine[:, 0:HALF], mine[:, HALF:PATCH]
                    term = re * re + im * im
                    sums[b] = term if sums[b] is None else sums[b] + term
        for b in range(2):
            inten[r, b] = sums[b]

    def set_ratio(repeat, r):
        low, high = row_parts(r)
        for b in range(2):
            total = inten[r, b] + inten_in[repeat, r, b].astype(F32)
            ratio[r, b] = root[r, b] * lax.rsqrt(jnp.maximum(total, 1.0)) - 1.0

    def change_and_right_half(r):
        low, high = row_parts(r)
        for first in range(0, 8, 2):
            plus, minus = [], []
            for m in (first, first + 1):
                ya = far[far_rows(m, 0, r), :] * beside([ratio[r, 0]] * 2)
                yb = far[far_rows(m, 1, r), :] * beside([ratio[r, 1]] * 2)
                plus.append((ya + yb).astype(BF16))
                minus.append((ya - yb).astype(BF16))
            for s, part in enumerate((plus, minus)):
                near = mm(stacked(part), tab[0, s])
                for i in range(2):
                    lo = near[i * HALF:i * HALF + QUARTER]
                    hi = near[i * HALF + QUARTER:(i + 1) * HALF]
                    for b, mixed in enumerate((lo + hi, lo - hi)):
                        mixed = mixed.astype(BF16)
                        for ri, rows in enumerate((low, high)):
                            half[first + i, b, rows, columns(s)] = mixed[:, columns(ri)]

    def left_and_update_half(c2):
        for s in range(2):
            sums = [None, None]
            for first in range(0, 8, 2):
                near = mm(tab[1, s], beside([half[m, s, :, columns(c2)] for m in (first, first + 1)]))
                nr, ni = near[0:HALF], near[HALF:PATCH]
                pr, pi = pair_probe(first, s, c2)
                for ri, term in enumerate((pr * nr + pi * ni, pr * ni - pi * nr)):
                    term = term[:, 0:HALF] + term[:, HALF:PATCH]
                    sums[ri] = term if sums[ri] is None else sums[ri] + term
            for ri in range(2):
                upd[c2, s, columns(ri), :] = sums[ri]

    def swap(src, dst, which):
        copy = to(src, dst, pair_send.at[which], pair_recv.at[which], partner, j)
        copy.start()
        return copy

    for r in range(2):
        low, high = row_parts(r)
        for b in range(2):
            root[r, b] = jnp.sqrt(stacked([pat[low, columns(b)], pat[high, columns(b)]]).astype(F32))

    mine = pl.ds(pl.multiple_of(c * HALF, HALF), HALF)
    other = pl.ds(pl.multiple_of((1 - c) * HALF, HALF), HALF)
    for repeat in range(PASSES):
        if repeat == 0:
            for k in range(8):
                finish(k)
                exit_and_left(k)
        copies = []
        for r in range(2):
            right_and_power_half(r)
            inten_b[repeat, r] = inten[r].astype(BF16)
            copies.append(swap(inten_b.at[repeat, r], inten_in.at[repeat, r], 2 * repeat + r))
        if repeat == 0:
            power_b[...] = power[...].astype(BF16)
            power_copy = swap(power_b, power_in, 8)
        for r in range(2):
            copies[r].wait()
            set_ratio(repeat, r)
            change_and_right_half(r)
        copies = []
        for c2 in range(2):
            left_and_update_half(c2)
            if repeat < PASSES - 1:
                upd_b[c2] = upd[c2].astype(BF16)
                copies.append(swap(upd_b.at[c2], upd_in.at[c2], 4 + c2))
            else:
                last_b[c2] = upd[c2, :, other, :].astype(BF16)
                copies.append(swap(last_b.at[c2], last_in.at[c2], 6 + c2))
        if repeat == 0:
            power_copy.wait()
            whole = power[...] + power_in[...].astype(F32)
            whole = jnp.maximum(whole[0], whole[1])
            highest = jnp.max(jnp.max(whole, axis=0, keepdims=True), axis=1, keepdims=True)
            scale = STEP_SIZE / highest
        if repeat < PASSES - 1:
            for c2 in range(2):
                copies[c2].wait()
                for s in range(2):
                    cur[c2, s] = init[s, :, columns(c2)] + scale * (upd[c2, s] + upd_in[c2, s].astype(F32))
                exit_and_left_half(c2)

    pl.semaphore_wait(ring_sem, 3)
    pl.semaphore_signal(plane_sem, inc=1, device_id=(partner, j), device_id_type=MESH)
    pl.semaphore_wait(plane_sem, 1)

    moved = []
    for c2 in range(2):
        copies[c2].wait()
        column = []
        for s in range(2):
            change = cur[c2, s, mine, :] - init[s, mine, columns(c2)]
            change += scale * (upd[c2, s, mine, :] + last_in[c2, s].astype(F32))
            column.append(change.astype(BF16))
        moved.append(stacked(column))
    moved = beside(moved)

    for dz in (2, 1, 3, 0):
        rows = pl.ds(pl.multiple_of((z + dz) % 4 * 64, 64), 64)
        placed = mm(place_r[rows, :], moved).astype(BF16)
        canvas[rows, :] = mm(placed, place_c[...]).astype(BF16)
        for dy in (2, 1, 3, 0):
            mode = ((z + dz) % 4) * 4 + (y + dy) % 4
            src = canvas.at[pl.ds(pl.multiple_of(mode * SLAB, SLAB), SLAB), :]
            dst = slabs.at[c * 8 + slot]

            if (dz, dy) == (0, 0):
                @pl.when(owner)
                def _():
                    pltpu.make_async_copy(src, dst, slab_recv).start()

                @pl.when(jnp.logical_not(owner))
                def _():
                    to(src, dst, slab_send, slab_recv, s_tile, mode).start()
            else:
                to(src, dst, slab_send, slab_recv, s_tile, mode).start()

    @pl.when(to_prev_x)
    def _():
        info_next.wait_recv()

    @pl.when(c == 0)
    def _():
        info[4] = info[2]

    @pl.when(c == 1)
    def _():
        info[4] = info[1]

    at_row = lax.broadcasted_iota(jnp.int32, (SLAB, 2 * PATCH), 0) + j * SLAB
    at_col = lax.broadcasted_iota(jnp.int32, (SLAB, 2 * PATCH), 1)
    from_above = jnp.where(t > 0, 1.0, 0.0)
    cover = jnp.zeros((SLAB, 2 * PATCH), F32)
    for k in range(2):
        here = info[4 * k]
        part = jnp.zeros((SLAB, 2 * PATCH), F32)
        for i in range(8):
            dr = at_row + k * PATCH - here[i:i + 1, 0:1]
            dc = at_col - here[i:i + 1, 1:2]
            inside = (dr >= 0) & (dr < PATCH) & (dc >= 0) & (dc < PATCH) & (here[i:i + 1, 2:3] > 0)
            part += jnp.where(inside, 1.0, 0.0)
        cover += part if k == 0 else part * from_above
    share = 1.0 / jnp.maximum(cover, 1.0)

    at_row = lax.broadcasted_iota(jnp.int32, (SLAB, PATCH), 0) + j * SLAB
    at_col = lax.broadcasted_iota(jnp.int32, (SLAB, PATCH), 1)

    for i in range(8):
        in_strip = at_row >= info[0, i:i + 1, 0:1]
        in_left = at_col >= info[0, i:i + 1, 1:2]
        for p, (kept, left) in enumerate(((True, True), (True, False), (False, True), (False, False))):
            wanted = (in_strip if kept else jnp.logical_not(in_strip)) & (in_left if left else jnp.logical_not(in_left))
            masks[p, i] = jnp.where(wanted, 1.0, 0.0)

    def gathered(ri, past_end):
        sums = [0.0, 0.0]
        for i in range(8):
            value = slabs[ri * 8 + i].astype(F32)
            for p in range(2):
                sums[p] += value * masks[2 * past_end + p, i]
        return jnp.concatenate(sums, axis=1)

    pltpu.make_async_copy(slabs, slabs, slab_recv).wait()
    spill_copy = to(spill, spill_in, spill_sem.at[0], spill_sem.at[1], up_tile, j)

    @pl.when(has_up)
    def _():
        for ri in range(2):
            spill[ri] = gathered(ri, 1).astype(BF16)
        spill_copy.start()

    for ri in range(2):
        own[ri] = gathered(ri, 0)

    @pl.when(has_down)
    def _():
        spill_copy.wait_recv()
        for ri in range(2):
            own[ri] += spill_in[ri].astype(F32)

    my_rows = out_ref.at[:, pl.ds(pl.multiple_of(j * SLAB, SLAB), SLAB), :]
    for ri in range(2):
        quot[ri] = (own[ri] * share).astype(BF16)
    for dz, dy in FAR_FIRST[:15]:
        to(quot, my_rows, quot_send, quot_recv, t, ((z + dz) % 4) * 4 + (y + dy) % 4).start()
    keep = pltpu.make_async_copy(quot, my_rows, local_sem.at[4])
    keep.start()

    info_pair.wait_send()

    @pl.when(to_next_x)
    def _():
        info_next.wait_send()

    @pl.when(has_up)
    def _():
        spill_copy.wait_send()

    for here, count in ((owner, 44), (jnp.logical_not(owner), 16)):
        @pl.when(here)
        def _():
            rows = far.at[pl.ds(0, count * 64), :]
            pltpu.make_async_copy(rows, rows, gather_send).wait()

    for here, count in ((owner, 15), (jnp.logical_not(owner), 16)):
        @pl.when(here)
        def _():
            rows = slabs.at[pl.ds(0, count)]
            pltpu.make_async_copy(rows, rows, slab_send).wait()

    rows = strip.at[0, pl.ds(0, 15 * SLAB), :]
    pltpu.make_async_copy(rows, rows, quot_send).wait()
    pltpu.make_async_copy(rows, rows, quot_recv).wait()
    keep.wait()


def shards(object_field, probe_modes, patterns, offsets, counts):
    tables = jnp.asarray(make_tables())
    in_hbm = pl.BlockSpec(memory_space=pltpu.HBM)
    vmem = pltpu.VMEM
    dma = pltpu.SemaphoreType.DMA
    change = pl.pallas_call(
        kernel,
        out_shape=vmem((2, PATCH, 2 * PATCH), BF16),
        in_specs=[
            in_hbm, in_hbm, in_hbm, in_hbm,
            in_hbm, in_hbm,
        ],
        out_specs=pl.BlockSpec(memory_space=vmem),
        scratch_shapes=[
            vmem((2, PATCH, PATCH), F32),
            vmem((2, PATCH, 2 * PATCH), F32),
            vmem((2, PATCH, 2 * PATCH), BF16),
            vmem((2, 2 * PATCH, 2 * PATCH), BF16),
            vmem((PATCH, PATCH), BF16),
            vmem((2, 2, PATCH, PATCH), BF16),
            vmem((5, 8, HALF), jnp.int32),
            vmem((8, 2, PATCH, PATCH), BF16),
            vmem((8, 2, PATCH, PATCH), BF16),
            vmem((16 * PATCH, PATCH), F32),
            vmem((2, PATCH, PATCH), F32),
            vmem((2, 2, PATCH, HALF), F32),
            vmem((2, 2, HALF, HALF), F32),
            vmem((2, 2, HALF, HALF), F32),
            vmem((2, 2, HALF, HALF), F32),
            vmem((2, 2, PATCH, HALF), F32),
            vmem((2, HALF, PATCH), F32),
            vmem((PASSES, 2, 2, HALF, HALF), BF16),
            vmem((2, 2, PATCH, HALF), BF16),
            vmem((2, 2, HALF, HALF), BF16),
            vmem((2, HALF, PATCH), BF16),
            vmem((PASSES, 2, 2, HALF, HALF), BF16),
            vmem((2, 2, PATCH, HALF), BF16),
            vmem((2, 2, HALF, HALF), BF16),
            vmem((2, HALF, PATCH), BF16),
            vmem((PATCH, PATCH), BF16),
            vmem((PATCH, PATCH), BF16),
            vmem((PATCH, PATCH), BF16),
            vmem((16, SLAB, PATCH), BF16),
            vmem((4, 8, SLAB, PATCH), F32),
            vmem((2, SLAB, 2 * PATCH), BF16),
            vmem((2, SLAB, 2 * PATCH), BF16),
            vmem((2, SLAB, 2 * PATCH), F32),
            vmem((2, SLAB, 2 * PATCH), BF16),
            pltpu.SMEM((2, 8), jnp.int32), pltpu.SMEM((1,), jnp.int32),
            dma((7,)), dma, dma((8, 2, 2)), dma((2,)), dma((4,)), dma((2,)), dma((2,)),
            dma((9,)), dma((9,)), dma, dma, dma((2,)), dma, dma,
            pltpu.SemaphoreType.REGULAR, pltpu.SemaphoreType.REGULAR,
        ],
        compiler_params=pltpu.CompilerParams(
            collective_id=0, has_side_effects=True, vmem_limit_bytes=56 * 1024 * 1024
        ),
        cost_estimate=pl.CostEstimate(flops=6 * 10**9, bytes_accessed=8 * 2**20, transcendentals=131072),
    )(object_field, probe_modes, patterns, tables, offsets.T, counts)
    return object_field + change.astype(F32)


def solution(mesh):
    return jax.shard_map(
        shards,
        mesh=mesh,
        in_specs=(
            P(None, "tile", None),
            P("mode", None, None, None),
            P("tile", None, None),
            P("tile", None),
            P("tile"),
        ),
        out_specs=P(None, "tile", None),
        check_vma=False,
    )
```
